256 devices in a mesh: lat: 4 (over x_hi, core), lon: 8 (over x_lo, y), lev: 8 (over z).
Axes of the slice: x: 4 (x_hi: 2, x_lo: 2; x = x_hi * 2 + x_lo), y: 4, z: 8, core: 2. Of those that a mesh axis runs over, the one named last changes fastest.
Arguments:
- target: bfloat16 [4, 768, 64, 1024], P(None, 'lev', 'lat', 'lon'), may hold values from -6 to 6
- hidden: bfloat16 [256, 64, 1024], P(None, 'lat', 'lon'), may hold values from -6 to 6
- weight: bfloat16 [16, 768, 256], P(None, 'lev'), may hold values from -0.1875 to 0.1875
- bias: float32 [768], P('lev'), may hold values from -3 to 3
- gamma: float32 [256, 256], replicated, may hold values from 0 to 0.02
- beta: float32 [256], replicated, may hold values from 0.5 to 2
Outputs:
- grad_hidden: float32 [256, 64, 1024], P(None, 'lat', 'lon')
- grad_weight: float32 [16, 768, 256], P(None, 'lev')
- grad_bias: float32 [768], P('lev')
- grad_gamma: float32 [256, 256], replicated
- grad_beta: float32 [256], replicated
The draws below stay inside these ranges and needn't reach their ends.
All inputs are finite; a program needn't handle non-finite values.
Results may differ from the reference program's by a relative error of at most 0.0021.
Values may be sent and summed in bfloat16 or wider, within the bound.
A program may use at most 128 MiB of HBM per device.

```python
import math
import jax
import jax.numpy as jnp
from jax import lax

C = 768
N = 256
TAPS = 16
HLOW = 64
WLOW = 1024


def steps_of(rng, shape, split, low, top_value):
    factor_of, own = 1.0, jax.random.fold_in(rng, 6)
    for axis_at, blocks in split:
        steps = jnp.exp(jax.random.uniform(jax.random.fold_in(own, axis_at), (blocks,), jnp.float32, low / len(split), top_value / len(split)))
        factor_of = factor_of * jnp.repeat(steps, shape[axis_at] // blocks).reshape([-1 if axis == axis_at else 1 for axis in range(len(shape))])
    return factor_of


def bell_draw(stream_key, shape, spread, bound, cuts=(), dtype=jnp.bfloat16):
    level = steps_of(stream_key, shape, cuts, -0.22, 0.18) if cuts else 1.0
    drawn = jax.random.normal(stream_key, shape, jnp.float32) * spread * level
    return jnp.minimum(jnp.maximum(drawn, -bound), bound).astype(dtype)


def setup_inputs(seed: int = 0) -> dict:
    seeds = jax.random.split(jax.random.key(seed), 7)
    return {
        "target": bell_draw(seeds[0], (4, C, HLOW, WLOW), 1.0, 6.0, ((1, 8), (2, 4), (3, 8))),
        "hidden": bell_draw(seeds[1], (N, HLOW, WLOW), 1.0, 6.0, ((1, 4), (2, 8))),
        "weight": bell_draw(seeds[2], (TAPS, C, N), (4 * N) ** -0.5, 0.1875, ((1, 8),)),
        "bias": bell_draw(seeds[3], (C,), 0.5, 3.0, ((0, 8),), jnp.float32),
        "gamma": jnp.clip(jax.random.uniform(seeds[4], (N, N), jnp.float32, 0.0, 0.02), 0.0, 0.02),
        "beta": jnp.clip(jnp.exp(jax.random.uniform(seeds[5], (N,), jnp.float32, math.log(0.5), math.log(2.0))), 0.5, 2.0),
    }


def shifted(field, drow, dcol):
    rolled = jnp.roll(field, -dcol, axis=2)
    padded = jnp.pad(rolled, ((0, 0), (1, 1), (0, 0)))
    return padded[:, 1 + drow:1 + drow + HLOW, :]

def reference(target, hidden, weight, bias, gamma, beta):
    cells = HLOW * WLOW
    values = hidden.astype(jnp.float32)
    squares = (values * values).reshape(N, cells)
    root = jnp.sqrt(beta[:, None] + jnp.dot(gamma, squares, precision=lax.Precision.HIGHEST))
    inverse = (values.reshape(N, cells) * root).astype(jnp.bfloat16).reshape(N, HLOW, WLOW)
    row_index = jnp.arange(HLOW).astype(jnp.float32)
    grad_u = jnp.zeros((N, HLOW, WLOW), jnp.float32)
    grad_bias = jnp.zeros((C,), jnp.float32)
    grad_list = []
    for phase in range(4):
        prow, pcol = (phase // 2, phase % 2)
        moved = []
        for tap in range(4):
            drow, dcol = (prow - 1 + tap // 2, pcol - 1 + tap % 2)
            moved.append(shifted(inverse, drow, dcol).reshape(N, cells))
        recon = bias[:, None] + jnp.zeros((C, cells), jnp.float32)
        for tap in range(4):
            recon = recon + jnp.dot(weight[4 * phase + tap], moved[tap], preferred_element_type=jnp.float32)
        area = jnp.cos(math.pi * ((2.0 * row_index + prow + 0.5) / (2.0 * HLOW) - 0.5))
        area_cells = jnp.broadcast_to(area[:, None], (HLOW, WLOW)).reshape(cells)
        diff = (recon - target[phase].reshape(C, cells).astype(jnp.float32)) * area_cells[None, :]
        grad_recon = diff.astype(jnp.bfloat16)
        grad_bias = grad_bias + lax.optimization_barrier(jnp.sum(diff, axis=1))
        for tap in range(4):
            drow, dcol = (prow - 1 + tap // 2, pcol - 1 + tap % 2)
            grad_list.append(jnp.dot(grad_recon, moved[tap].T, preferred_element_type=jnp.float32))
            term = jnp.dot(weight[4 * phase + tap].T, grad_recon, preferred_element_type=jnp.float32)
            grad_u = grad_u + shifted(term.reshape(N, HLOW, WLOW), -drow, -dcol)
    flat_grad = grad_u.reshape(N, cells)
    flat_values = values.reshape(N, cells)
    mixing = flat_grad * flat_values / (2.0 * root)
    grad_hidden = flat_grad * root + 2.0 * flat_values * jnp.dot(gamma.T, mixing, precision=lax.Precision.HIGHEST)
    grad_gamma = jnp.dot(mixing, squares.T, precision=lax.Precision.HIGHEST) / cells
    grad_beta = lax.optimization_barrier(jnp.sum(mixing, axis=1)) / cells
    grad_weight = jnp.stack(grad_list, axis=0) / cells
    return (grad_hidden.reshape(N, HLOW, WLOW), grad_weight, grad_bias / cells, grad_gamma, grad_beta)
```

```python
import functools
import math

import jax
import jax.numpy as jnp
import numpy as np
from jax import lax
from jax.experimental import pallas as pl
from jax.experimental.pallas import tpu as pltpu
from jax.sharding import PartitionSpec as P

F32 = jnp.float32
BF16 = jnp.bfloat16
MESH = pl.DeviceIdType.MESH
LANES = 128


def split(x):
    hi = x.astype(BF16)
    return hi, (x - hi.astype(F32)).astype(BF16)


def dot(a, b):
    return jnp.dot(a, b, preferred_element_type=F32)


def dot_nt(a, b):
    return lax.dot_general(a, b, (((1,), (1,)), ((), ())), preferred_element_type=F32)


def wrap(index, size):
    return lax.rem(index + size, size)


def kernel(
    dims,
    area_ref, hidden_ref, target_ref, weight_ref, bias_ref, gamma_ref, beta_ref,
    gh_out, gw_out, gb_out, gg_out, gbeta_out,
    hid_v, tgt_v, w_v, gamma_v,
    hf, tf, hx, root_s, hr_s, sqh, sql, g3, gt3, wt,
    us, gs, sel, sr,
    hh_send, hh_recv, eu_send, eu_recv, eg_send, eg_recv,
    dw, dwp, rsb, rsr, wg,
    gu, bacc, mh, ml, ext, extp, exts, extr, extz, extg,
    abuf, arecv, agr, gho,
    in_sem, out_sem,
    row_ss, row_rs, eu_ss, eu_rs, grow_ss, grow_rs, eg_ss, eg_rs,
    pw_ss, pw_rs, rb_ss, rb_rs, ab_ss, ab_rs, pg_ss, pg_rs,
    pe_ss, pe_rs, rc_ss, rc_rs, z_ss, z_rs, ac_ss, ac_rs, pc_ss, pc_rs,
    a_ss, a_rs, g_ss, g_rs,
):
    nn, rows, chans, n_lat, n_lon, n_lev, n_y, total_cells = dims
    cells = rows * LANES
    rpad = rows + 2
    lat, lon, lev = lax.axis_index("lat"), lax.axis_index("lon"), lax.axis_index("lev")
    core = lax.rem(lat, 2)
    n_chip = (n_lat // 2) * n_lon
    n_xlo = n_lon // n_y
    chip = lax.div(lat, 2) * n_lon + lon
    half = 16 // 2 * chans // n_chip
    share = nn // 2 // n_chip

    def at_chip(k):
        return (lax.div(k, n_lon) * 2 + core, lax.rem(k, n_lon), lev)

    pair = (lat + 1 - 2 * core, lon, lev)
    north = (wrap(lat - 1, n_lat), lon, lev)
    south = (wrap(lat + 1, n_lat), lon, lev)
    west = (lat, wrap(lon - 1, n_lon), lev)
    east = (lat, wrap(lon + 1, n_lon), lev)
    below = (lat, lon, wrap(lev - 1, n_lev))
    above = (lat, lon, wrap(lev + 1, n_lev))

    def remote(src, dst, ss, rs, device):
        return pltpu.make_async_remote_copy(
            src_ref=src, dst_ref=dst, send_sem=ss, recv_sem=rs,
            device_id=device, device_id_type=MESH,
        )

    def lanes(r, count=1):
        if isinstance(r, int):
            return pl.ds(r * LANES, count * LANES)
        return pl.ds(pl.multiple_of(r * LANES, LANES), count * LANES)

    inputs = [
        pltpu.make_async_copy(s, d, in_sem.at[i])
        for i, (s, d) in enumerate(
            ((hidden_ref, hid_v), (gamma_ref, gamma_v), (target_ref, tgt_v), (weight_ref, w_v))
        )
    ]
    for c in inputs:
        c.start()

    barrier = pltpu.get_barrier_semaphore()

    def greet(device):
        pl.semaphore_signal(barrier, inc=1, device_id=device, device_id_type=MESH)

    greet(pair)
    greet((n_lat - 1 - lat, lon, lev))

    def greet_chip(j, c):
        greet(at_chip(wrap(chip + j, n_chip)))
        return c

    lax.fori_loop(1, n_chip, greet_chip, 0)

    def greet_lev(j, c):
        greet((lat, lon, wrap(lev + j, n_lev)))
        return c

    lax.fori_loop(1, n_lev, greet_lev, 0)

    inputs[0].wait()
    hf[...] = hid_v[...].astype(F32).reshape(nn * rows, LANES)

    def spread(i, c):
        hx[:, lanes(i + 1)] = hf[pl.ds(i, nn, stride=rows), :]
        return c

    lax.fori_loop(0, rows, spread, 0)
    hh_send[0] = hx[:, lanes(1)].astype(BF16)
    hh_send[1] = hx[:, lanes(rows)].astype(BF16)
    pl.semaphore_wait(barrier, 2 + (n_chip - 1) + (n_lev - 1))

    sends = []

    def go(copy):
        copy.start()
        sends.append(copy)
        return copy

    row_copies = [
        go(remote(hh_send.at[0], hh_recv.at[1], row_ss.at[0], row_rs.at[0], north)),
        go(remote(hh_send.at[1], hh_recv.at[0], row_ss.at[1], row_rs.at[1], south)),
    ]

    def make_sel(r, c):
        k = lax.broadcasted_iota(jnp.int32, (LANES, LANES), 0)
        e = lax.broadcasted_iota(jnp.int32, (LANES, LANES), 1)
        hit = ((k == LANES - 1) & (e == r)) | ((k == 0) & (e == 32 + r))
        sel[lanes(r), :] = jnp.where(hit, 1.0, 0.0).astype(BF16)
        ki = lax.broadcasted_iota(jnp.int32, (2 * LANES, 2 * LANES), 0)
        o = lax.broadcasted_iota(jnp.int32, (2 * LANES, 2 * LANES), 1)
        low = ki < LANES
        hit = (
            (low & (o < LANES) & (ki == o - 1))
            | (low & (o >= LANES) & (ki == o - LANES + 1))
            | ((o == 0) & (ki == LANES + r))
            | ((o == 2 * LANES - 1) & (ki == LANES + 32 + r))
        )
        sr[r] = jnp.where(hit, 1.0, 0.0).astype(BF16)
        return c

    lax.fori_loop(0, rpad, make_sel, 0)

    inputs[1].wait()
    gamma = gamma_v[...]
    g_hi, g_lo = split(gamma)
    g3[...] = jnp.concatenate([g_hi, g_lo, g_hi], axis=1)
    g_hi, g_lo = split(gamma.T)
    gt3[...] = jnp.concatenate([g_hi, g_lo, g_hi], axis=1)
    eye = lax.broadcasted_iota(jnp.int32, (nn, nn), 0) == lax.broadcasted_iota(
        jnp.int32, (nn, nn), 1
    )
    beta_col = jnp.sum(jnp.where(eye, beta_ref[...], 0.0), axis=1, keepdims=True)
    eye_c = lax.broadcasted_iota(jnp.int32, (chans, chans), 0) == lax.broadcasted_iota(
        jnp.int32, (chans, chans), 1
    )
    bias_col = jnp.sum(jnp.where(eye_c, bias_ref[...], 0.0), axis=1, keepdims=True)

    def root_of(x):
        s_hi, s_lo = split(x * x)
        total = dot(g3[...], jnp.concatenate([s_hi, s_hi, s_lo], axis=0))
        return jnp.sqrt(beta_col + total), s_hi, s_lo

    def root_tile(t, c):
        at = lanes(2 * t, 2)
        x = hx[:, lanes(2 * t + 1, 2)]
        root, s_hi, s_lo = root_of(x)
        root_s[:, at] = root
        hr_s[:, at] = x * (0.5 / root)
        sqh[:, at] = s_hi
        sql[:, at] = s_lo
        us[nn : 2 * nn, lanes(2 * t + 1, 2)] = (x * root).astype(BF16)
        return c

    lax.fori_loop(0, rows // 2, root_tile, 0)

    for c in row_copies:
        c.wait_recv()
    north_in = jnp.where(lat > 0, 1.0, 0.0).astype(F32)
    south_in = jnp.where(lat < n_lat - 1, 1.0, 0.0).astype(F32)
    x = jnp.concatenate(
        [hh_recv[0].astype(F32) * north_in, hh_recv[1].astype(F32) * south_in], axis=1
    )
    root, _, _ = root_of(x)
    edge = (x * root).astype(BF16)
    us[nn : 2 * nn, lanes(0)] = edge[:, :LANES]
    us[nn : 2 * nn, lanes(rpad - 1)] = edge[:, LANES:]

    eu_send[...] = dot(us[nn : 2 * nn, :], sel[...]).astype(BF16)
    eu_copies = [
        go(remote(eu_send, eu_recv.at[0], eu_ss.at[0], eu_rs.at[0], east)),
        go(remote(eu_send, eu_recv.at[1], eu_ss.at[1], eu_rs.at[1], west)),
    ]

    inputs[3].wait()
    order = []
    for p in range(2):
        for a in range(2):
            for v in range(2):
                for q in range(2):
                    b = v if q else 1 - v
                    order.append(4 * (2 * p + q) + 2 * a + b)
    for g in range(4):
        block = jnp.concatenate([w_v[t] for t in order[4 * g : 4 * g + 4]], axis=0)
        wt[:, 4 * chans * g : 4 * chans * (g + 1)] = block.T

    inputs[2].wait()

    def widen(k, c):
        span = chans * rows
        tf[pl.ds(pl.multiple_of(k * span, span), span), :] = (
            tgt_v[k].astype(F32).reshape(span, LANES)
        )
        return c

    lax.fori_loop(0, 4, widen, 0)
    bacc[...] = jnp.zeros_like(bacc)
    gs[0, : 2 * chans, lanes(0)] = jnp.zeros((2 * chans, LANES), BF16)
    gs[1, : 2 * chans, lanes(rpad - 1)] = jnp.zeros((2 * chans, LANES), BF16)

    for c in eu_copies:
        c.wait_recv()
    lane = lax.broadcasted_iota(jnp.int32, (nn, LANES), 1)
    eu_send_mix = jnp.where(lane < 32, eu_recv[0].astype(F32), eu_recv[1].astype(F32))
    eu_mix = eu_send_mix.astype(BF16)

    def shift_u(r, c):
        y = dot(jnp.concatenate([us[nn : 2 * nn, lanes(r)], eu_mix], axis=1), sr[r])
        us[:nn, lanes(r)] = y[:, :LANES].astype(BF16)
        us[2 * nn :, lanes(r)] = y[:, LANES:].astype(BF16)
        return c

    lax.fori_loop(0, rpad, shift_u, 0)

    def recon_tile(it, c):
        t = lax.rem(it + rows // 2 - 1, rows // 2)
        for p in range(2):
            area = [area_ref[lat * 2 * rows + p * rows + 2 * t + i] for i in range(2)]
            for q in range(2):
                phase = 2 * p + q
                moved = jnp.concatenate(
                    [us[q * nn : (q + 2) * nn, lanes(2 * t + p + a, 2)] for a in range(2)], axis=0
                )
                w = jnp.concatenate([w_v[4 * phase + k] for k in range(4)], axis=1)
                recon = dot(w, moved) + bias_col
                total = jnp.zeros((chans, LANES), F32)
                for i in range(2):
                    want = tf[pl.ds(phase * chans * rows + 2 * t + i, chans, stride=rows), :]
                    diff = (recon[:, i * LANES : (i + 1) * LANES] - want) * area[i]
                    total = total + diff
                    gs[p, q * chans : (q + 1) * chans, lanes(2 * t + i + 1)] = diff.astype(BF16)
                bacc[:chans, :] += total
        return c

    lax.fori_loop(0, 2, recon_tile, 0)
    top, bottom = gs.at[0, : 2 * chans], gs.at[1, : 2 * chans]
    grow_copies = [
        go(remote(gs.at[0, 0 : 2 * chans, lanes(1)], gs.at[0, 0 : 2 * chans, lanes(rpad - 1)],
                  grow_ss.at[0], grow_rs.at[0], north)),
        go(remote(gs.at[1, 0 : 2 * chans, lanes(rows)], gs.at[1, 0 : 2 * chans, lanes(0)],
                  grow_ss.at[1], grow_rs.at[1], south)),
    ]
    lax.fori_loop(2, rows // 2, recon_tile, 0)
    for c in grow_copies:
        c.wait_recv()
    gs[0, : 2 * chans, lanes(rpad - 1)] = (
        gs[0, : 2 * chans, lanes(rpad - 1)].astype(F32) * south_in
    ).astype(BF16)
    gs[1, : 2 * chans, lanes(0)] = (
        gs[1, : 2 * chans, lanes(0)].astype(F32) * north_in
    ).astype(BF16)
    for p in range(2):
        eg_send[p] = dot(gs[p, : 2 * chans, :], sel[...]).astype(BF16)
    eg_copies = [
        go(remote(eg_send.at[:, 0:chans], eg_recv.at[:, 0:chans], eg_ss.at[0], eg_rs.at[0], west)),
        go(remote(eg_send.at[:, chans : 2 * chans], eg_recv.at[:, chans : 2 * chans],
                  eg_ss.at[1], eg_rs.at[1], east)),
    ]

    per_tap = chans // half

    def grad_taps(slot, p):
        for q in range(2):
            for a in range(2):
                y = dot_nt(
                    gs[p, q * chans : (q + 1) * chans, lanes(1, rows)],
                    us[q * nn : (q + 2) * nn, lanes(p + a, rows)],
                )
                for b in range(2):
                    for k in range(per_tap):
                        dw[slot, (4 * q + 2 * a + b) * per_tap + k] = y[
                            k * half : (k + 1) * half, b * nn : (b + 1) * nn
                        ]

    grad_taps(0, 1 - core)
    pw = go(remote(dw.at[0], dwp, pw_ss, pw_rs, pair))
    grad_taps(1, core)

    for c in eg_copies:
        c.wait_recv()

    def shift_g(r, c):
        for p in range(2):
            rr = r + 1 - p
            y = dot(jnp.concatenate([gs[p, : 2 * chans, lanes(rr)], eg_recv[p]], axis=1), sr[rr])
            gs[p, 2 * chans : 3 * chans, lanes(rr)] = y[:chans, LANES:].astype(BF16)
            gs[p, 3 * chans :, lanes(rr)] = y[chans:, :LANES].astype(BF16)
        return c

    lax.fori_loop(0, rows + 1, shift_g, 0)

    def grad_rows(k):
        moved = jnp.concatenate(
            [gs[p, :, lanes(2 * k + 2 - p - a, 2)] for p in range(2) for a in range(2)], axis=0
        )
        y = dot(wt[...], moved)
        gu[2 * k] = y[:, :LANES]
        gu[2 * k + 1] = y[:, LANES:]

    far = n_lev // 2
    rs_copies = {}

    def rs_send(way, s, h, first):
        owner = wrap(lev + (far + 1 - s if way else s - far - 1), n_lev)
        row = 2 * owner + h
        if first:
            src = gu.at[row]
        else:
            rs_copies[way, s - 1, h].wait_recv()
            abuf[way, s, h] = gu[row] + arecv[way, s - 1, h]
            src = abuf.at[way, s, h]
        rs_copies[way, s, h] = go(
            remote(src, arecv.at[way, s, h], a_ss.at[way, s, h], a_rs.at[way, s, h],
                   above if way else below)
        )

    grad_rows(wrap(lev + far, n_lev))
    rs_send(0, 1, 0, True)
    rs_send(1, 1, 1, True)
    grad_rows(wrap(lev + far - 1, n_lev))
    rs_send(1, 2, 0, True)
    grad_rows(wrap(lev + far + 1, n_lev))
    rs_send(0, 2, 1, True)

    def over_chips(make):
        def start(j, c):
            make(j).start()
            return c

        def arrive(j, c):
            make(j).wait_recv()
            return c

        def sent(j, c):
            make(j).wait_send()
            return c

        lax.fori_loop(1, n_chip, start, 0)
        return (
            lambda: lax.fori_loop(1, n_chip, arrive, 0),
            lambda: lax.fori_loop(1, n_chip, sent, 0),
        )

    def rb_make(j):
        k = wrap(chip + j, n_chip)
        return remote(rsb.at[k], rsr.at[j], rb_ss.at[j], rb_rs.at[j], at_chip(k))

    pw.wait_recv()

    def join(k, c):
        dw[1, k] = dw[1, k] + dwp[k]
        rsb[k] = dw[1, k].astype(BF16)
        return c

    lax.fori_loop(0, n_chip, join, 0)
    rb_arrive, rb_sent = over_chips(rb_make)

    rs_send(0, 2, 0, False)
    rs_send(1, 2, 1, False)
    grad_rows(wrap(lev + far - 2, n_lev))
    grad_rows(wrap(lev + far + 2, n_lev))
    for way, h in ((0, 1), (1, 0), (0, 0), (1, 1)):
        rs_send(way, 3, h, False)
    grad_rows(wrap(lev + 1, n_lev))
    grad_rows(wrap(lev + n_lev - 1, n_lev))
    grad_rows(lev)

    def mix_tile(t, acc):
        at = lanes(2 * t, 2)
        g = jnp.concatenate([gu[2 * t], gu[2 * t + 1]], axis=1)
        mixing = g * hr_s[:, at]
        m_hi, m_lo = split(mixing)
        mh[:, at] = m_hi
        ml[:, at] = m_lo
        return acc + mixing[:, :LANES] + mixing[:, LANES:]

    msum = lax.fori_loop(0, rows // 2, mix_tile, jnp.zeros((nn, LANES), F32))
    beta_part = jnp.sum(msum, axis=1, keepdims=True)
    bias_part = jnp.sum(bacc[...].T, axis=0, keepdims=True)
    ext[:, :nn] = dot_nt(mh[...], sqh[...]) + (
        dot_nt(ml[...], sqh[...]) + dot_nt(mh[...], sql[...])
    )
    lane = lax.broadcasted_iota(jnp.int32, (nn, LANES), 1)
    ext[:, nn:] = jnp.where(lane == LANES - 1, beta_part, bias_part)
    mine = pl.multiple_of(core * (nn // 2), nn // 2)
    others = pl.multiple_of((1 - core) * (nn // 2), nn // 2)
    pe = go(remote(ext.at[pl.ds(others, nn // 2)], extp, pe_ss, pe_rs, pair))

    for way, h in ((0, 1), (1, 0), (0, 0), (1, 1)):
        rs_send(way, 4, h, False)

    rb_arrive()

    def add_taps(j, acc):
        return acc + rsr[j].astype(F32)

    wg[core, chip] = lax.fori_loop(1, n_chip, add_taps, dw[1, chip]) * (1.0 / total_cells)

    def ab_make(j):
        k = wrap(chip + j, n_chip)
        return remote(
            wg.at[core, chip], wg.at[core, chip], ab_ss.at[j], ab_rs.at[j], at_chip(k)
        )

    ab_arrive, ab_sent = over_chips(ab_make)

    pe.wait_recv()

    def join_ext(k, c):
        at = pl.ds(pl.multiple_of(mine + k * share, share), share)
        exts[k] = ext[at, :] + extp[pl.ds(pl.multiple_of(k * share, share), share), :]
        return c

    lax.fori_loop(0, n_chip, join_ext, 0)
    extr[chip] = exts[chip]

    def rc_make(j):
        k = wrap(chip + j, n_chip)
        return remote(exts.at[k], extr.at[chip], rc_ss.at[j], rc_rs.at[j], at_chip(k))

    rc_arrive, rc_sent = over_chips(rc_make)

    for way in range(2):
        for h in range(2):
            rs_copies[way, 4, h].wait_recv()
    g = jnp.concatenate(
        [gu[2 * lev + h] + (arecv[0, 4, h] + arecv[1, 4, h]) for h in range(2)], axis=1
    )
    at = lanes(2 * lev, 2)
    m_hi, m_lo = split(g * hr_s[:, at])
    back = dot(gt3[...], jnp.concatenate([m_hi, m_hi, m_lo], axis=0))
    gh = (g * root_s[:, at] + 2.0 * hx[:, lanes(2 * lev + 1, 2)] * back).astype(BF16)
    agr[2 * lev] = gh[:, :LANES]
    agr[2 * lev + 1] = gh[:, LANES:]

    ag_copies = {}

    def ag_send(s):
        for way in range(2):
            for h in range(2):
                if s == far and h != way:
                    continue
                if s > 1:
                    ag_copies[way, s - 1, h].wait_recv()
                owner = wrap(lev + (1 - s if way else s - 1), n_lev)
                block = agr.at[2 * owner + h]
                ag_copies[way, s, h] = go(
                    remote(block, block, g_ss.at[way, s, h], g_rs.at[way, s, h],
                           above if way else below)
                )

    def put(owner, h):
        row = 2 * owner + h
        gho[pl.ds(row, nn, stride=rows), :] = agr[row].astype(F32)

    def put_step(s):
        for way in range(2):
            for h in range(2):
                put(wrap(lev + (-s if way else s), n_lev), h)

    ag_send(1)
    put(lev, 0)
    put(lev, 1)

    rc_arrive()

    def add_ext(k, acc):
        return acc + extr[k]

    plane = lax.fori_loop(1, n_chip, add_ext, extr[0])
    gb_out[...] = plane[0:1, nn : nn + chans] * (1.0 / total_cells)
    extz[lev] = plane

    def z_make(j):
        return remote(
            extz.at[lev], extz.at[lev], z_ss.at[j], z_rs.at[j], (lat, lon, wrap(lev + j, n_lev))
        )

    for j in range(1, n_lev):
        z_make(j).start()

    ag_send(2)
    put_step(1)

    ab_arrive()
    pg = go(remote(wg.at[core], wg.at[core], pg_ss, pg_rs, pair))
    for j in range(1, n_lev):
        z_make(j).wait_recv()
    whole = extz[0]
    for k in range(1, n_lev):
        whole = whole + extz[k]
    extg[core, chip] = whole * (1.0 / total_cells)

    def ac_make(j):
        k = wrap(chip + j, n_chip)
        return remote(
            extg.at[core, chip], extg.at[core, chip], ac_ss.at[j], ac_rs.at[j], at_chip(k)
        )

    ac_arrive, ac_sent = over_chips(ac_make)
    ag_send(3)
    put_step(2)
    ac_arrive()
    pc = go(remote(extg.at[core], extg.at[core], pc_ss, pc_rs, pair))
    ag_send(4)
    for way in range(2):
        ag_copies[way, 3, 1 - way].wait_recv()
    put_step(3)
    pg.wait_recv()
    gw_copy = pltpu.make_async_copy(wg, gw_out, out_sem.at[0])
    gw_copy.start()
    pc.wait_recv()
    full = extg[...].reshape(nn, nn + LANES)
    gg_out[...] = full[:, :nn]
    gbeta_out[...] = jnp.sum(
        jnp.where(eye, full[:, nn + LANES - 1 : nn + LANES], 0.0), axis=0, keepdims=True
    )
    for way in range(2):
        ag_copies[way, far, way].wait_recv()
        put(wrap(lev + far, n_lev), way)
    gh_copy = pltpu.make_async_copy(gho, gh_out, out_sem.at[1])
    gh_copy.start()

    for c in sends:
        c.wait_send()
    rb_sent()
    ab_sent()
    rc_sent()
    ac_sent()
    for j in range(1, n_lev):
        z_make(j).wait_send()
    gw_copy.wait()
    gh_copy.wait()


def local(sizes, target, hidden, weight, bias, gamma, beta):
    n_lat, n_lon, n_lev = sizes
    nn, rows, cols = hidden.shape
    chans = weight.shape[1]
    taps = weight.shape[0]
    n_chip = n_lat // 2 * n_lon
    half = taps // 2 * chans // n_chip
    share = nn // 2 // n_chip
    cells = rows * cols
    rpad = rows + 2
    total_rows = rows * n_lat
    total_cells = total_rows * cols * n_lon
    far = n_lev // 2
    at = np.arange(total_rows).reshape(n_lat, 1, rows) * 2.0 + np.arange(2).reshape(1, 2, 1)
    area = np.cos(math.pi * ((at + 0.5) / (2.0 * total_rows) - 0.5)).astype(np.float32)
    dims = (nn, rows, chans, n_lat, n_lon, n_lev, 4, total_cells)
    wide = nn + LANES
    V = pltpu.VMEM
    D = pltpu.SemaphoreType.DMA
    scratch = [
        V((nn, rows, cols), BF16), V((4, chans, rows, cols), BF16), V((taps, chans, nn), BF16),
        V((nn, nn), F32),
        V((nn * rows, cols), F32), V((4 * chans * rows, cols), F32), V((nn, rpad * cols), F32),
        V((nn, cells), F32), V((nn, cells), F32), V((nn, cells), BF16), V((nn, cells), BF16),
        V((nn, 3 * nn), BF16), V((nn, 3 * nn), BF16), V((nn, taps * chans), BF16),
        V((3 * nn, rpad * cols), BF16), V((2, 4 * chans, rpad * cols), BF16),
        V((rpad * cols, cols), BF16), V((rpad, 2 * cols, 2 * cols), BF16),
        V((2, nn, cols), BF16), V((2, nn, cols), BF16), V((nn, cols), BF16),
        V((2, nn, cols), BF16), V((2, 2 * chans, cols), BF16), V((2, 2 * chans, cols), BF16),
        V((2, n_chip, half, nn), F32), V((n_chip, half, nn), F32), V((n_chip, half, nn), BF16),
        V((n_chip, half, nn), BF16), V((2, n_chip, half, nn), F32),
        V((rows, nn, cols), F32), V((cols, cols), F32), V((nn, cells), BF16), V((nn, cells), BF16),
        V((nn, wide), F32), V((nn // 2, wide), F32), V((n_chip, share, wide), F32),
        V((n_chip, share, wide), F32), V((n_lev, share, wide), F32),
        V((2, n_chip, share, wide), F32),
        V((2, far + 1, 2, nn, cols), F32), V((2, far + 1, 2, nn, cols), F32),
        V((rows, nn, cols), BF16), V((nn * rows, cols), F32),
        D((4,)), D((2,)),
        D((2,)), D((2,)), D((2,)), D((2,)), D((2,)), D((2,)), D((2,)), D((2,)),
        D, D, D((n_chip,)), D((n_chip,)), D((n_chip,)), D((n_chip,)), D, D,
        D, D, D((n_chip,)), D((n_chip,)), D((n_lev,)), D((n_lev,)), D((n_chip,)), D((n_chip,)),
        D, D,
        D((2, far + 1, 2)), D((2, far + 1, 2)), D((2, far + 1, 2)), D((2, far + 1, 2)),
    ]
    hbm = pl.BlockSpec(memory_space=pl.ANY)
    vmem = pl.BlockSpec(memory_space=pltpu.VMEM)
    smem = pl.BlockSpec(memory_space=pltpu.SMEM)
    gh, gw, gb, gg, gbeta = pl.pallas_call(
        functools.partial(kernel, dims),
        out_shape=(
            jax.ShapeDtypeStruct((nn * rows, cols), F32),
            jax.ShapeDtypeStruct((2, n_chip, half, nn), F32),
            jax.ShapeDtypeStruct((1, chans), F32),
            jax.ShapeDtypeStruct((nn, nn), F32),
            jax.ShapeDtypeStruct((1, nn), F32),
        ),
        in_specs=[smem, hbm, hbm, hbm, vmem, hbm, vmem],
        out_specs=(hbm, hbm, vmem, vmem, vmem),
        scratch_shapes=scratch,
        compiler_params=pltpu.CompilerParams(
            collective_id=0, has_side_effects=True, vmem_limit_bytes=60 * 2**20
        ),
    )(
        jnp.asarray(area.reshape(-1)), hidden, target, weight, bias.reshape(1, chans),
        gamma, beta.reshape(1, nn),
    )
    return (
        gh.reshape(nn, rows, cols), gw.reshape(taps, chans, nn), gb.reshape(chans), gg,
        gbeta.reshape(nn),
    )


def solution(mesh):
    sizes = tuple(mesh.shape[a] for a in ("lat", "lon", "lev"))
    return jax.shard_map(
        functools.partial(local, sizes),
        mesh=mesh,
        in_specs=(
            P(None, "lev", "lat", "lon"),
            P(None, "lat", "lon"),
            P(None, "lev", None),
            P("lev"),
            P(),
            P(),
        ),
        out_specs=(P(None, "lat", "lon"), P(None, "lev", None), P("lev"), P(), P()),
        check_vma=False,
    )
```

```python
import functools
import math

import jax
import jax.numpy as jnp
import numpy as np
from jax import lax
from jax.experimental import pallas as pl
from jax.experimental.pallas import tpu as pltpu
from jax.sharding import PartitionSpec as P

F32 = jnp.float32
BF16 = jnp.bfloat16
MESH = pl.DeviceIdType.MESH
LANES = 128


def split(x):
    hi = x.astype(BF16)
    return hi, (x - hi.astype(F32)).astype(BF16)


def dot(a, b):
    return jnp.dot(a, b, preferred_element_type=F32)


def dot_nt(a, b):
    return lax.dot_general(a, b, (((1,), (1,)), ((), ())), preferred_element_type=F32)


def wrap(index, size):
    return lax.rem(index + size, size)


def kernel(
    dims,
    area_ref, hidden_ref, target_ref, weight_ref, bias_ref, gamma_ref, beta_ref,
    gh_out, gw_out, ext_out, gb_out,
    hid_v, tgt_v, w_v, gamma_v,
    hf, tf, hx, root_s, hr_s, sqh, sql, g3, gt3, wt,
    us, gs, sel, eu_send, eu_recv, eg_send, eg_recv, eg_corner,
    dw, dwp, rsb, rsr, wown,
    gu, bacc, mh, ml, ext, extp, exts, extr, extz, eown,
    abuf, arecv, ghown,
    in_sem, out_sem,
    row_ss, row_rs, eu_ss, eu_rs, grow_ss, grow_rs, eg_ss, eg_rs,
    pw_ss, pw_rs, rb_ss, rb_rs, ab_ss, ab_rs, pg_ss, pg_rs,
    pe_ss, pe_rs, rc_ss, rc_rs, z_ss, z_rs, ac_ss, ac_rs, pc_ss, pc_rs,
    a_ss, a_rs, g_ss, g_rs,
):
    nn, rows, chans, n_lat, n_lon, n_lev, n_y, total_cells = dims
    cells = rows * LANES
    rpad = rows + 2
    lat, lon, lev = lax.axis_index("lat"), lax.axis_index("lon"), lax.axis_index("lev")
    core = lax.rem(lat, 2)
    n_chip = (n_lat // 2) * n_lon
    n_xlo = n_lon // n_y
    chip = lax.div(lat, 2) * n_lon + lon
    half = 16 // 2 * chans // n_chip
    share = nn // 2 // n_chip

    def at_chip(k):
        return (lax.div(k, n_lon) * 2 + core, lax.rem(k, n_lon), lev)

    pair = (lat + 1 - 2 * core, lon, lev)
    north = (wrap(lat - 1, n_lat), lon, lev)
    south = (wrap(lat + 1, n_lat), lon, lev)
    west = (lat, wrap(lon - 1, n_lon), lev)
    east = (lat, wrap(lon + 1, n_lon), lev)
    below = (lat, lon, wrap(lev - 1, n_lev))
    above = (lat, lon, wrap(lev + 1, n_lev))

    def remote(src, dst, ss, rs, device):
        return pltpu.make_async_remote_copy(
            src_ref=src, dst_ref=dst, send_sem=ss, recv_sem=rs,
            device_id=device, device_id_type=MESH,
        )

    def lanes(r, count=1):
        if isinstance(r, int):
            return pl.ds(r * LANES, count * LANES)
        return pl.ds(pl.multiple_of(r * LANES, LANES), count * LANES)

    inputs = [
        pltpu.make_async_copy(s, d, in_sem.at[i])
        for i, (s, d) in enumerate(
            ((hidden_ref, hid_v), (gamma_ref, gamma_v), (target_ref, tgt_v), (weight_ref, w_v))
        )
    ]
    for c in inputs:
        c.start()

    barrier = pltpu.get_barrier_semaphore()

    def greet(device):
        pl.semaphore_signal(barrier, inc=1, device_id=device, device_id_type=MESH)

    corners = [
        (wrap(lat + i, n_lat), wrap(lon + j, n_lon), lev) for i in (-1, 1) for j in (-1, 1)
    ]
    northwest, northeast, southwest, southeast = corners
    for device in [north, south] + corners:
        greet(device)

    def greet_chip(j, c):
        greet(at_chip(wrap(chip + j, n_chip)))
        return c

    lax.fori_loop(1, n_chip, greet_chip, 0)

    def greet_lev(j, c):
        greet((lat, lon, wrap(lev + j, n_lev)))
        return c

    lax.fori_loop(1, n_lev, greet_lev, 0)

    inputs[0].wait()
    hf[...] = hid_v[...].astype(F32).reshape(nn * rows, LANES)

    def spread(i, c):
        hx[:, lanes(i + 1)] = hf[pl.ds(i, nn, stride=rows), :]
        return c

    lax.fori_loop(0, rows, spread, 0)
    def make_sel(r, c):
        k = lax.broadcasted_iota(jnp.int32, (LANES, LANES), 0)
        e = lax.broadcasted_iota(jnp.int32, (LANES, LANES), 1)
        last, first = k == LANES - 1, k == 0
        hit = (last & (e == r)) | (first & (e == 32 + r))
        hit = hit | ((r == rows) & ((last & (e == 0)) | (first & (e == 32))))
        hit = hit | ((r == 1) & ((last & (e == rows + 1)) | (first & (e == 33 + rows))))
        sel[lanes(r - 1), :] = jnp.where(hit, 1.0, 0.0).astype(BF16)
        return c

    lax.fori_loop(1, rows + 1, make_sel, 0)

    inputs[1].wait()
    gamma = gamma_v[...]
    g_hi, g_lo = split(gamma)
    g3[...] = jnp.concatenate([g_hi, g_lo, g_hi], axis=1)
    g_hi, g_lo = split(gamma.T)
    gt3[...] = jnp.concatenate([g_hi, g_lo, g_hi], axis=1)
    eye = lax.broadcasted_iota(jnp.int32, (nn, nn), 0) == lax.broadcasted_iota(
        jnp.int32, (nn, nn), 1
    )
    beta_col = jnp.sum(jnp.where(eye, beta_ref[...], 0.0), axis=1, keepdims=True)
    eye_c = lax.broadcasted_iota(jnp.int32, (chans, chans), 0) == lax.broadcasted_iota(
        jnp.int32, (chans, chans), 1
    )
    bias_col = jnp.sum(jnp.where(eye_c, bias_ref[...], 0.0), axis=1, keepdims=True)

    def root_of(x):
        s_hi, s_lo = split(x * x)
        total = dot(g3[...], jnp.concatenate([s_hi, s_hi, s_lo], axis=0))
        return jnp.sqrt(beta_col + total), s_hi, s_lo

    def root_tile(t, c):
        at = lanes(2 * t, 2)
        x = hx[:, lanes(2 * t + 1, 2)]
        root, s_hi, s_lo = root_of(x)
        root_s[:, at] = root
        hr_s[:, at] = x * (0.5 / root)
        sqh[:, at] = s_hi
        sql[:, at] = s_lo
        us[nn : 2 * nn, lanes(2 * t + 1, 2)] = (x * root).astype(BF16)
        return c

    lax.fori_loop(0, rows // 2, root_tile, 0, unroll=2)

    north_in = jnp.where(lat > 0, 1.0, 0.0).astype(F32)
    south_in = jnp.where(lat < n_lat - 1, 1.0, 0.0).astype(F32)
    eu_send[...] = dot(us[nn : 2 * nn, lanes(1, rows)], sel[...]).astype(BF16)

    pl.semaphore_wait(barrier, 6 + (n_chip - 1) + (n_lev - 1))

    sends = []

    def go(copy):
        copy.start()
        sends.append(copy)
        return copy

    mid = slice(nn, 2 * nn)
    eu_copies = [
        go(remote(us.at[mid, lanes(1)], us.at[mid, lanes(rpad - 1)],
                  row_ss.at[0], row_rs.at[0], north)),
        go(remote(us.at[mid, lanes(rows)], us.at[mid, lanes(0)],
                  row_ss.at[1], row_rs.at[1], south)),
    ] + [
        go(remote(eu_send, eu_recv.at[i], eu_ss.at[i], eu_rs.at[i], device))
        for i, device in enumerate((east, west, southeast, southwest, northeast, northwest))
    ]

    inputs[3].wait()
    order = []
    for p in range(2):
        for a in range(2):
            for v in range(2):
                for q in range(2):
                    b = v if q else 1 - v
                    order.append(4 * (2 * p + q) + 2 * a + b)
    for g in range(4):
        block = jnp.concatenate([w_v[t] for t in order[4 * g : 4 * g + 4]], axis=0)
        wt[:, 4 * chans * g : 4 * chans * (g + 1)] = block.T

    inputs[2].wait()

    def widen(k, c):
        span = chans * rows
        tf[pl.ds(pl.multiple_of(k * span, span), span), :] = (
            tgt_v[k].astype(F32).reshape(span, LANES)
        )
        return c

    lax.fori_loop(0, 4, widen, 0)
    bacc[...] = jnp.zeros_like(bacc)
    gs[0, : 2 * chans, lanes(0)] = jnp.zeros((2 * chans, LANES), BF16)
    gs[1, : 2 * chans, lanes(rpad - 1)] = jnp.zeros((2 * chans, LANES), BF16)

    for c in eu_copies:
        c.wait_recv()
    us[mid, lanes(0)] = (us[mid, lanes(0)].astype(F32) * north_in).astype(BF16)
    us[mid, lanes(rpad - 1)] = (us[mid, lanes(rpad - 1)].astype(F32) * south_in).astype(BF16)
    lane = lax.broadcasted_iota(jnp.int32, (nn, LANES), 1)
    eu_mix = jnp.where(lane < 32, eu_recv[0].astype(F32), eu_recv[1].astype(F32))
    for i, at, keep in (
        (2, 0, north_in), (3, 32, north_in), (4, rows + 1, south_in), (5, rows + 33, south_in)
    ):
        eu_mix = jnp.where(lane == at, eu_recv[i].astype(F32) * keep, eu_mix)

    def from_west(x, e, r):
        at = lax.broadcasted_iota(jnp.int32, x.shape, 1)
        return jnp.where(at == 0, pltpu.roll(e, LANES - r, 1), pltpu.roll(x, 1, 1))

    def from_east(x, e, r):
        at = lax.broadcasted_iota(jnp.int32, x.shape, 1)
        edge = pltpu.roll(e, LANES - 33 - r, 1)
        return jnp.where(at == LANES - 1, edge, pltpu.roll(x, LANES - 1, 1))

    def shift_u(r, c):
        x = us[mid, lanes(r)].astype(F32)
        us[:nn, lanes(r)] = from_west(x, eu_mix, r).astype(BF16)
        us[2 * nn :, lanes(r)] = from_east(x, eu_mix, r).astype(BF16)
        return c

    lax.fori_loop(0, rpad, shift_u, 0, unroll=3)

    def recon_tile(it, c):
        t = lax.rem(it + rows // 2 - 1, rows // 2)
        for p in range(2):
            area = [area_ref[lat * 2 * rows + p * rows + 2 * t + i] for i in range(2)]
            for q in range(2):
                phase = 2 * p + q
                moved = jnp.concatenate(
                    [us[q * nn : (q + 2) * nn, lanes(2 * t + p + a, 2)] for a in range(2)], axis=0
                )
                w = jnp.concatenate([w_v[4 * phase + k] for k in range(4)], axis=1)
                recon = dot(w, moved) + bias_col
                total = jnp.zeros((chans, LANES), F32)
                for i in range(2):
                    want = tf[pl.ds(phase * chans * rows + 2 * t + i, chans, stride=rows), :]
                    diff = (recon[:, i * LANES : (i + 1) * LANES] - want) * area[i]
                    total = total + diff
                    gs[p, q * chans : (q + 1) * chans, lanes(2 * t + i + 1)] = diff.astype(BF16)
                bacc[:chans, :] += total
        return c

    lax.fori_loop(0, 2, recon_tile, 0, unroll=2)
    grow_copies = [
        go(remote(gs.at[0, 0 : 2 * chans, lanes(1)], gs.at[0, 0 : 2 * chans, lanes(rpad - 1)],
                  grow_ss.at[0], grow_rs.at[0], north)),
        go(remote(gs.at[1, 0 : 2 * chans, lanes(rows)], gs.at[1, 0 : 2 * chans, lanes(0)],
                  grow_ss.at[1], grow_rs.at[1], south)),
    ]
    lax.fori_loop(2, rows // 2, recon_tile, 0, unroll=2)
    for p in range(2):
        eg_send[p] = dot(gs[p, : 2 * chans, lanes(1, rows)], sel[...]).astype(BF16)
    east_part, west_part = slice(0, chans), slice(chans, 2 * chans)
    eg_copies = [
        go(remote(src, dst, eg_ss.at[i], eg_rs.at[i], device))
        for i, (src, dst, device) in enumerate((
            (eg_send.at[:, east_part], eg_recv.at[:, east_part], west),
            (eg_send.at[:, west_part], eg_recv.at[:, west_part], east),
            (eg_send.at[0, east_part], eg_corner.at[0, east_part], northwest),
            (eg_send.at[0, west_part], eg_corner.at[0, west_part], northeast),
            (eg_send.at[1, east_part], eg_corner.at[1, east_part], southwest),
            (eg_send.at[1, west_part], eg_corner.at[1, west_part], southeast),
        ))
    ]

    per_tap = chans // half

    def grad_taps(slot, p):
        for q in range(2):
            for a in range(2):
                y = dot_nt(
                    gs[p, q * chans : (q + 1) * chans, lanes(1, rows)],
                    us[q * nn : (q + 2) * nn, lanes(p + a, rows)],
                )
                for b in range(2):
                    for k in range(per_tap):
                        dw[slot, (4 * q + 2 * a + b) * per_tap + k] = y[
                            k * half : (k + 1) * half, b * nn : (b + 1) * nn
                        ]

    grad_taps(0, 1 - core)
    pw = go(remote(dw.at[0], dwp, pw_ss, pw_rs, pair))

    for c in grow_copies + eg_copies:
        c.wait_recv()
    gs[0, : 2 * chans, lanes(rpad - 1)] = (
        gs[0, : 2 * chans, lanes(rpad - 1)].astype(F32) * south_in
    ).astype(BF16)
    gs[1, : 2 * chans, lanes(0)] = (
        gs[1, : 2 * chans, lanes(0)].astype(F32) * north_in
    ).astype(BF16)
    lane = lax.broadcasted_iota(jnp.int32, (2 * chans, LANES), 1)
    eg_mix = []
    for p, at, keep in ((0, rows + 1, south_in), (1, 0, north_in)):
        corner = eg_corner[p].astype(F32) * keep
        eg_mix.append(
            jnp.where((lane == at) | (lane == at + 32), corner, eg_recv[p].astype(F32))
        )

    def shift_g(r, c):
        for p in range(2):
            rr = r + 1 - p
            x = gs[p, : 2 * chans, lanes(rr)].astype(F32)
            gs[p, 2 * chans : 3 * chans, lanes(rr)] = from_east(
                x[:chans], eg_mix[p][:chans], rr
            ).astype(BF16)
            gs[p, 3 * chans :, lanes(rr)] = from_west(
                x[chans:], eg_mix[p][chans:], rr
            ).astype(BF16)
        return c

    lax.fori_loop(0, rows + 1, shift_g, 0)

    def grad_rows(*chunks):
        moved = jnp.concatenate(
            [
                jnp.concatenate([gs[p, :, lanes(2 * k + 2 - p - a, 2)] for k in chunks], axis=1)
                for p in range(2)
                for a in range(2)
            ],
            axis=0,
        )
        y = dot(wt[...], moved)
        for i, k in enumerate(chunks):
            gu[2 * k] = y[:, 2 * i * LANES : (2 * i + 1) * LANES]
            gu[2 * k + 1] = y[:, (2 * i + 1) * LANES : (2 * i + 2) * LANES]

    far = n_lev // 2
    rs_copies = {}

    def rs_send(way, s, h, first):
        owner = wrap(lev + (far + 1 - s if way else s - far - 1), n_lev)
        row = 2 * owner + h
        if first:
            src = gu.at[row]
        else:
            rs_copies[way, s - 1, h].wait_recv()
            abuf[way, s, h] = gu[row] + arecv[way, s - 1, h]
            src = abuf.at[way, s, h]
        rs_copies[way, s, h] = go(
            remote(src, arecv.at[way, s, h], a_ss.at[way, s, h], a_rs.at[way, s, h],
                   above if way else below)
        )

    grad_rows(wrap(lev + far, n_lev))
    rs_send(0, 1, 0, True)
    rs_send(1, 1, 1, True)
    grad_rows(wrap(lev + far - 1, n_lev), wrap(lev + far + 1, n_lev))
    rs_send(1, 2, 0, True)
    rs_send(0, 2, 1, True)
    grad_taps(1, core)

    def over_chips(make):
        def start(j, c):
            make(j).start()
            return c

        def arrive(j, c):
            make(j).wait_recv()
            return c

        def sent(j, c):
            make(j).wait_send()
            return c

        lax.fori_loop(1, n_chip, start, 0)
        return (
            lambda: lax.fori_loop(1, n_chip, arrive, 0),
            lambda: lax.fori_loop(1, n_chip, sent, 0),
        )

    def rb_make(j):
        k = wrap(chip + j, n_chip)
        return remote(rsb.at[k], rsr.at[j], rb_ss.at[j], rb_rs.at[j], at_chip(k))

    rs_send(0, 2, 0, False)
    rs_send(1, 2, 1, False)
    grad_rows(wrap(lev + far - 2, n_lev), wrap(lev + far + 2, n_lev))
    pw.wait_recv()

    def join(k, c):
        dw[1, k] = dw[1, k] + dwp[k]
        rsb[k] = dw[1, k].astype(BF16)
        return c

    lax.fori_loop(0, n_chip, join, 0)
    rb_arrive, rb_sent = over_chips(rb_make)

    for way, h in ((0, 1), (1, 0), (0, 0), (1, 1)):
        rs_send(way, 3, h, False)
    grad_rows(wrap(lev + 1, n_lev), wrap(lev + n_lev - 1, n_lev))
    grad_rows(lev)

    def mix_tile(t, acc):
        at = lanes(2 * t, 2)
        g = jnp.concatenate([gu[2 * t], gu[2 * t + 1]], axis=1)
        mixing = g * hr_s[:, at]
        m_hi, m_lo = split(mixing)
        mh[:, at] = m_hi
        ml[:, at] = m_lo
        return acc + mixing[:, :LANES] + mixing[:, LANES:]

    msum = lax.fori_loop(0, rows // 2, mix_tile, jnp.zeros((nn, LANES), F32))
    beta_part = jnp.sum(msum, axis=1, keepdims=True)
    bias_part = jnp.sum(bacc[...].T, axis=0, keepdims=True)
    ext[:, :nn] = dot_nt(mh[...], sqh[...]) + (
        dot_nt(ml[...], sqh[...]) + dot_nt(mh[...], sql[...])
    )
    lane = lax.broadcasted_iota(jnp.int32, (nn, LANES), 1)
    ext[:, nn:] = jnp.where(lane == LANES - 1, beta_part, bias_part)
    mine = pl.multiple_of(core * (nn // 2), nn // 2)
    others = pl.multiple_of((1 - core) * (nn // 2), nn // 2)
    pe = go(remote(ext.at[pl.ds(others, nn // 2)], extp, pe_ss, pe_rs, pair))

    for way, h in ((0, 1), (1, 0), (0, 0), (1, 1)):
        rs_send(way, 4, h, False)

    rb_arrive()

    def add_taps(j, acc):
        return acc + rsr[j].astype(F32)

    wown[...] = lax.fori_loop(1, n_chip, add_taps, dw[1, chip]) * (1.0 / total_cells)
    own_copies = [pltpu.make_async_copy(wown, gw_out.at[core, chip], out_sem.at[0])]
    own_copies[0].start()

    def ab_make(j):
        k = wrap(chip + j, n_chip)
        return remote(
            wown, gw_out.at[core, chip], ab_ss.at[j], ab_rs.at[j], at_chip(k)
        )

    ab_arrive, ab_sent = over_chips(ab_make)

    pe.wait_recv()

    def join_ext(k, c):
        at = pl.ds(pl.multiple_of(mine + k * share, share), share)
        exts[k] = ext[at, :] + extp[pl.ds(pl.multiple_of(k * share, share), share), :]
        return c

    lax.fori_loop(0, n_chip, join_ext, 0)
    extr[chip] = exts[chip]

    def rc_make(j):
        k = wrap(chip + j, n_chip)
        return remote(exts.at[k], extr.at[chip], rc_ss.at[j], rc_rs.at[j], at_chip(k))

    rc_arrive, rc_sent = over_chips(rc_make)

    for way in range(2):
        for h in range(2):
            rs_copies[way, 4, h].wait_recv()
    g = jnp.concatenate(
        [gu[2 * lev + h] + (arecv[0, 4, h] + arecv[1, 4, h]) for h in range(2)], axis=1
    )
    at = lanes(2 * lev, 2)
    m_hi, m_lo = split(g * hr_s[:, at])
    back = dot(gt3[...], jnp.concatenate([m_hi, m_hi, m_lo], axis=0))
    gh = (g * root_s[:, at] + 2.0 * hx[:, lanes(2 * lev + 1, 2)] * back).astype(BF16)
    ghown[0] = gh[:, :LANES]
    ghown[1] = gh[:, LANES:]
    own_copies.append(
        pltpu.make_async_copy(ghown, gh_out.at[pl.ds(2 * lev, 2)], out_sem.at[1])
    )
    own_copies[1].start()

    ag_copies = {}

    def ag_send(way, hops, origin, kind, src=None):
        step = hops if way else -hops
        owner = wrap(lev - origin if way else lev + origin, n_lev)
        if kind == 2:
            rows_of = pl.ds(2 * owner, 2)
        else:
            rows_of = pl.ds(2 * owner + kind, 1)
        block = gh_out.at[rows_of]
        ag_copies[way, hops + origin] = go(
            remote(block if src is None else src, block, g_ss.at[way, hops + origin],
                   g_rs.at[way, hops + origin], (lat, lon, wrap(lev + step, n_lev)))
        )

    for way in range(2):
        ag_send(way, 1, 0, 2, ghown)
    for way in range(2):
        ag_send(way, 2, 0, 2, ghown)

    rc_arrive()

    def add_ext(k, acc):
        return acc + extr[k]

    plane = lax.fori_loop(1, n_chip, add_ext, extr[0])
    gb_out[...] = plane[0:1, nn : nn + chans] * (1.0 / total_cells)
    extz[lev] = plane

    def z_make(j):
        return remote(
            extz.at[lev], extz.at[lev], z_ss.at[j], z_rs.at[j], (lat, lon, wrap(lev + j, n_lev))
        )

    for j in range(1, n_lev):
        z_make(j).start()

    for way in range(2):
        ag_copies[way, 1].wait_recv()
        ag_send(way, 2, 1, 2)

    ab_arrive()
    own_copies[0].wait()
    pg = go(remote(gw_out.at[core], gw_out.at[core], pg_ss, pg_rs, pair))

    for way in range(2):
        ag_copies[way, 2].wait_recv()
        ag_send(way, 2, 2, way)

    for j in range(1, n_lev):
        z_make(j).wait_recv()
    whole = extz[0]
    for k in range(1, n_lev):
        whole = whole + extz[k]
    eown[...] = whole * (1.0 / total_cells)
    own_copies.append(pltpu.make_async_copy(eown, ext_out.at[core, chip], out_sem.at[2]))
    own_copies[2].start()

    def ac_make(j):
        k = wrap(chip + j, n_chip)
        return remote(eown, ext_out.at[core, chip], ac_ss.at[j], ac_rs.at[j], at_chip(k))

    ac_arrive, ac_sent = over_chips(ac_make)
    ac_arrive()
    own_copies[2].wait()
    pc = go(remote(ext_out.at[core], ext_out.at[core], pc_ss, pc_rs, pair))
    pg.wait_recv()
    for way in range(2):
        ag_copies[way, 3].wait_recv()
        ag_copies[way, 4].wait_recv()
    pc.wait_recv()
    own_copies[1].wait()

    for c in sends:
        c.wait_send()
    rb_sent()
    ab_sent()
    rc_sent()
    ac_sent()
    for j in range(1, n_lev):
        z_make(j).wait_send()


def finish(
    dims, agr_ref, wg_ref, ext_ref, gb_ref,
    gh_out, gw_out, gg_out, gbeta_out, gb_out,
    agr, gho, gw_v, in_sem, out_sem, gw_sem,
):
    nn, rows, parts = dims
    step = nn // parts

    def fetch(k):
        at = pl.ds(k * step, step)
        return pltpu.make_async_copy(agr_ref.at[:, at], agr.at[:, at], in_sem.at[k])

    def store(k):
        at = pl.ds(k * step * rows, step * rows)
        return pltpu.make_async_copy(gho.at[at], gh_out.at[at], out_sem.at[k])

    def fetch_gw(k):
        return pltpu.make_async_copy(wg_ref.at[k], gw_v.at[k], gw_sem.at[0, k])

    def store_gw(k):
        return pltpu.make_async_copy(gw_v.at[k], gw_out.at[k], gw_sem.at[1, k])

    for k in range(parts):
        fetch(k).start()
    for k in range(2):
        fetch_gw(k).start()
    full = ext_ref[...].reshape(nn, nn + LANES)
    gg_out[...] = full[:, :nn]
    eye = lax.broadcasted_iota(jnp.int32, (nn, nn), 0) == lax.broadcasted_iota(
        jnp.int32, (nn, nn), 1
    )
    gbeta_out[...] = jnp.sum(
        jnp.where(eye, full[:, nn + LANES - 1 : nn + LANES], 0.0), axis=0, keepdims=True
    )
    gb_out[...] = gb_ref[...]
    for k in range(parts):
        fetch(k).wait()
        for i in range(rows):
            gho[pl.ds(k * step * rows + i, step, stride=rows), :] = agr[
                i, k * step : (k + 1) * step, :
            ].astype(F32)
        store(k).start()
        if k >= parts - 2:
            fetch_gw(k - parts + 2).wait()
            store_gw(k - parts + 2).start()
    for k in range(parts):
        store(k).wait()
    for k in range(2):
        store_gw(k).wait()


def local(sizes, target, hidden, weight, bias, gamma, beta):
    n_lat, n_lon, n_lev = sizes
    nn, rows, cols = hidden.shape
    chans = weight.shape[1]
    taps = weight.shape[0]
    n_chip = n_lat // 2 * n_lon
    half = taps // 2 * chans // n_chip
    share = nn // 2 // n_chip
    cells = rows * cols
    rpad = rows + 2
    total_rows = rows * n_lat
    total_cells = total_rows * cols * n_lon
    far = n_lev // 2
    at = np.arange(total_rows).reshape(n_lat, 1, rows) * 2.0 + np.arange(2).reshape(1, 2, 1)
    area = np.cos(math.pi * ((at + 0.5) / (2.0 * total_rows) - 0.5)).astype(np.float32)
    dims = (nn, rows, chans, n_lat, n_lon, n_lev, 4, total_cells)
    wide = nn + LANES
    V = pltpu.VMEM
    D = pltpu.SemaphoreType.DMA
    scratch = [
        V((nn, rows, cols), BF16), V((4, chans, rows, cols), BF16), V((taps, chans, nn), BF16),
        V((nn, nn), F32),
        V((nn * rows, cols), F32), V((4 * chans * rows, cols), F32), V((nn, rpad * cols), F32),
        V((nn, cells), F32), V((nn, cells), F32), V((nn, cells), BF16), V((nn, cells), BF16),
        V((nn, 3 * nn), BF16), V((nn, 3 * nn), BF16), V((nn, taps * chans), BF16),
        V((3 * nn, rpad * cols), BF16), V((2, 4 * chans, rpad * cols), BF16),
        V((cells, cols), BF16), V((nn, cols), BF16), V((6, nn, cols), BF16),
        V((2, 2 * chans, cols), BF16), V((2, 2 * chans, cols), BF16),
        V((2, 2 * chans, cols), BF16),
        V((2, n_chip, half, nn), F32), V((n_chip, half, nn), F32), V((n_chip, half, nn), BF16),
        V((n_chip, half, nn), BF16), V((half, nn), F32),
        V((rows, nn, cols), F32), V((cols, cols), F32), V((nn, cells), BF16), V((nn, cells), BF16),
        V((nn, wide), F32), V((nn // 2, wide), F32), V((n_chip, share, wide), F32),
        V((n_chip, share, wide), F32), V((n_lev, share, wide), F32),
        V((share, wide), F32),
        V((2, far + 1, 2, nn, cols), F32), V((2, far + 1, 2, nn, cols), F32),
        V((2, nn, cols), BF16),
        D((4,)), D((3,)),
        D((2,)), D((2,)), D((6,)), D((6,)), D((2,)), D((2,)), D((6,)), D((6,)),
        D, D, D((n_chip,)), D((n_chip,)), D((n_chip,)), D((n_chip,)), D, D,
        D, D, D((n_chip,)), D((n_chip,)), D((n_lev,)), D((n_lev,)), D((n_chip,)), D((n_chip,)),
        D, D,
        D((2, far + 1, 2)), D((2, far + 1, 2)), D((2, far + 1)), D((2, far + 1)),
    ]
    hbm = pl.BlockSpec(memory_space=pl.ANY)
    vmem = pl.BlockSpec(memory_space=pltpu.VMEM)
    smem = pl.BlockSpec(memory_space=pltpu.SMEM)
    agr, wg, ext, gb = pl.pallas_call(
        functools.partial(kernel, dims),
        out_shape=(
            jax.ShapeDtypeStruct((rows, nn, cols), BF16),
            jax.ShapeDtypeStruct((2, n_chip, half, nn), F32),
            jax.ShapeDtypeStruct((2, n_chip, share, wide), F32),
            jax.ShapeDtypeStruct((1, chans), F32),
        ),
        in_specs=[smem, hbm, hbm, hbm, vmem, hbm, vmem],
        out_specs=(hbm, hbm, hbm, vmem),
        scratch_shapes=scratch,
        compiler_params=pltpu.CompilerParams(
            collective_id=0, has_side_effects=True, vmem_limit_bytes=60 * 2**20
        ),
    )(
        jnp.asarray(area.reshape(-1)), hidden, target, weight, bias.reshape(1, chans),
        gamma, beta.reshape(1, nn),
    )
    parts = 4
    gh, gw, gg, gbeta, gb = pl.pallas_call(
        functools.partial(finish, (nn, rows, parts)),
        out_shape=(
            jax.ShapeDtypeStruct((nn * rows, cols), F32),
            jax.ShapeDtypeStruct((2, n_chip, half, nn), F32),
            jax.ShapeDtypeStruct((nn, nn), F32),
            jax.ShapeDtypeStruct((1, nn), F32),
            jax.ShapeDtypeStruct((1, chans), F32),
        ),
        in_specs=[hbm, hbm, vmem, vmem],
        out_specs=(hbm, hbm, vmem, vmem, vmem),
        scratch_shapes=[
            V((rows, nn, cols), BF16), V((nn * rows, cols), F32), V((2, n_chip, half, nn), F32),
            D((parts,)), D((parts,)), D((2, 2)),
        ],
        compiler_params=pltpu.CompilerParams(vmem_limit_bytes=60 * 2**20),
    )(agr, wg, ext, gb)
    return (
        gh.reshape(nn, rows, cols), gw.reshape(taps, chans, nn), gb.reshape(chans), gg,
        gbeta.reshape(nn),
    )


def solution(mesh):
    sizes = tuple(mesh.shape[a] for a in ("lat", "lon", "lev"))
    return jax.shard_map(
        functools.partial(local, sizes),
        mesh=mesh,
        in_specs=(
            P(None, "lev", "lat", "lon"),
            P(None, "lat", "lon"),
            P(None, "lev", None),
            P("lev"),
            P(),
            P(),
        ),
        out_specs=(P(None, "lat", "lon"), P(None, "lev", None), P("lev"), P(), P()),
        check_vma=False,
    )
```

```python
import functools
import math

import jax
import jax.numpy as jnp
import numpy as np
from jax import lax
from jax.experimental import pallas as pl
from jax.experimental.pallas import tpu as pltpu
from jax.sharding import PartitionSpec as P

F32 = jnp.float32
BF16 = jnp.bfloat16
MESH = pl.DeviceIdType.MESH
LANES = 128


def split(x):
    hi = x.astype(BF16)
    return hi, (x - hi.astype(F32)).astype(BF16)


def dot(a, b):
    return jnp.dot(a, b, preferred_element_type=F32)


def dot_nt(a, b):
    return lax.dot_general(a, b, (((1,), (1,)), ((), ())), preferred_element_type=F32)


def wrap(index, size):
    return lax.rem(index + size, size)


def kernel(
    dims,
    area_ref, hidden_ref, target_ref, weight_ref, bias_ref, gamma_ref, beta_ref,
    gh_out, gw_out, ext_out, gb_out,
    hid_v, tgt_v, w_v, gamma_v,
    hf, tf, hx, root_s, hr_s, sqh, sql, g3, gt3, wt,
    us, gs, sel, hh_send, hh_recv, eu_send, eu_recv, eg_send, eg_recv, eg_corner,
    dw, dwp, rsb, rsr, wown,
    gu, bacc, mh, ml, ext, extp, exts, extr, extz, eown,
    abuf, arecv, agr,
    in_sem, out_sem, put_sem,
    row_ss, row_rs, eu_ss, eu_rs, grow_ss, grow_rs, eg_ss, eg_rs,
    pw_ss, pw_rs, rb_ss, rb_rs, ab_ss, ab_rs, pg_ss, pg_rs,
    pe_ss, pe_rs, rc_ss, rc_rs, z_ss, z_rs, ac_ss, ac_rs, pc_ss, pc_rs,
    a_ss, a_rs, g_ss, g_rs,
):
    nn, rows, chans, n_lat, n_lon, n_lev, n_y, total_cells = dims
    cells = rows * LANES
    rpad = rows + 2
    lat, lon, lev = lax.axis_index("lat"), lax.axis_index("lon"), lax.axis_index("lev")
    core = lax.rem(lat, 2)
    n_chip = (n_lat // 2) * n_lon
    n_xlo = n_lon // n_y
    chip = lax.div(lat, 2) * n_lon + lon
    half = 16 // 2 * chans // n_chip
    share = nn // 2 // n_chip

    def at_chip(k):
        return (lax.div(k, n_lon) * 2 + core, lax.rem(k, n_lon), lev)

    pair = (lat + 1 - 2 * core, lon, lev)
    north = (wrap(lat - 1, n_lat), lon, lev)
    south = (wrap(lat + 1, n_lat), lon, lev)
    west = (lat, wrap(lon - 1, n_lon), lev)
    east = (lat, wrap(lon + 1, n_lon), lev)
    below = (lat, lon, wrap(lev - 1, n_lev))
    above = (lat, lon, wrap(lev + 1, n_lev))

    def remote(src, dst, ss, rs, device):
        return pltpu.make_async_remote_copy(
            src_ref=src, dst_ref=dst, send_sem=ss, recv_sem=rs,
            device_id=device, device_id_type=MESH,
        )

    def lanes(r, count=1):
        if isinstance(r, int):
            return pl.ds(r * LANES, count * LANES)
        return pl.ds(pl.multiple_of(r * LANES, LANES), count * LANES)

    inputs = [
        pltpu.make_async_copy(s, d, in_sem.at[i])
        for i, (s, d) in enumerate(
            ((hidden_ref, hid_v), (gamma_ref, gamma_v), (target_ref, tgt_v), (weight_ref, w_v))
        )
    ]
    for c in inputs:
        c.start()

    barrier = pltpu.get_barrier_semaphore()

    def greet(device):
        pl.semaphore_signal(barrier, inc=1, device_id=device, device_id_type=MESH)

    corners = [
        (wrap(lat + i, n_lat), wrap(lon + j, n_lon), lev) for i in (-1, 1) for j in (-1, 1)
    ]
    northwest, northeast, southwest, southeast = corners
    for device in [north, south] + corners:
        greet(device)

    def greet_chip(j, c):
        greet(at_chip(wrap(chip + j, n_chip)))
        return c

    lax.fori_loop(1, n_chip, greet_chip, 0)

    def greet_lev(j, c):
        greet((lat, lon, wrap(lev + j, n_lev)))
        return c

    lax.fori_loop(1, n_lev, greet_lev, 0)

    inputs[0].wait()
    hf[...] = hid_v[...].astype(F32).reshape(nn * rows, LANES)

    mid = slice(nn, 2 * nn)

    def spread(i, c):
        x = hf[pl.ds(i, nn, stride=rows), :]
        hx[:, lanes(i + 1)] = x
        us[mid, lanes(i + 1)] = x.astype(BF16)
        return c

    lax.fori_loop(0, rows, spread, 0, unroll=2)
    hh_send[0] = us[mid, lanes(1)]
    hh_send[1] = us[mid, lanes(rows)]

    def make_sel(r, c):
        e = lax.broadcasted_iota(jnp.int32, (64, LANES), 0)
        k = lax.broadcasted_iota(jnp.int32, (64, LANES), 1)
        last, first = k == LANES - 1, k == 0
        hit = (last & (e == r)) | (first & (e == 32 + r))
        hit = hit | ((r == rows) & ((last & (e == 0)) | (first & (e == 32))))
        hit = hit | ((r == 1) & ((last & (e == rows + 1)) | (first & (e == 33 + rows))))
        sel[:, lanes(r - 1)] = jnp.where(hit, 1.0, 0.0).astype(BF16)
        return c

    lax.fori_loop(1, rows + 1, make_sel, 0)
    columns = dot_nt(sel[...], us[mid, lanes(1, rows)]).astype(BF16)
    eu_send[0] = columns[:32]
    eu_send[1] = columns[32:]

    inputs[1].wait()
    gamma = gamma_v[...]
    g_hi, g_lo = split(gamma)
    g3[...] = jnp.concatenate([g_hi, g_lo, g_hi], axis=1)
    g_hi, g_lo = split(gamma.T)
    gt3[...] = jnp.concatenate([g_hi, g_lo, g_hi], axis=1)
    eye = lax.broadcasted_iota(jnp.int32, (nn, nn), 0) == lax.broadcasted_iota(
        jnp.int32, (nn, nn), 1
    )
    beta_col = jnp.sum(jnp.where(eye, beta_ref[...], 0.0), axis=1, keepdims=True)
    eye_c = lax.broadcasted_iota(jnp.int32, (chans, chans), 0) == lax.broadcasted_iota(
        jnp.int32, (chans, chans), 1
    )
    bias_col = jnp.sum(jnp.where(eye_c, bias_ref[...], 0.0), axis=1, keepdims=True)

    pl.semaphore_wait(barrier, 6 + (n_chip - 1) + (n_lev - 1))

    sends = []

    def go(copy):
        copy.start()
        sends.append(copy)
        return copy

    eu_copies = [
        go(remote(eu_send.at[i % 2], eu_recv.at[i], eu_ss.at[i], eu_rs.at[i], device))
        for i, device in enumerate((east, west, southeast, southwest, northeast, northwest))
    ] + [
        go(remote(hh_send.at[0], hh_recv.at[1], row_ss.at[0], row_rs.at[0], north)),
        go(remote(hh_send.at[1], hh_recv.at[0], row_ss.at[1], row_rs.at[1], south)),
    ]

    def root_of(x):
        s_hi, s_lo = split(x * x)
        total = dot(g3[...], jnp.concatenate([s_hi, s_hi, s_lo], axis=0))
        return jnp.sqrt(beta_col + total), s_hi, s_lo

    def root_tile(t, c):
        at = lanes(2 * t, 2)
        x = hx[:, lanes(2 * t + 1, 2)]
        root, s_hi, s_lo = root_of(x)
        root_s[:, at] = root
        hr_s[:, at] = x * (0.5 / root)
        sqh[:, at] = s_hi
        sql[:, at] = s_lo
        us[nn : 2 * nn, lanes(2 * t + 1, 2)] = (x * root).astype(BF16)
        return c

    lax.fori_loop(0, rows // 2, root_tile, 0, unroll=2)

    north_in = jnp.where(lat > 0, 1.0, 0.0).astype(F32)
    south_in = jnp.where(lat < n_lat - 1, 1.0, 0.0).astype(F32)

    inputs[3].wait()
    order = []
    for p in range(2):
        for a in range(2):
            for v in range(2):
                for q in range(2):
                    b = v if q else 1 - v
                    order.append(4 * (2 * p + q) + 2 * a + b)
    for g in range(4):
        block = jnp.concatenate([w_v[t] for t in order[4 * g : 4 * g + 4]], axis=0)
        wt[:, 4 * chans * g : 4 * chans * (g + 1)] = block.T

    inputs[2].wait()

    def widen(k, c):
        span = chans * rows
        tf[pl.ds(pl.multiple_of(k * span, span), span), :] = (
            tgt_v[k].astype(F32).reshape(span, LANES)
        )
        return c

    lax.fori_loop(0, 4, widen, 0)
    bacc[...] = jnp.zeros_like(bacc)
    gs[0, : 2 * chans, lanes(0)] = jnp.zeros((2 * chans, LANES), BF16)
    gs[1, : 2 * chans, lanes(rpad - 1)] = jnp.zeros((2 * chans, LANES), BF16)

    for c in eu_copies:
        c.wait_recv()
    row = lax.broadcasted_iota(jnp.int32, (32, nn), 0)

    def side(i):
        x = eu_recv[i].astype(F32)
        x = jnp.where(row == 0, eu_recv[i + 2].astype(F32) * north_in, x)
        return jnp.where(row == rows + 1, eu_recv[i + 4].astype(F32) * south_in, x)

    columns = jnp.concatenate([side(0), side(1), jnp.zeros((64, nn), F32)], axis=0).T
    x = jnp.concatenate(
        [hh_recv[0].astype(F32) * north_in, hh_recv[1].astype(F32) * south_in, columns], axis=1
    )
    root, _, _ = root_of(x)
    edge = (x * root).astype(BF16)
    us[mid, lanes(0)] = edge[:, :LANES]
    us[mid, lanes(rpad - 1)] = edge[:, LANES : 2 * LANES]
    eu_mix = edge[:, 2 * LANES :].astype(F32)

    def from_west(x, e, r):
        at = lax.broadcasted_iota(jnp.int32, x.shape, 1)
        return jnp.where(at == 0, pltpu.roll(e, LANES - r, 1), pltpu.roll(x, 1, 1))

    def from_east(x, e, r):
        at = lax.broadcasted_iota(jnp.int32, x.shape, 1)
        edge = pltpu.roll(e, LANES - 1 - r, 1)
        return jnp.where(at == LANES - 1, edge, pltpu.roll(x, LANES - 1, 1))

    def shift_u(r, c):
        x = us[mid, lanes(r)].astype(F32)
        us[:nn, lanes(r)] = from_west(x, eu_mix, r).astype(BF16)
        us[2 * nn :, lanes(r)] = from_east(x, eu_mix, 32 + r).astype(BF16)
        return c

    lax.fori_loop(0, rpad, shift_u, 0, unroll=3)

    def recon_tile(it, c):
        t = lax.rem(it + rows // 2 - 1, rows // 2)
        for p in range(2):
            area = [area_ref[lat * 2 * rows + p * rows + 2 * t + i] for i in range(2)]
            for q in range(2):
                phase = 2 * p + q
                moved = jnp.concatenate(
                    [us[q * nn : (q + 2) * nn, lanes(2 * t + p + a, 2)] for a in range(2)], axis=0
                )
                w = jnp.concatenate([w_v[4 * phase + k] for k in range(4)], axis=1)
                recon = dot(w, moved) + bias_col
                total = jnp.zeros((chans, LANES), F32)
                for i in range(2):
                    want = tf[pl.ds(phase * chans * rows + 2 * t + i, chans, stride=rows), :]
                    diff = (recon[:, i * LANES : (i + 1) * LANES] - want) * area[i]
                    total = total + diff
                    gs[p, q * chans : (q + 1) * chans, lanes(2 * t + i + 1)] = diff.astype(BF16)
                bacc[:chans, :] += total
        return c

    lax.fori_loop(0, 2, recon_tile, 0, unroll=2)
    grow_copies = [
        go(remote(gs.at[0, 0 : 2 * chans, lanes(1)], gs.at[0, 0 : 2 * chans, lanes(rpad - 1)],
                  grow_ss.at[0], grow_rs.at[0], north)),
        go(remote(gs.at[1, 0 : 2 * chans, lanes(rows)], gs.at[1, 0 : 2 * chans, lanes(0)],
                  grow_ss.at[1], grow_rs.at[1], south)),
    ]
    lax.fori_loop(2, rows // 2, recon_tile, 0, unroll=2)
    pad = LANES - chans
    for p in range(2):
        for q in range(2):
            block = gs[p, q * (chans - pad) : q * (chans - pad) + LANES, lanes(1, rows)]
            eg_send[q, p] = dot_nt(sel[32 * (1 - q) : 32 * (2 - q), :], block).astype(BF16)
    eg_copies = [
        go(remote(src, dst, eg_ss.at[i], eg_rs.at[i], device))
        for i, (src, dst, device) in enumerate((
            (eg_send.at[0], eg_recv.at[0], west),
            (eg_send.at[1], eg_recv.at[1], east),
            (eg_send.at[0, 0], eg_corner.at[0, 0], northwest),
            (eg_send.at[1, 0], eg_corner.at[1, 0], northeast),
            (eg_send.at[0, 1], eg_corner.at[0, 1], southwest),
            (eg_send.at[1, 1], eg_corner.at[1, 1], southeast),
        ))
    ]

    per_tap = chans // half

    def grad_taps(slot, p, q):
        for a in range(2):
            y = dot_nt(
                gs[p, q * chans : (q + 1) * chans, lanes(1, rows)],
                us[q * nn : (q + 2) * nn, lanes(p + a, rows)],
            )
            for b in range(2):
                for k in range(per_tap):
                    dw[slot, (4 * q + 2 * a + b) * per_tap + k] = y[
                        k * half : (k + 1) * half, b * nn : (b + 1) * nn
                    ]

    grad_taps(0, 1 - core, 0)
    grad_taps(0, 1 - core, 1)
    pw = go(remote(dw.at[0], dwp, pw_ss, pw_rs, pair))

    for c in grow_copies + eg_copies:
        c.wait_recv()
    gs[0, : 2 * chans, lanes(rpad - 1)] = (
        gs[0, : 2 * chans, lanes(rpad - 1)].astype(F32) * south_in
    ).astype(BF16)
    gs[1, : 2 * chans, lanes(0)] = (
        gs[1, : 2 * chans, lanes(0)].astype(F32) * north_in
    ).astype(BF16)
    row = lax.broadcasted_iota(jnp.int32, (32, LANES), 0)
    eg_mix = {}
    for p, at, keep in ((0, rows + 1, south_in), (1, 0, north_in)):
        for q in range(2):
            x = jnp.where(
                row == at, eg_corner[q, p].astype(F32) * keep, eg_recv[q, p].astype(F32)
            )
            x = jnp.concatenate([x, jnp.zeros((LANES - 32, LANES), F32)], axis=0).T
            eg_mix[p, q] = x[q * pad : q * pad + chans]

    def shift_g(r, c):
        for p in range(2):
            rr = r + 1 - p
            x = gs[p, : 2 * chans, lanes(rr)].astype(F32)
            gs[p, 2 * chans : 3 * chans, lanes(rr)] = from_east(
                x[:chans], eg_mix[p, 0], rr
            ).astype(BF16)
            gs[p, 3 * chans :, lanes(rr)] = from_west(
                x[chans:], eg_mix[p, 1], rr
            ).astype(BF16)
        return c

    lax.fori_loop(0, rows + 1, shift_g, 0)

    def grad_rows(*chunks):
        moved = jnp.concatenate(
            [
                jnp.concatenate([gs[p, :, lanes(2 * k + 2 - p - a, 2)] for k in chunks], axis=1)
                for p in range(2)
                for a in range(2)
            ],
            axis=0,
        )
        y = dot(wt[...], moved)
        for i, k in enumerate(chunks):
            gu[2 * k] = y[:, 2 * i * LANES : (2 * i + 1) * LANES]
            gu[2 * k + 1] = y[:, (2 * i + 1) * LANES : (2 * i + 2) * LANES]

    far = n_lev // 2
    cuts = 2
    piece = nn // cuts
    rs_copies = {}

    def rs_send(way, s, h, first):
        owner = wrap(lev + (far + 1 - s if way else s - far - 1), n_lev)
        for k in range(cuts):
            at = pl.ds(k * piece, piece)
            src = gu.at[2 * owner + h, at]
            if not first:
                rs_copies[way, s - 1, h, k].wait_recv()
                abuf[way, s, h, at] = gu[2 * owner + h, at] + arecv[way, s - 1, h, at]
                src = abuf.at[way, s, h, at]
            rs_copies[way, s, h, k] = go(
                remote(src, arecv.at[way, s, h, at], a_ss.at[way, s, h, k],
                       a_rs.at[way, s, h, k], above if way else below)
            )

    def over_chips(make):
        def start(j, c):
            make(j).start()
            return c

        def arrive(j, c):
            make(j).wait_recv()
            return c

        def sent(j, c):
            make(j).wait_send()
            return c

        lax.fori_loop(1, n_chip, start, 0)
        return (
            lambda: lax.fori_loop(1, n_chip, arrive, 0),
            lambda: lax.fori_loop(1, n_chip, sent, 0),
        )

    grad_rows(wrap(lev + far, n_lev))
    rs_send(0, 1, 0, True)
    rs_send(1, 1, 1, True)
    grad_rows(wrap(lev + far - 1, n_lev), wrap(lev + far + 1, n_lev))
    rs_send(1, 2, 0, True)
    rs_send(0, 2, 1, True)
    grad_rows(wrap(lev + far - 2, n_lev), wrap(lev + far + 2, n_lev))
    grad_rows(wrap(lev + 1, n_lev), wrap(lev + n_lev - 1, n_lev))
    grad_rows(lev)

    def mix_tile(t, acc):
        at = lanes(2 * t, 2)
        g = jnp.concatenate([gu[2 * t], gu[2 * t + 1]], axis=1)
        mixing = g * hr_s[:, at]
        m_hi, m_lo = split(mixing)
        mh[:, at] = m_hi
        ml[:, at] = m_lo
        return acc + mixing[:, :LANES] + mixing[:, LANES:]

    msum = lax.fori_loop(0, rows // 2, mix_tile, jnp.zeros((nn, LANES), F32))
    beta_part = jnp.sum(msum, axis=1, keepdims=True)
    bias_part = jnp.sum(bacc[...].T, axis=0, keepdims=True)
    ext[:, :nn] = dot_nt(mh[...], sqh[...]) + (
        dot_nt(ml[...], sqh[...]) + dot_nt(mh[...], sql[...])
    )
    lane = lax.broadcasted_iota(jnp.int32, (nn, LANES), 1)
    ext[:, nn:] = jnp.where(lane == LANES - 1, beta_part, bias_part)
    mine = pl.multiple_of(core * (nn // 2), nn // 2)
    others = pl.multiple_of((1 - core) * (nn // 2), nn // 2)
    pe = go(remote(ext.at[pl.ds(others, nn // 2)], extp, pe_ss, pe_rs, pair))

    rs_send(0, 2, 0, False)
    rs_send(1, 2, 1, False)

    pe.wait_recv()

    def join_ext(k, c):
        at = pl.ds(pl.multiple_of(mine + k * share, share), share)
        exts[k] = ext[at, :] + extp[pl.ds(pl.multiple_of(k * share, share), share), :]
        return c

    lax.fori_loop(0, n_chip, join_ext, 0)
    extr[chip] = exts[chip]

    def rc_make(j):
        k = wrap(chip + j, n_chip)
        return remote(exts.at[k], extr.at[chip], rc_ss.at[j], rc_rs.at[j], at_chip(k))

    rc_arrive, rc_sent = over_chips(rc_make)
    grad_taps(1, core, 0)
    rs_send(1, 3, 0, False)
    rs_send(0, 3, 1, False)
    grad_taps(1, core, 1)
    pw.wait_recv()

    def join(k, c):
        dw[1, k] = dw[1, k] + dwp[k]
        rsb[k] = dw[1, k].astype(BF16)
        return c

    lax.fori_loop(0, n_chip, join, 0)

    def rb_make(j):
        k = wrap(chip + j, n_chip)
        return remote(rsb.at[k], rsr.at[j], rb_ss.at[j], rb_rs.at[j], at_chip(k))

    rb_arrive, rb_sent = over_chips(rb_make)
    rs_send(0, 3, 0, False)
    rs_send(1, 3, 1, False)

    rc_arrive()

    def add_ext(k, acc):
        return acc + extr[k]

    plane = lax.fori_loop(1, n_chip, add_ext, extr[0])
    gb_out[...] = plane[0:1, nn : nn + chans] * (1.0 / total_cells)
    extz[lev] = plane

    def z_make(j):
        return remote(
            extz.at[lev], extz.at[lev], z_ss.at[j], z_rs.at[j], (lat, lon, wrap(lev + j, n_lev))
        )

    for j in range(1, n_lev):
        z_make(j).start()

    rs_send(1, 4, 0, False)
    rs_send(0, 4, 1, False)

    rb_arrive()

    def add_taps(j, acc):
        return acc + rsr[j].astype(F32)

    wown[...] = lax.fori_loop(1, n_chip, add_taps, dw[1, chip]) * (1.0 / total_cells)
    w_copy = pltpu.make_async_copy(wown, gw_out.at[core, chip], out_sem.at[0])
    w_copy.start()

    def ab_make(j):
        k = wrap(chip + j, n_chip)
        return remote(wown, gw_out.at[core, chip], ab_ss.at[j], ab_rs.at[j], at_chip(k))

    ab_arrive, ab_sent = over_chips(ab_make)
    rs_send(0, 4, 0, False)
    rs_send(1, 4, 1, False)

    for j in range(1, n_lev):
        z_make(j).wait_recv()
    whole = extz[0]
    for k in range(1, n_lev):
        whole = whole + extz[k]
    eown[...] = whole * (1.0 / total_cells)
    e_copy = pltpu.make_async_copy(eown, ext_out.at[core, chip], out_sem.at[1])
    e_copy.start()

    def ac_make(j):
        k = wrap(chip + j, n_chip)
        return remote(eown, ext_out.at[core, chip], ac_ss.at[j], ac_rs.at[j], at_chip(k))

    ac_arrive, ac_sent = over_chips(ac_make)

    for way, h in ((1, 0), (0, 1), (0, 0), (1, 1)):
        for k in range(cuts):
            rs_copies[way, far, h, k].wait_recv()
    g = jnp.concatenate(
        [gu[2 * lev + h] + (arecv[0, far, h] + arecv[1, far, h]) for h in range(2)], axis=1
    )
    at = lanes(2 * lev, 2)
    m_hi, m_lo = split(g * hr_s[:, at])
    back = dot(gt3[...], jnp.concatenate([m_hi, m_hi, m_lo], axis=0))
    gh = (g * root_s[:, at] + 2.0 * hx[:, lanes(2 * lev + 1, 2)] * back).astype(BF16)
    agr[2 * lev] = gh[:, :LANES]
    agr[2 * lev + 1] = gh[:, LANES:]

    ag_copies = {}

    def ag_send(s):
        for h in range(2):
            for way in range(2):
                if s == far and h != way:
                    continue
                owner = wrap(lev + (1 - s if way else s - 1), n_lev)
                for k in range(cuts):
                    if s > 1:
                        ag_copies[way, s - 1, h, k].wait_recv()
                    block = agr.at[2 * owner + h, pl.ds(k * piece, piece)]
                    ag_copies[way, s, h, k] = go(
                        remote(block, block, g_ss.at[way, s, h, k], g_rs.at[way, s, h, k],
                               above if way else below)
                    )

    put_copies = []

    def put(i, owner):
        block = pl.ds(2 * owner, 2)
        copy = pltpu.make_async_copy(agr.at[block], gh_out.at[block], put_sem.at[i])
        copy.start()
        put_copies.append(copy)

    ag_send(1)
    put(0, lev)
    ac_arrive()
    e_copy.wait()
    pc = go(remote(ext_out.at[core], ext_out.at[core], pc_ss, pc_rs, pair))
    ag_send(2)
    put(1, wrap(lev + 1, n_lev))
    put(2, wrap(lev - 1, n_lev))
    ab_arrive()
    w_copy.wait()
    pg = go(remote(gw_out.at[core], gw_out.at[core], pg_ss, pg_rs, pair))
    ag_send(3)
    put(3, wrap(lev + 2, n_lev))
    put(4, wrap(lev - 2, n_lev))
    ag_send(4)
    for way in range(2):
        for k in range(cuts):
            ag_copies[way, far - 1, 1 - way, k].wait_recv()
    put(5, wrap(lev + 3, n_lev))
    put(6, wrap(lev - 3, n_lev))
    pc.wait_recv()
    pg.wait_recv()
    for way in range(2):
        for k in range(cuts):
            ag_copies[way, far, way, k].wait_recv()
    put(7, wrap(lev + far, n_lev))

    for c in sends:
        c.wait_send()
    rb_sent()
    ab_sent()
    rc_sent()
    ac_sent()
    for j in range(1, n_lev):
        z_make(j).wait_send()
    for c in put_copies:
        c.wait()


def finish(
    dims, agr_ref, wg_ref, ext_ref, gb_ref,
    gh_out, gw_out, gg_out, gbeta_out, gb_out,
    agr, gho, gw_v, ext_v, gg_v, in_sem, out_sem, gw_sem, ext_sem,
):
    nn, rows, parts = dims
    step = nn // parts

    def fetch(k):
        at = pl.ds(k * step, step)
        return pltpu.make_async_copy(agr_ref.at[:, at], agr.at[:, at], in_sem.at[k])

    def store(k):
        at = pl.ds(k * step * rows, step * rows)
        return pltpu.make_async_copy(gho.at[at], gh_out.at[at], out_sem.at[k])

    def fetch_gw(k):
        return pltpu.make_async_copy(wg_ref.at[k], gw_v.at[k], gw_sem.at[0, k])

    def store_gw(k):
        return pltpu.make_async_copy(gw_v.at[k], gw_out.at[k], gw_sem.at[1, k])

    fetch_ext = pltpu.make_async_copy(ext_ref, ext_v, ext_sem.at[0])
    store_gg = pltpu.make_async_copy(gg_v, gg_out, ext_sem.at[1])
    for k in range(parts):
        fetch(k).start()
    fetch_ext.start()
    for k in range(2):
        fetch_gw(k).start()
    gb_out[...] = gb_ref[...]
    eye = lax.broadcasted_iota(jnp.int32, (nn, nn), 0) == lax.broadcasted_iota(
        jnp.int32, (nn, nn), 1
    )
    for k in range(parts):
        fetch(k).wait()
        for i in range(rows):
            gho[pl.ds(k * step * rows + i, step, stride=rows), :] = agr[
                i, k * step : (k + 1) * step, :
            ].astype(F32)
        store(k).start()
    fetch_ext.wait()
    full = ext_v[...].reshape(nn, nn + LANES)
    gg_v[...] = full[:, :nn]
    store_gg.start()
    gbeta_out[...] = jnp.sum(
        jnp.where(eye, full[:, nn + LANES - 1 : nn + LANES], 0.0), axis=0, keepdims=True
    )
    for k in range(2):
        fetch_gw(k).wait()
        store_gw(k).start()
    for k in range(parts):
        store(k).wait()
    store_gg.wait()
    for k in range(2):
        store_gw(k).wait()


def local(sizes, target, hidden, weight, bias, gamma, beta):
    n_lat, n_lon, n_lev = sizes
    nn, rows, cols = hidden.shape
    chans = weight.shape[1]
    taps = weight.shape[0]
    n_chip = n_lat // 2 * n_lon
    half = taps // 2 * chans // n_chip
    share = nn // 2 // n_chip
    cells = rows * cols
    rpad = rows + 2
    total_rows = rows * n_lat
    total_cells = total_rows * cols * n_lon
    far = n_lev // 2
    at = np.arange(total_rows).reshape(n_lat, 1, rows) * 2.0 + np.arange(2).reshape(1, 2, 1)
    area = np.cos(math.pi * ((at + 0.5) / (2.0 * total_rows) - 0.5)).astype(np.float32)
    dims = (nn, rows, chans, n_lat, n_lon, n_lev, 4, total_cells)
    wide = nn + LANES
    V = pltpu.VMEM
    D = pltpu.SemaphoreType.DMA
    scratch = [
        V((nn, rows, cols), BF16), V((4, chans, rows, cols), BF16), V((taps, chans, nn), BF16),
        V((nn, nn), F32),
        V((nn * rows, cols), F32), V((4 * chans * rows, cols), F32), V((nn, rpad * cols), F32),
        V((nn, cells), F32), V((nn, cells), F32), V((nn, cells), BF16), V((nn, cells), BF16),
        V((nn, 3 * nn), BF16), V((nn, 3 * nn), BF16), V((nn, taps * chans), BF16),
        V((3 * nn, rpad * cols), BF16), V((2, 4 * chans, rpad * cols), BF16),
        V((64, cells), BF16), V((2, nn, cols), BF16), V((2, nn, cols), BF16),
        V((2, 32, nn), BF16), V((6, 32, nn), BF16),
        V((2, 2, 32, cols), BF16), V((2, 2, 32, cols), BF16), V((2, 2, 32, cols), BF16),
        V((2, n_chip, half, nn), F32), V((n_chip, half, nn), F32), V((n_chip, half, nn), BF16),
        V((n_chip, half, nn), BF16), V((half, nn), F32),
        V((rows, nn, cols), F32), V((cols, cols), F32), V((nn, cells), BF16), V((nn, cells), BF16),
        V((nn, wide), F32), V((nn // 2, wide), F32), V((n_chip, share, wide), F32),
        V((n_chip, share, wide), F32), V((n_lev, share, wide), F32),
        V((share, wide), F32),
        V((2, far + 1, 2, nn, cols), F32), V((2, far + 1, 2, nn, cols), F32),
        V((rows, nn, cols), BF16),
        D((4,)), D((2,)), D((n_lev,)),
        D((2,)), D((2,)), D((6,)), D((6,)), D((2,)), D((2,)), D((6,)), D((6,)),
        D, D, D((n_chip,)), D((n_chip,)), D((n_chip,)), D((n_chip,)), D, D,
        D, D, D((n_chip,)), D((n_chip,)), D((n_lev,)), D((n_lev,)), D((n_chip,)), D((n_chip,)),
        D, D,
        D((2, far + 1, 2, 2)), D((2, far + 1, 2, 2)),
        D((2, far + 1, 2, 2)), D((2, far + 1, 2, 2)),
    ]
    hbm = pl.BlockSpec(memory_space=pl.ANY)
    vmem = pl.BlockSpec(memory_space=pltpu.VMEM)
    smem = pl.BlockSpec(memory_space=pltpu.SMEM)
    agr, wg, ext, gb = pl.pallas_call(
        functools.partial(kernel, dims),
        out_shape=(
            jax.ShapeDtypeStruct((rows, nn, cols), BF16),
            jax.ShapeDtypeStruct((2, n_chip, half, nn), F32),
            jax.ShapeDtypeStruct((2, n_chip, share, wide), F32),
            jax.ShapeDtypeStruct((1, chans), F32),
        ),
        in_specs=[smem, hbm, hbm, hbm, vmem, hbm, vmem],
        out_specs=(hbm, hbm, hbm, vmem),
        scratch_shapes=scratch,
        compiler_params=pltpu.CompilerParams(
            collective_id=0, has_side_effects=True, vmem_limit_bytes=60 * 2**20
        ),
    )(
        jnp.asarray(area.reshape(-1)), hidden, target, weight, bias.reshape(1, chans),
        gamma, beta.reshape(1, nn),
    )
    parts = 4
    gh, gw, gg, gbeta, gb = pl.pallas_call(
        functools.partial(finish, (nn, rows, parts)),
        out_shape=(
            jax.ShapeDtypeStruct((nn * rows, cols), F32),
            jax.ShapeDtypeStruct((2, n_chip, half, nn), F32),
            jax.ShapeDtypeStruct((nn, nn), F32),
            jax.ShapeDtypeStruct((1, nn), F32),
            jax.ShapeDtypeStruct((1, chans), F32),
        ),
        in_specs=[hbm, hbm, hbm, vmem],
        out_specs=(hbm, hbm, hbm, vmem, vmem),
        scratch_shapes=[
            V((rows, nn, cols), BF16), V((nn * rows, cols), F32), V((2, n_chip, half, nn), F32),
            V((2, n_chip, share, wide), F32), V((nn, nn), F32),
            D((parts,)), D((parts,)), D((2, 2)), D((2,)),
        ],
        compiler_params=pltpu.CompilerParams(vmem_limit_bytes=60 * 2**20),
    )(agr, wg, ext, gb)
    return (
        gh.reshape(nn, rows, cols), gw.reshape(taps, chans, nn), gb.reshape(chans), gg,
        gbeta.reshape(nn),
    )


def solution(mesh):
    sizes = tuple(mesh.shape[a] for a in ("lat", "lon", "lev"))
    return jax.shard_map(
        functools.partial(local, sizes),
        mesh=mesh,
        in_specs=(
            P(None, "lev", "lat", "lon"),
            P(None, "lat", "lon"),
            P(None, "lev", None),
            P("lev"),
            P(),
            P(),
        ),
        out_specs=(P(None, "lat", "lon"), P(None, "lev", None), P("lev"), P(), P()),
        check_vma=False,
    )
```

```python
import functools
import math

import jax
import jax.numpy as jnp
import numpy as np
from jax import lax
from jax.experimental import pallas as pl
from jax.experimental.pallas import tpu as pltpu
from jax.sharding import PartitionSpec as P

F32 = jnp.float32
BF16 = jnp.bfloat16
MESH = pl.DeviceIdType.MESH
LANES = 128


def split(x):
    hi = x.astype(BF16)
    return hi, (x - hi.astype(F32)).astype(BF16)


def dot(a, b):
    return jnp.dot(a, b, preferred_element_type=F32)


def dot_nt(a, b):
    return lax.dot_general(a, b, (((1,), (1,)), ((), ())), preferred_element_type=F32)


STEPS = 1920.0


def pack(x):
    hi = x.astype(BF16)
    h = hi.astype(F32)
    scale = pl.reciprocal(jnp.maximum(jnp.abs(h), 1e-30), approx=True) * STEPS
    q = jnp.clip(jnp.floor((x - h) * scale + 0.5), -8.0, 7.0)
    m = x.shape[0] // 2
    return jnp.concatenate([hi, (16.0 * q[:m] + q[m:]).astype(BF16)], axis=0)


def unpack(y):
    m = y.shape[0] // 3
    h, p = y[: 2 * m].astype(F32), y[2 * m :].astype(F32)
    a = jnp.floor((p + 8.0) * 0.0625)
    q = jnp.concatenate([a, p - 16.0 * a], axis=0)
    return h + jnp.abs(h) * (q * (1.0 / STEPS))


def wrap(index, size):
    return lax.rem(index + size, size)


def kernel(
    dims,
    area_ref, hidden_ref, target_ref, weight_ref, bias_ref, gamma_ref, beta_ref,
    gh_out, gw_out, ext_out, gb_out,
    hid_v, tgt_v, w_v, gamma_v,
    hf, tf, hx, root_s, hr_s, sqh, sql, g3, gt3, wt,
    us, gs, sel, hh_send, hh_recv, eu_send, eu_recv, eg_send, eg_recv, eg_corner,
    dw, dwp, rsb, rsr, wown,
    gu, bacc, mh, ml, ext, extp, exts, extr, extz, eown,
    abuf, arecv, agr,
    in_sem, out_sem, put_sem,
    row_ss, row_rs, eu_ss, eu_rs, grow_ss, grow_rs, eg_ss, eg_rs,
    pw_ss, pw_rs, rb_ss, rb_rs, ab_ss, ab_rs, pg_ss, pg_rs,
    pe_ss, pe_rs, rc_ss, rc_rs, z_ss, z_rs, ac_ss, ac_rs, pc_ss, pc_rs,
    a_ss, a_rs, g_ss, g_rs,
):
    nn, rows, chans, n_lat, n_lon, n_lev, n_y, total_cells = dims
    cells = rows * LANES
    rpad = rows + 2
    lat, lon, lev = lax.axis_index("lat"), lax.axis_index("lon"), lax.axis_index("lev")
    core = lax.rem(lat, 2)
    n_chip = (n_lat // 2) * n_lon
    n_xlo = n_lon // n_y
    chip = lax.div(lat, 2) * n_lon + lon
    half = 16 // 2 * chans // n_chip
    share = nn // 2 // n_chip

    def at_chip(k):
        return (lax.div(k, n_lon) * 2 + core, lax.rem(k, n_lon), lev)

    pair = (lat + 1 - 2 * core, lon, lev)
    north = (wrap(lat - 1, n_lat), lon, lev)
    south = (wrap(lat + 1, n_lat), lon, lev)
    west = (lat, wrap(lon - 1, n_lon), lev)
    east = (lat, wrap(lon + 1, n_lon), lev)
    below = (lat, lon, wrap(lev - 1, n_lev))
    above = (lat, lon, wrap(lev + 1, n_lev))

    def remote(src, dst, ss, rs, device):
        return pltpu.make_async_remote_copy(
            src_ref=src, dst_ref=dst, send_sem=ss, recv_sem=rs,
            device_id=device, device_id_type=MESH,
        )

    def lanes(r, count=1):
        if isinstance(r, int):
            return pl.ds(r * LANES, count * LANES)
        return pl.ds(pl.multiple_of(r * LANES, LANES), count * LANES)

    inputs = [
        pltpu.make_async_copy(s, d, in_sem.at[i])
        for i, (s, d) in enumerate(
            ((hidden_ref, hid_v), (gamma_ref, gamma_v), (target_ref, tgt_v), (weight_ref, w_v))
        )
    ]
    for c in inputs:
        c.start()

    barrier = pltpu.get_barrier_semaphore()

    def greet(device):
        pl.semaphore_signal(barrier, inc=1, device_id=device, device_id_type=MESH)

    corners = [
        (wrap(lat + i, n_lat), wrap(lon + j, n_lon), lev) for i in (-1, 1) for j in (-1, 1)
    ]
    northwest, northeast, southwest, southeast = corners
    for device in [north, south] + corners:
        greet(device)

    def greet_chip(j, c):
        greet(at_chip(wrap(chip + j, n_chip)))
        return c

    lax.fori_loop(1, n_chip, greet_chip, 0)

    def greet_lev(j, c):
        greet((lat, lon, wrap(lev + j, n_lev)))
        return c

    lax.fori_loop(1, n_lev, greet_lev, 0)

    inputs[0].wait()
    hf[...] = hid_v[...].astype(F32).reshape(nn * rows, LANES)

    mid = slice(nn, 2 * nn)

    def spread(i, c):
        x = hf[pl.ds(i, nn, stride=rows), :]
        hx[:, lanes(i + 1)] = x
        us[mid, lanes(i + 1)] = x.astype(BF16)
        return c

    lax.fori_loop(0, rows, spread, 0, unroll=2)
    hh_send[0] = us[mid, lanes(1)]
    hh_send[1] = us[mid, lanes(rows)]

    def make_sel(r, c):
        e = lax.broadcasted_iota(jnp.int32, (64, LANES), 0)
        k = lax.broadcasted_iota(jnp.int32, (64, LANES), 1)
        last, first = k == LANES - 1, k == 0
        hit = (last & (e == r)) | (first & (e == 32 + r))
        hit = hit | ((r == rows) & ((last & (e == 0)) | (first & (e == 32))))
        hit = hit | ((r == 1) & ((last & (e == rows + 1)) | (first & (e == 33 + rows))))
        sel[:, lanes(r - 1)] = jnp.where(hit, 1.0, 0.0).astype(BF16)
        return c

    lax.fori_loop(1, rows + 1, make_sel, 0)
    columns = dot_nt(sel[...], us[mid, lanes(1, rows)]).astype(BF16)
    eu_send[0] = columns[:32]
    eu_send[1] = columns[32:]

    pl.semaphore_wait(barrier, 6 + (n_chip - 1) + (n_lev - 1))

    sends = []

    def go(copy):
        copy.start()
        sends.append(copy)
        return copy

    eu_copies = [
        go(remote(eu_send.at[i % 2], eu_recv.at[i], eu_ss.at[i], eu_rs.at[i], device))
        for i, device in enumerate((east, west, southeast, southwest, northeast, northwest))
    ] + [
        go(remote(hh_send.at[0], hh_recv.at[1], row_ss.at[0], row_rs.at[0], north)),
        go(remote(hh_send.at[1], hh_recv.at[0], row_ss.at[1], row_rs.at[1], south)),
    ]

    inputs[1].wait()
    gamma = gamma_v[...]
    g_hi, g_lo = split(gamma)
    g3[...] = jnp.concatenate([g_hi, g_lo, g_hi], axis=1)
    g_hi, g_lo = split(gamma.T)
    gt3[...] = jnp.concatenate([g_hi, g_lo, g_hi], axis=1)
    eye = lax.broadcasted_iota(jnp.int32, (nn, nn), 0) == lax.broadcasted_iota(
        jnp.int32, (nn, nn), 1
    )
    beta_col = jnp.sum(jnp.where(eye, beta_ref[...], 0.0), axis=1, keepdims=True)
    eye_c = lax.broadcasted_iota(jnp.int32, (chans, chans), 0) == lax.broadcasted_iota(
        jnp.int32, (chans, chans), 1
    )
    bias_col = jnp.sum(jnp.where(eye_c, bias_ref[...], 0.0), axis=1, keepdims=True)

    def root_of(x):
        s_hi, s_lo = split(x * x)
        total = dot(g3[...], jnp.concatenate([s_hi, s_hi, s_lo], axis=0))
        return jnp.sqrt(beta_col + total), s_hi, s_lo

    def root_tile(t, c):
        at = lanes(2 * t, 2)
        x = hx[:, lanes(2 * t + 1, 2)]
        root, s_hi, s_lo = root_of(x)
        root_s[:, at] = root
        hr_s[:, at] = x * (0.5 / root)
        sqh[:, at] = s_hi
        sql[:, at] = s_lo
        us[nn : 2 * nn, lanes(2 * t + 1, 2)] = (x * root).astype(BF16)
        return c

    lax.fori_loop(0, rows // 2, root_tile, 0, unroll=2)

    north_in = jnp.where(lat > 0, 1.0, 0.0).astype(F32)
    south_in = jnp.where(lat < n_lat - 1, 1.0, 0.0).astype(F32)

    inputs[3].wait()
    order = []
    for p in range(2):
        for a in range(2):
            for v in range(2):
                for q in range(2):
                    b = v if q else 1 - v
                    order.append(4 * (2 * p + q) + 2 * a + b)
    for g in range(4):
        block = jnp.concatenate([w_v[t] for t in order[4 * g : 4 * g + 4]], axis=0)
        wt[:, 4 * chans * g : 4 * chans * (g + 1)] = block.T

    inputs[2].wait()

    def widen(k, c):
        span = chans * rows
        tf[pl.ds(pl.multiple_of(k * span, span), span), :] = (
            tgt_v[k].astype(F32).reshape(span, LANES)
        )
        return c

    lax.fori_loop(0, 4, widen, 0)
    bacc[...] = jnp.zeros_like(bacc)
    gs[0, : 2 * chans, lanes(0)] = jnp.zeros((2 * chans, LANES), BF16)
    gs[1, : 2 * chans, lanes(rpad - 1)] = jnp.zeros((2 * chans, LANES), BF16)

    for c in eu_copies:
        c.wait_recv()
    row = lax.broadcasted_iota(jnp.int32, (32, nn), 0)

    def side(i):
        x = eu_recv[i].astype(F32)
        x = jnp.where(row == 0, eu_recv[i + 2].astype(F32) * north_in, x)
        return jnp.where(row == rows + 1, eu_recv[i + 4].astype(F32) * south_in, x)

    columns = jnp.concatenate([side(0), side(1), jnp.zeros((64, nn), F32)], axis=0).T
    x = jnp.concatenate(
        [hh_recv[0].astype(F32) * north_in, hh_recv[1].astype(F32) * south_in, columns], axis=1
    )
    root, _, _ = root_of(x)
    edge = (x * root).astype(BF16)
    us[mid, lanes(0)] = edge[:, :LANES]
    us[mid, lanes(rpad - 1)] = edge[:, LANES : 2 * LANES]
    eu_mix = edge[:, 2 * LANES :].astype(F32)

    def from_west(x, e, r):
        at = lax.broadcasted_iota(jnp.int32, x.shape, 1)
        return jnp.where(at == 0, pltpu.roll(e, LANES - r, 1), pltpu.roll(x, 1, 1))

    def from_east(x, e, r):
        at = lax.broadcasted_iota(jnp.int32, x.shape, 1)
        edge = pltpu.roll(e, LANES - 1 - r, 1)
        return jnp.where(at == LANES - 1, edge, pltpu.roll(x, LANES - 1, 1))

    def shift_u(r, c):
        x = us[mid, lanes(r)].astype(F32)
        us[:nn, lanes(r)] = from_west(x, eu_mix, r).astype(BF16)
        us[2 * nn :, lanes(r)] = from_east(x, eu_mix, 32 + r).astype(BF16)
        return c

    lax.fori_loop(0, rpad, shift_u, 0, unroll=3)

    def recon_tile(it, c):
        t = lax.rem(it + rows // 2 - 1, rows // 2)
        for p in range(2):
            area = [area_ref[lat * 2 * rows + p * rows + 2 * t + i] for i in range(2)]
            for q in range(2):
                phase = 2 * p + q
                moved = jnp.concatenate(
                    [us[q * nn : (q + 2) * nn, lanes(2 * t + p + a, 2)] for a in range(2)], axis=0
                )
                w = jnp.concatenate([w_v[4 * phase + k] for k in range(4)], axis=1)
                recon = dot(w, moved) + bias_col
                total = jnp.zeros((chans, LANES), F32)
                for i in range(2):
                    want = tf[pl.ds(phase * chans * rows + 2 * t + i, chans, stride=rows), :]
                    diff = (recon[:, i * LANES : (i + 1) * LANES] - want) * area[i]
                    total = total + diff
                    gs[p, q * chans : (q + 1) * chans, lanes(2 * t + i + 1)] = diff.astype(BF16)
                bacc[:chans, :] += total
        return c

    lax.fori_loop(0, 2, recon_tile, 0, unroll=2)
    grow_copies = [
        go(remote(gs.at[0, 0 : 2 * chans, lanes(1)], gs.at[0, 0 : 2 * chans, lanes(rpad - 1)],
                  grow_ss.at[0], grow_rs.at[0], north)),
        go(remote(gs.at[1, 0 : 2 * chans, lanes(rows)], gs.at[1, 0 : 2 * chans, lanes(0)],
                  grow_ss.at[1], grow_rs.at[1], south)),
    ]
    lax.fori_loop(2, rows // 2, recon_tile, 0, unroll=2)
    pad = LANES - chans
    for p in range(2):
        for q in range(2):
            block = gs[p, q * (chans - pad) : q * (chans - pad) + LANES, lanes(1, rows)]
            eg_send[q, p] = dot_nt(sel[32 * (1 - q) : 32 * (2 - q), :], block).astype(BF16)
    eg_copies = [
        go(remote(src, dst, eg_ss.at[i], eg_rs.at[i], device))
        for i, (src, dst, device) in enumerate((
            (eg_send.at[0], eg_recv.at[0], west),
            (eg_send.at[1], eg_recv.at[1], east),
            (eg_send.at[0, 0], eg_corner.at[0, 0], northwest),
            (eg_send.at[1, 0], eg_corner.at[1, 0], northeast),
            (eg_send.at[0, 1], eg_corner.at[0, 1], southwest),
            (eg_send.at[1, 1], eg_corner.at[1, 1], southeast),
        ))
    ]

    per_tap = chans // half

    def grad_taps(slot, p, q):
        for a in range(2):
            y = dot_nt(
                gs[p, q * chans : (q + 1) * chans, lanes(1, rows)],
                us[q * nn : (q + 2) * nn, lanes(p + a, rows)],
            )
            for b in range(2):
                for k in range(per_tap):
                    dw[slot, (4 * q + 2 * a + b) * per_tap + k] = y[
                        k * half : (k + 1) * half, b * nn : (b + 1) * nn
                    ]

    grad_taps(0, 1 - core, 0)
    grad_taps(0, 1 - core, 1)
    pw = go(remote(dw.at[0], dwp, pw_ss, pw_rs, pair))
    grad_taps(1, core, 0)

    for c in grow_copies + eg_copies:
        c.wait_recv()
    gs[0, : 2 * chans, lanes(rpad - 1)] = (
        gs[0, : 2 * chans, lanes(rpad - 1)].astype(F32) * south_in
    ).astype(BF16)
    gs[1, : 2 * chans, lanes(0)] = (
        gs[1, : 2 * chans, lanes(0)].astype(F32) * north_in
    ).astype(BF16)
    row = lax.broadcasted_iota(jnp.int32, (32, LANES), 0)
    eg_mix = {}
    for p, at, keep in ((0, rows + 1, south_in), (1, 0, north_in)):
        for q in range(2):
            x = jnp.where(
                row == at, eg_corner[q, p].astype(F32) * keep, eg_recv[q, p].astype(F32)
            )
            x = jnp.concatenate([x, jnp.zeros((LANES - 32, LANES), F32)], axis=0).T
            eg_mix[p, q] = x[q * pad : q * pad + chans]

    def shift_g(r, c):
        for p in range(2):
            rr = r + 1 - p
            x = gs[p, : 2 * chans, lanes(rr)].astype(F32)
            gs[p, 2 * chans : 3 * chans, lanes(rr)] = from_east(
                x[:chans], eg_mix[p, 0], rr
            ).astype(BF16)
            gs[p, 3 * chans :, lanes(rr)] = from_west(
                x[chans:], eg_mix[p, 1], rr
            ).astype(BF16)
        return c

    lax.fori_loop(0, rows + 1, shift_g, 0)

    def grad_rows(*chunks):
        moved = jnp.concatenate(
            [
                jnp.concatenate([gs[p, :, lanes(2 * k + 2 - p - a, 2)] for k in chunks], axis=1)
                for p in range(2)
                for a in range(2)
            ],
            axis=0,
        )
        y = dot(wt[...], moved)
        for i, k in enumerate(chunks):
            gu[2 * k] = y[:, 2 * i * LANES : (2 * i + 1) * LANES]
            gu[2 * k + 1] = y[:, (2 * i + 1) * LANES : (2 * i + 2) * LANES]

    far = n_lev // 2
    cuts = 2
    piece = nn // cuts
    rs_copies = {}

    def rs_send(way, s, h, first):
        owner = wrap(lev + (far + 1 - s if way else s - far - 1), n_lev)
        for k in range(cuts):
            at = pl.ds(k * piece, piece)
            x = gu[2 * owner + h, at]
            if not first:
                rs_copies[way, s - 1, h, k].wait_recv()
                x = x + unpack(arecv[way, s - 1, h, k])
            abuf[way, s, h, k] = pack(x)
            rs_copies[way, s, h, k] = go(
                remote(abuf.at[way, s, h, k], arecv.at[way, s, h, k], a_ss.at[way, s, h, k],
                       a_rs.at[way, s, h, k], above if way else below)
            )

    def over_chips(make):
        def start(j, c):
            make(j).start()
            return c

        def arrive(j, c):
            make(j).wait_recv()
            return c

        def sent(j, c):
            make(j).wait_send()
            return c

        lax.fori_loop(1, n_chip, start, 0)
        return (
            lambda: lax.fori_loop(1, n_chip, arrive, 0),
            lambda: lax.fori_loop(1, n_chip, sent, 0),
        )

    grad_rows(wrap(lev + far, n_lev))
    rs_send(0, 1, 0, True)
    rs_send(1, 1, 1, True)
    grad_rows(wrap(lev + far - 1, n_lev), wrap(lev + far + 1, n_lev))
    rs_send(1, 2, 0, True)
    rs_send(0, 2, 1, True)
    grad_taps(1, core, 1)
    pw.wait_recv()

    def join(k, c):
        dw[1, k] = dw[1, k] + dwp[k]
        rsb[k] = dw[1, k].astype(BF16)
        return c

    lax.fori_loop(0, n_chip, join, 0)

    def rb_make(j):
        k = wrap(chip + j, n_chip)
        return remote(rsb.at[k], rsr.at[j], rb_ss.at[j], rb_rs.at[j], at_chip(k))

    rb_arrive, rb_sent = over_chips(rb_make)
    grad_rows(wrap(lev + far - 2, n_lev), wrap(lev + far + 2, n_lev))
    grad_rows(wrap(lev + 1, n_lev), wrap(lev + n_lev - 1, n_lev))
    grad_rows(lev)

    def mix_tile(t, acc):
        at = lanes(2 * t, 2)
        g = jnp.concatenate([gu[2 * t], gu[2 * t + 1]], axis=1)
        mixing = g * hr_s[:, at]
        m_hi, m_lo = split(mixing)
        mh[:, at] = m_hi
        ml[:, at] = m_lo
        return acc + mixing[:, :LANES] + mixing[:, LANES:]

    msum = lax.fori_loop(0, rows // 2, mix_tile, jnp.zeros((nn, LANES), F32))
    beta_part = jnp.sum(msum, axis=1, keepdims=True)
    bias_part = jnp.sum(bacc[...].T, axis=0, keepdims=True)
    ext[:, :nn] = dot_nt(mh[...], sqh[...]) + (
        dot_nt(ml[...], sqh[...]) + dot_nt(mh[...], sql[...])
    )
    lane = lax.broadcasted_iota(jnp.int32, (nn, LANES), 1)
    ext[:, nn:] = jnp.where(lane == LANES - 1, beta_part, bias_part)
    mine = pl.multiple_of(core * (nn // 2), nn // 2)
    others = pl.multiple_of((1 - core) * (nn // 2), nn // 2)
    pe = go(remote(ext.at[pl.ds(others, nn // 2)], extp, pe_ss, pe_rs, pair))

    rs_send(0, 2, 0, False)
    rs_send(1, 2, 1, False)

    pe.wait_recv()

    def join_ext(k, c):
        at = pl.ds(pl.multiple_of(mine + k * share, share), share)
        exts[k] = ext[at, :] + extp[pl.ds(pl.multiple_of(k * share, share), share), :]
        return c

    lax.fori_loop(0, n_chip, join_ext, 0)
    extr[chip] = exts[chip]

    def rc_make(j):
        k = wrap(chip + j, n_chip)
        return remote(exts.at[k], extr.at[chip], rc_ss.at[j], rc_rs.at[j], at_chip(k))

    rc_arrive, rc_sent = over_chips(rc_make)
    rs_send(1, 3, 0, False)
    rs_send(0, 3, 1, False)
    rs_send(0, 3, 0, False)
    rs_send(1, 3, 1, False)

    rs_send(1, 4, 0, False)
    rs_send(0, 4, 1, False)

    rb_arrive()

    def add_taps(j, acc):
        return acc + rsr[j].astype(F32)

    wown[...] = lax.fori_loop(1, n_chip, add_taps, dw[1, chip]) * (1.0 / total_cells)
    w_copy = pltpu.make_async_copy(wown, gw_out.at[core, chip], out_sem.at[0])
    w_copy.start()

    def ab_make(j):
        k = wrap(chip + j, n_chip)
        return remote(wown, gw_out.at[core, chip], ab_ss.at[j], ab_rs.at[j], at_chip(k))

    ab_arrive, ab_sent = over_chips(ab_make)
    rs_send(0, 4, 0, False)
    rs_send(1, 4, 1, False)

    rc_arrive()

    def add_ext(k, acc):
        return acc + extr[k]

    plane = lax.fori_loop(1, n_chip, add_ext, extr[0])
    gb_out[...] = plane[0:1, nn : nn + chans] * (1.0 / total_cells)
    extz[lev] = plane

    def z_make(j):
        return remote(
            extz.at[lev], extz.at[lev], z_ss.at[j], z_rs.at[j], (lat, lon, wrap(lev + j, n_lev))
        )

    for j in range(1, n_lev):
        z_make(j).start()

    for way, h in ((1, 0), (0, 1), (0, 0), (1, 1)):
        for k in range(cuts):
            rs_copies[way, far, h, k].wait_recv()
    g = jnp.concatenate(
        [
            gu[2 * lev + h]
            + jnp.concatenate(
                [unpack(arecv[0, far, h, k]) + unpack(arecv[1, far, h, k]) for k in range(cuts)],
                axis=0,
            )
            for h in range(2)
        ],
        axis=1,
    )
    at = lanes(2 * lev, 2)
    m_hi, m_lo = split(g * hr_s[:, at])
    back = dot(gt3[...], jnp.concatenate([m_hi, m_hi, m_lo], axis=0))
    gh = (g * root_s[:, at] + 2.0 * hx[:, lanes(2 * lev + 1, 2)] * back).astype(BF16)
    agr[2 * lev] = gh[:, :LANES]
    agr[2 * lev + 1] = gh[:, LANES:]

    ag_copies = {}

    def ag_send(s):
        for h in range(2):
            for way in range(2):
                if s == far and h != way:
                    continue
                owner = wrap(lev + (1 - s if way else s - 1), n_lev)
                for k in range(cuts):
                    if s > 1:
                        ag_copies[way, s - 1, h, k].wait_recv()
                    block = agr.at[2 * owner + h, pl.ds(k * piece, piece)]
                    ag_copies[way, s, h, k] = go(
                        remote(block, block, g_ss.at[way, s, h, k], g_rs.at[way, s, h, k],
                               above if way else below)
                    )

    put_copies = []

    def put(i, owner):
        block = pl.ds(2 * owner, 2)
        copy = pltpu.make_async_copy(agr.at[block], gh_out.at[block], put_sem.at[i])
        copy.start()
        put_copies.append(copy)

    ag_send(1)
    put(0, lev)
    for j in range(1, n_lev):
        z_make(j).wait_recv()
    whole = extz[0]
    for k in range(1, n_lev):
        whole = whole + extz[k]
    eown[...] = whole * (1.0 / total_cells)
    e_copy = pltpu.make_async_copy(eown, ext_out.at[core, chip], out_sem.at[1])
    e_copy.start()

    def ac_make(j):
        k = wrap(chip + j, n_chip)
        return remote(eown, ext_out.at[core, chip], ac_ss.at[j], ac_rs.at[j], at_chip(k))

    ac_arrive, ac_sent = over_chips(ac_make)
    ag_send(2)
    put(1, wrap(lev + 1, n_lev))
    put(2, wrap(lev - 1, n_lev))
    ab_arrive()
    w_copy.wait()
    pg = go(remote(gw_out.at[core], gw_out.at[core], pg_ss, pg_rs, pair))
    ag_send(3)
    put(3, wrap(lev + 2, n_lev))
    put(4, wrap(lev - 2, n_lev))
    ac_arrive()
    e_copy.wait()
    pc = go(remote(ext_out.at[core], ext_out.at[core], pc_ss, pc_rs, pair))
    ag_send(4)
    for way in range(2):
        for k in range(cuts):
            ag_copies[way, far - 1, 1 - way, k].wait_recv()
    put(5, wrap(lev + 3, n_lev))
    put(6, wrap(lev - 3, n_lev))
    pc.wait_recv()
    pg.wait_recv()
    for way in range(2):
        for k in range(cuts):
            ag_copies[way, far, way, k].wait_recv()
    put(7, wrap(lev + far, n_lev))

    for c in sends:
        c.wait_send()
    rb_sent()
    ab_sent()
    rc_sent()
    ac_sent()
    for j in range(1, n_lev):
        z_make(j).wait_send()
    for c in put_copies:
        c.wait()


def finish(
    dims, agr_ref, wg_ref, ext_ref, gb_ref,
    gh_out, gw_out, gg_out, gbeta_out, gb_out,
    agr, gho, gw_v, ext_v, gg_v, in_sem, out_sem, gw_sem, ext_sem,
):
    nn, rows, parts = dims
    step = nn // parts

    def fetch(k):
        at = pl.ds(k * step, step)
        return pltpu.make_async_copy(agr_ref.at[:, at], agr.at[:, at], in_sem.at[k])

    def store(k):
        at = pl.ds(k * step * rows, step * rows)
        return pltpu.make_async_copy(gho.at[at], gh_out.at[at], out_sem.at[k])

    def fetch_gw(k):
        return pltpu.make_async_copy(wg_ref.at[k], gw_v.at[k], gw_sem.at[0, k])

    def store_gw(k):
        return pltpu.make_async_copy(gw_v.at[k], gw_out.at[k], gw_sem.at[1, k])

    fetch_ext = pltpu.make_async_copy(ext_ref, ext_v, ext_sem.at[0])
    store_gg = pltpu.make_async_copy(gg_v, gg_out, ext_sem.at[1])
    for k in range(parts):
        fetch(k).start()
    fetch_ext.start()
    for k in range(2):
        fetch_gw(k).start()
    gb_out[...] = gb_ref[...]
    eye = lax.broadcasted_iota(jnp.int32, (nn, nn), 0) == lax.broadcasted_iota(
        jnp.int32, (nn, nn), 1
    )
    for k in range(parts):
        fetch(k).wait()
        for i in range(rows):
            gho[pl.ds(k * step * rows + i, step, stride=rows), :] = agr[
                i, k * step : (k + 1) * step, :
            ].astype(F32)
        store(k).start()
    fetch_ext.wait()
    full = ext_v[...].reshape(nn, nn + LANES)
    gg_v[...] = full[:, :nn]
    store_gg.start()
    gbeta_out[...] = jnp.sum(
        jnp.where(eye, full[:, nn + LANES - 1 : nn + LANES], 0.0), axis=0, keepdims=True
    )
    for k in range(2):
        fetch_gw(k).wait()
        store_gw(k).start()
    for k in range(parts):
        store(k).wait()
    store_gg.wait()
    for k in range(2):
        store_gw(k).wait()


def local(sizes, target, hidden, weight, bias, gamma, beta):
    n_lat, n_lon, n_lev = sizes
    nn, rows, cols = hidden.shape
    chans = weight.shape[1]
    taps = weight.shape[0]
    n_chip = n_lat // 2 * n_lon
    half = taps // 2 * chans // n_chip
    share = nn // 2 // n_chip
    cells = rows * cols
    rpad = rows + 2
    total_rows = rows * n_lat
    total_cells = total_rows * cols * n_lon
    far = n_lev // 2
    at = np.arange(total_rows).reshape(n_lat, 1, rows) * 2.0 + np.arange(2).reshape(1, 2, 1)
    area = np.cos(math.pi * ((at + 0.5) / (2.0 * total_rows) - 0.5)).astype(np.float32)
    dims = (nn, rows, chans, n_lat, n_lon, n_lev, 4, total_cells)
    wide = nn + LANES
    V = pltpu.VMEM
    D = pltpu.SemaphoreType.DMA
    scratch = [
        V((nn, rows, cols), BF16), V((4, chans, rows, cols), BF16), V((taps, chans, nn), BF16),
        V((nn, nn), F32),
        V((nn * rows, cols), F32), V((4 * chans * rows, cols), F32), V((nn, rpad * cols), F32),
        V((nn, cells), F32), V((nn, cells), F32), V((nn, cells), BF16), V((nn, cells), BF16),
        V((nn, 3 * nn), BF16), V((nn, 3 * nn), BF16), V((nn, taps * chans), BF16),
        V((3 * nn, rpad * cols), BF16), V((2, 4 * chans, rpad * cols), BF16),
        V((64, cells), BF16), V((2, nn, cols), BF16), V((2, nn, cols), BF16),
        V((2, 32, nn), BF16), V((6, 32, nn), BF16),
        V((2, 2, 32, cols), BF16), V((2, 2, 32, cols), BF16), V((2, 2, 32, cols), BF16),
        V((2, n_chip, half, nn), F32), V((n_chip, half, nn), F32), V((n_chip, half, nn), BF16),
        V((n_chip, half, nn), BF16), V((half, nn), F32),
        V((rows, nn, cols), F32), V((cols, cols), F32), V((nn, cells), BF16), V((nn, cells), BF16),
        V((nn, wide), F32), V((nn // 2, wide), F32), V((n_chip, share, wide), F32),
        V((n_chip, share, wide), F32), V((n_lev, share, wide), F32),
        V((share, wide), F32),
        V((2, far + 1, 2, 2, nn // 4 * 3, cols), BF16),
        V((2, far + 1, 2, 2, nn // 4 * 3, cols), BF16),
        V((rows, nn, cols), BF16),
        D((4,)), D((2,)), D((n_lev,)),
        D((2,)), D((2,)), D((6,)), D((6,)), D((2,)), D((2,)), D((6,)), D((6,)),
        D, D, D((n_chip,)), D((n_chip,)), D((n_chip,)), D((n_chip,)), D, D,
        D, D, D((n_chip,)), D((n_chip,)), D((n_lev,)), D((n_lev,)), D((n_chip,)), D((n_chip,)),
        D, D,
        D((2, far + 1, 2, 2)), D((2, far + 1, 2, 2)),
        D((2, far + 1, 2, 2)), D((2, far + 1, 2, 2)),
    ]
    hbm = pl.BlockSpec(memory_space=pl.ANY)
    vmem = pl.BlockSpec(memory_space=pltpu.VMEM)
    smem = pl.BlockSpec(memory_space=pltpu.SMEM)
    agr, wg, ext, gb = pl.pallas_call(
        functools.partial(kernel, dims),
        out_shape=(
            jax.ShapeDtypeStruct((rows, nn, cols), BF16),
            jax.ShapeDtypeStruct((2, n_chip, half, nn), F32),
            jax.ShapeDtypeStruct((2, n_chip, share, wide), F32),
            jax.ShapeDtypeStruct((1, chans), F32),
        ),
        in_specs=[smem, hbm, hbm, hbm, vmem, hbm, vmem],
        out_specs=(hbm, hbm, hbm, vmem),
        scratch_shapes=scratch,
        compiler_params=pltpu.CompilerParams(
            collective_id=0, has_side_effects=True, vmem_limit_bytes=60 * 2**20
        ),
    )(
        jnp.asarray(area.reshape(-1)), hidden, target, weight, bias.reshape(1, chans),
        gamma, beta.reshape(1, nn),
    )
    parts = 4
    gh, gw, gg, gbeta, gb = pl.pallas_call(
        functools.partial(finish, (nn, rows, parts)),
        out_shape=(
            jax.ShapeDtypeStruct((nn * rows, cols), F32),
            jax.ShapeDtypeStruct((2, n_chip, half, nn), F32),
            jax.ShapeDtypeStruct((nn, nn), F32),
            jax.ShapeDtypeStruct((1, nn), F32),
            jax.ShapeDtypeStruct((1, chans), F32),
        ),
        in_specs=[hbm, hbm, hbm, vmem],
        out_specs=(hbm, hbm, hbm, vmem, vmem),
        scratch_shapes=[
            V((rows, nn, cols), BF16), V((nn * rows, cols), F32), V((2, n_chip, half, nn), F32),
            V((2, n_chip, share, wide), F32), V((nn, nn), F32),
            D((parts,)), D((parts,)), D((2, 2)), D((2,)),
        ],
        compiler_params=pltpu.CompilerParams(vmem_limit_bytes=60 * 2**20),
    )(agr, wg, ext, gb)
    return (
        gh.reshape(nn, rows, cols), gw.reshape(taps, chans, nn), gb.reshape(chans), gg,
        gbeta.reshape(nn),
    )


def solution(mesh):
    sizes = tuple(mesh.shape[a] for a in ("lat", "lon", "lev"))
    return jax.shard_map(
        functools.partial(local, sizes),
        mesh=mesh,
        in_specs=(
            P(None, "lev", "lat", "lon"),
            P(None, "lat", "lon"),
            P(None, "lev", None),
            P("lev"),
            P(),
            P(),
        ),
        out_specs=(P(None, "lat", "lon"), P(None, "lev", None), P("lev"), P(), P()),
        check_vma=False,
    )
```

```python
import functools
import math

import jax
import jax.numpy as jnp
import numpy as np
from jax import lax
from jax.experimental import pallas as pl
from jax.experimental.pallas import tpu as pltpu
from jax.sharding import PartitionSpec as P

F32 = jnp.float32
BF16 = jnp.bfloat16
MESH = pl.DeviceIdType.MESH
LANES = 128


def split(x):
    hi = x.astype(BF16)
    return hi, (x - hi.astype(F32)).astype(BF16)


def dot(a, b):
    return jnp.dot(a, b, preferred_element_type=F32)


def dot_nt(a, b):
    return lax.dot_general(a, b, (((1,), (1,)), ((), ())), preferred_element_type=F32)


STEPS = 1920.0


def pack(x):
    hi = x.astype(BF16)
    h = hi.astype(F32)
    scale = pl.reciprocal(jnp.maximum(jnp.abs(h), 1e-30), approx=True) * STEPS
    q = jnp.clip(jnp.floor((x - h) * scale + 0.5), -8.0, 7.0)
    m = x.shape[0] // 2
    return jnp.concatenate([hi, (16.0 * q[:m] + q[m:]).astype(BF16)], axis=0)


def unpack(y):
    m = y.shape[0] // 3
    h, p = y[: 2 * m].astype(F32), y[2 * m :].astype(F32)
    a = jnp.floor((p + 8.0) * 0.0625)
    q = jnp.concatenate([a, p - 16.0 * a], axis=0)
    return h + jnp.abs(h) * (q * (1.0 / STEPS))


def wrap(index, size):
    return lax.rem(index + size, size)


def kernel(
    dims,
    area_ref, hidden_ref, target_ref, weight_ref, bias_ref, gamma_ref, beta_ref,
    gh_out, gw_out, ext_out, gb_out,
    hid_v, tgt_v, w_v, gamma_v,
    hf, tf, hx, root_s, hr_s, sqh, sql, g3, gt3, wt,
    us, gs, sel, hh_send, hh_recv, eu_send, eu_recv, eg_send, eg_recv, eg_corner,
    dw, dwp, rsb, rsr, wown,
    gu, bacc, mh, ml, ext, extp, exts, extr, extz, eown,
    abuf, arecv, agr,
    in_sem, out_sem, put_sem,
    row_ss, row_rs, eu_ss, eu_rs, grow_ss, grow_rs, eg_ss, eg_rs,
    pw_ss, pw_rs, rb_ss, rb_rs, ab_ss, ab_rs, pg_ss, pg_rs,
    pe_ss, pe_rs, rc_ss, rc_rs, z_ss, z_rs, ac_ss, ac_rs, pc_ss, pc_rs,
    a_ss, a_rs, g_ss, g_rs,
):
    nn, rows, chans, n_lat, n_lon, n_lev, n_y, total_cells = dims
    cells = rows * LANES
    rpad = rows + 2
    lat, lon, lev = lax.axis_index("lat"), lax.axis_index("lon"), lax.axis_index("lev")
    core = lax.rem(lat, 2)
    n_chip = (n_lat // 2) * n_lon
    n_xlo = n_lon // n_y
    chip = lax.div(lat, 2) * n_lon + lon
    half = 16 // 2 * chans // n_chip
    share = nn // 2 // n_chip

    def at_chip(k):
        return (lax.div(k, n_lon) * 2 + core, lax.rem(k, n_lon), lev)

    pair = (lat + 1 - 2 * core, lon, lev)
    north = (wrap(lat - 1, n_lat), lon, lev)
    south = (wrap(lat + 1, n_lat), lon, lev)
    west = (lat, wrap(lon - 1, n_lon), lev)
    east = (lat, wrap(lon + 1, n_lon), lev)
    below = (lat, lon, wrap(lev - 1, n_lev))
    above = (lat, lon, wrap(lev + 1, n_lev))

    def remote(src, dst, ss, rs, device):
        return pltpu.make_async_remote_copy(
            src_ref=src, dst_ref=dst, send_sem=ss, recv_sem=rs,
            device_id=device, device_id_type=MESH,
        )

    def lanes(r, count=1):
        if isinstance(r, int):
            return pl.ds(r * LANES, count * LANES)
        return pl.ds(pl.multiple_of(r * LANES, LANES), count * LANES)

    inputs = [
        pltpu.make_async_copy(s, d, in_sem.at[i])
        for i, (s, d) in enumerate(
            ((hidden_ref, hid_v), (gamma_ref, gamma_v), (target_ref, tgt_v), (weight_ref, w_v))
        )
    ]
    for c in inputs:
        c.start()

    barrier = pltpu.get_barrier_semaphore()

    def greet(device):
        pl.semaphore_signal(barrier, inc=1, device_id=device, device_id_type=MESH)

    corners = [
        (wrap(lat + i, n_lat), wrap(lon + j, n_lon), lev) for i in (-1, 1) for j in (-1, 1)
    ]
    northwest, northeast, southwest, southeast = corners
    for device in [north, south] + corners:
        greet(device)

    def greet_chip(j, c):
        greet(at_chip(wrap(chip + j, n_chip)))
        return c

    lax.fori_loop(1, n_chip, greet_chip, 0)

    def greet_lev(j, c):
        greet((lat, lon, wrap(lev + j, n_lev)))
        return c

    lax.fori_loop(1, n_lev, greet_lev, 0)

    inputs[0].wait()
    hf[...] = hid_v[...].astype(F32).reshape(nn * rows, LANES)

    mid = slice(nn, 2 * nn)

    def spread(i, c):
        x = hf[pl.ds(i, nn, stride=rows), :]
        hx[:, lanes(i + 1)] = x
        us[mid, lanes(i + 1)] = x.astype(BF16)
        return c

    lax.fori_loop(0, rows, spread, 0, unroll=2)
    hh_send[0] = us[mid, lanes(1)]
    hh_send[1] = us[mid, lanes(rows)]

    def make_sel(r, c):
        e = lax.broadcasted_iota(jnp.int32, (64, LANES), 0)
        k = lax.broadcasted_iota(jnp.int32, (64, LANES), 1)
        last, first = k == LANES - 1, k == 0
        hit = (last & (e == r)) | (first & (e == 32 + r))
        hit = hit | ((r == rows) & ((last & (e == 0)) | (first & (e == 32))))
        hit = hit | ((r == 1) & ((last & (e == rows + 1)) | (first & (e == 33 + rows))))
        sel[:, lanes(r - 1)] = jnp.where(hit, 1.0, 0.0).astype(BF16)
        return c

    lax.fori_loop(1, rows + 1, make_sel, 0)
    columns = dot_nt(sel[...], us[mid, lanes(1, rows)]).astype(BF16)
    eu_send[0] = columns[:32]
    eu_send[1] = columns[32:]

    pl.semaphore_wait(barrier, 6 + (n_chip - 1) + (n_lev - 1))

    sends = []

    def go(copy):
        copy.start()
        sends.append(copy)
        return copy

    eu_copies = [
        go(remote(eu_send.at[i % 2], eu_recv.at[i], eu_ss.at[i], eu_rs.at[i], device))
        for i, device in enumerate((east, west, southeast, southwest, northeast, northwest))
    ] + [
        go(remote(hh_send.at[0], hh_recv.at[1], row_ss.at[0], row_rs.at[0], north)),
        go(remote(hh_send.at[1], hh_recv.at[0], row_ss.at[1], row_rs.at[1], south)),
    ]

    inputs[1].wait()
    gamma = gamma_v[...]
    g_hi, g_lo = split(gamma)
    g3[...] = jnp.concatenate([g_hi, g_lo, g_hi], axis=1)
    g_hi, g_lo = split(gamma.T)
    gt3[...] = jnp.concatenate([g_hi, g_lo, g_hi], axis=1)
    eye = lax.broadcasted_iota(jnp.int32, (nn, nn), 0) == lax.broadcasted_iota(
        jnp.int32, (nn, nn), 1
    )
    beta_col = jnp.sum(jnp.where(eye, beta_ref[...], 0.0), axis=1, keepdims=True)
    eye_c = lax.broadcasted_iota(jnp.int32, (chans, chans), 0) == lax.broadcasted_iota(
        jnp.int32, (chans, chans), 1
    )
    bias_col = jnp.sum(jnp.where(eye_c, bias_ref[...], 0.0), axis=1, keepdims=True)

    def root_of(x):
        s_hi, s_lo = split(x * x)
        total = dot(g3[...], jnp.concatenate([s_hi, s_hi, s_lo], axis=0))
        return jnp.sqrt(beta_col + total), s_hi, s_lo

    def root_tile(t, c):
        at = lanes(2 * t, 2)
        x = hx[:, lanes(2 * t + 1, 2)]
        root, s_hi, s_lo = root_of(x)
        root_s[:, at] = root
        hr_s[:, at] = x * (0.5 / root)
        sqh[:, at] = s_hi
        sql[:, at] = s_lo
        us[nn : 2 * nn, lanes(2 * t + 1, 2)] = (x * root).astype(BF16)
        return c

    lax.fori_loop(0, rows // 2, root_tile, 0, unroll=2)

    north_in = jnp.where(lat > 0, 1.0, 0.0).astype(F32)
    south_in = jnp.where(lat < n_lat - 1, 1.0, 0.0).astype(F32)

    inputs[3].wait()
    order = []
    for p in range(2):
        for a in range(2):
            for v in range(2):
                for q in range(2):
                    b = v if q else 1 - v
                    order.append(4 * (2 * p + q) + 2 * a + b)
    for g in range(4):
        block = jnp.concatenate([w_v[t] for t in order[4 * g : 4 * g + 4]], axis=0)
        wt[:, 4 * chans * g : 4 * chans * (g + 1)] = block.T

    inputs[2].wait()

    def widen(k, c):
        span = chans * rows
        tf[pl.ds(pl.multiple_of(k * span, span), span), :] = (
            tgt_v[k].astype(F32).reshape(span, LANES)
        )
        return c

    lax.fori_loop(0, 4, widen, 0)
    bacc[...] = jnp.zeros_like(bacc)
    gs[0, : 2 * chans, lanes(0)] = jnp.zeros((2 * chans, LANES), BF16)
    gs[1, : 2 * chans, lanes(rpad - 1)] = jnp.zeros((2 * chans, LANES), BF16)

    for c in eu_copies:
        c.wait_recv()
    row = lax.broadcasted_iota(jnp.int32, (32, nn), 0)

    def side(i):
        x = eu_recv[i].astype(F32)
        x = jnp.where(row == 0, eu_recv[i + 2].astype(F32) * north_in, x)
        return jnp.where(row == rows + 1, eu_recv[i + 4].astype(F32) * south_in, x)

    columns = jnp.concatenate([side(0), side(1), jnp.zeros((64, nn), F32)], axis=0).T
    x = jnp.concatenate(
        [hh_recv[0].astype(F32) * north_in, hh_recv[1].astype(F32) * south_in, columns], axis=1
    )
    root, _, _ = root_of(x)
    edge = (x * root).astype(BF16)
    us[mid, lanes(0)] = edge[:, :LANES]
    us[mid, lanes(rpad - 1)] = edge[:, LANES : 2 * LANES]
    eu_mix = edge[:, 2 * LANES :].astype(F32)

    def from_west(x, e, r):
        at = lax.broadcasted_iota(jnp.int32, x.shape, 1)
        return jnp.where(at == 0, pltpu.roll(e, LANES - r, 1), pltpu.roll(x, 1, 1))

    def from_east(x, e, r):
        at = lax.broadcasted_iota(jnp.int32, x.shape, 1)
        edge = pltpu.roll(e, LANES - 1 - r, 1)
        return jnp.where(at == LANES - 1, edge, pltpu.roll(x, LANES - 1, 1))

    def shift_u(r, c):
        x = us[mid, lanes(r)].astype(F32)
        us[:nn, lanes(r)] = from_west(x, eu_mix, r).astype(BF16)
        us[2 * nn :, lanes(r)] = from_east(x, eu_mix, 32 + r).astype(BF16)
        return c

    lax.fori_loop(0, rpad, shift_u, 0, unroll=3)

    def recon_tile(it, c):
        t = lax.rem(it + rows // 2 - 1, rows // 2)
        for p in range(2):
            area = [area_ref[lat * 2 * rows + p * rows + 2 * t + i] for i in range(2)]
            for q in range(2):
                phase = 2 * p + q
                moved = jnp.concatenate(
                    [us[q * nn : (q + 2) * nn, lanes(2 * t + p + a, 2)] for a in range(2)], axis=0
                )
                w = jnp.concatenate([w_v[4 * phase + k] for k in range(4)], axis=1)
                recon = dot(w, moved) + bias_col
                total = jnp.zeros((chans, LANES), F32)
                for i in range(2):
                    want = tf[pl.ds(phase * chans * rows + 2 * t + i, chans, stride=rows), :]
                    diff = (recon[:, i * LANES : (i + 1) * LANES] - want) * area[i]
                    total = total + diff
                    gs[p, q * chans : (q + 1) * chans, lanes(2 * t + i + 1)] = diff.astype(BF16)
                bacc[:chans, :] += total
        return c

    lax.fori_loop(0, 2, recon_tile, 0, unroll=2)
    grow_copies = [
        go(remote(gs.at[0, 0 : 2 * chans, lanes(1)], gs.at[0, 0 : 2 * chans, lanes(rpad - 1)],
                  grow_ss.at[0], grow_rs.at[0], north)),
        go(remote(gs.at[1, 0 : 2 * chans, lanes(rows)], gs.at[1, 0 : 2 * chans, lanes(0)],
                  grow_ss.at[1], grow_rs.at[1], south)),
    ]
    lax.fori_loop(2, rows // 2, recon_tile, 0, unroll=2)
    pad = LANES - chans
    for p in range(2):
        for q in range(2):
            block = gs[p, q * (chans - pad) : q * (chans - pad) + LANES, lanes(1, rows)]
            eg_send[q, p] = dot_nt(sel[32 * (1 - q) : 32 * (2 - q), :], block).astype(BF16)
    eg_copies = [
        go(remote(src, dst, eg_ss.at[i], eg_rs.at[i], device))
        for i, (src, dst, device) in enumerate((
            (eg_send.at[0], eg_recv.at[0], west),
            (eg_send.at[1], eg_recv.at[1], east),
            (eg_send.at[0, 0], eg_corner.at[0, 0], northwest),
            (eg_send.at[1, 0], eg_corner.at[1, 0], northeast),
            (eg_send.at[0, 1], eg_corner.at[0, 1], southwest),
            (eg_send.at[1, 1], eg_corner.at[1, 1], southeast),
        ))
    ]

    per_tap = chans // half

    def grad_taps(slot, p, q):
        for a in range(2):
            y = dot_nt(
                gs[p, q * chans : (q + 1) * chans, lanes(1, rows)],
                us[q * nn : (q + 2) * nn, lanes(p + a, rows)],
            )
            for b in range(2):
                for k in range(per_tap):
                    dw[slot, (4 * q + 2 * a + b) * per_tap + k] = y[
                        k * half : (k + 1) * half, b * nn : (b + 1) * nn
                    ]

    grad_taps(0, 1 - core, 0)
    grad_taps(0, 1 - core, 1)
    pw = go(remote(dw.at[0], dwp, pw_ss, pw_rs, pair))
    grad_taps(1, core, 0)

    for c in grow_copies + eg_copies:
        c.wait_recv()
    gs[0, : 2 * chans, lanes(rpad - 1)] = (
        gs[0, : 2 * chans, lanes(rpad - 1)].astype(F32) * south_in
    ).astype(BF16)
    gs[1, : 2 * chans, lanes(0)] = (
        gs[1, : 2 * chans, lanes(0)].astype(F32) * north_in
    ).astype(BF16)
    row = lax.broadcasted_iota(jnp.int32, (32, LANES), 0)
    eg_mix = {}
    for p, at, keep in ((0, rows + 1, south_in), (1, 0, north_in)):
        for q in range(2):
            x = jnp.where(
                row == at, eg_corner[q, p].astype(F32) * keep, eg_recv[q, p].astype(F32)
            )
            x = jnp.concatenate([x, jnp.zeros((LANES - 32, LANES), F32)], axis=0).T
            eg_mix[p, q] = x[q * pad : q * pad + chans]

    def shift_g(r, c):
        for p in range(2):
            rr = r + 1 - p
            x = gs[p, : 2 * chans, lanes(rr)].astype(F32)
            gs[p, 2 * chans : 3 * chans, lanes(rr)] = from_east(
                x[:chans], eg_mix[p, 0], rr
            ).astype(BF16)
            gs[p, 3 * chans :, lanes(rr)] = from_west(
                x[chans:], eg_mix[p, 1], rr
            ).astype(BF16)
        return c

    def shift_pair(i, c):
        shift_g(2 * i, c)
        return shift_g(2 * i + 1, c)

    far = n_lev // 2
    opposite = wrap(lev + far, n_lev)
    for r in range(3):
        shift_g(2 * opposite + r, 0)

    def grad_rows(*chunks):
        moved = jnp.concatenate(
            [
                jnp.concatenate([gs[p, :, lanes(2 * k + 2 - p - a, 2)] for k in chunks], axis=1)
                for p in range(2)
                for a in range(2)
            ],
            axis=0,
        )
        y = dot(wt[...], moved)
        for i, k in enumerate(chunks):
            gu[2 * k] = y[:, 2 * i * LANES : (2 * i + 1) * LANES]
            gu[2 * k + 1] = y[:, (2 * i + 1) * LANES : (2 * i + 2) * LANES]

    cuts = 2
    piece = nn // cuts
    rs_copies = {}

    def rs_send(way, s, h, first):
        owner = wrap(lev + (far + 1 - s if way else s - far - 1), n_lev)
        for k in range(cuts):
            at = pl.ds(k * piece, piece)
            x = gu[2 * owner + h, at]
            if not first:
                rs_copies[way, s - 1, h, k].wait_recv()
                x = x + unpack(arecv[way, s - 1, h, k])
            abuf[way, s, h, k] = pack(x)
            rs_copies[way, s, h, k] = go(
                remote(abuf.at[way, s, h, k], arecv.at[way, s, h, k], a_ss.at[way, s, h, k],
                       a_rs.at[way, s, h, k], above if way else below)
            )

    def over_chips(make):
        def start(j, c):
            make(j).start()
            return c

        def arrive(j, c):
            make(j).wait_recv()
            return c

        def sent(j, c):
            make(j).wait_send()
            return c

        lax.fori_loop(1, n_chip, start, 0)
        return (
            lambda: lax.fori_loop(1, n_chip, arrive, 0),
            lambda: lax.fori_loop(1, n_chip, sent, 0),
        )

    grad_rows(opposite)
    rs_send(0, 1, 0, True)
    rs_send(1, 1, 1, True)
    lax.fori_loop(0, (rows + 1) // 2, shift_pair, 0)
    shift_g(rows, 0)
    grad_rows(wrap(lev + far - 1, n_lev), wrap(lev + far + 1, n_lev))
    rs_send(1, 2, 0, True)
    rs_send(0, 2, 1, True)
    grad_taps(1, core, 1)
    pw.wait_recv()

    def join(k, c):
        dw[1, k] = dw[1, k] + dwp[k]
        rsb[k] = dw[1, k].astype(BF16)
        return c

    lax.fori_loop(0, n_chip, join, 0)

    def rb_make(j):
        k = wrap(chip + j, n_chip)
        return remote(rsb.at[k], rsr.at[j], rb_ss.at[j], rb_rs.at[j], at_chip(k))

    rb_arrive, rb_sent = over_chips(rb_make)
    grad_rows(wrap(lev + far - 2, n_lev), wrap(lev + far + 2, n_lev))
    grad_rows(wrap(lev + 1, n_lev), wrap(lev + n_lev - 1, n_lev))
    grad_rows(lev)

    def mix_tile(t, acc):
        at = lanes(2 * t, 2)
        g = jnp.concatenate([gu[2 * t], gu[2 * t + 1]], axis=1)
        mixing = g * hr_s[:, at]
        m_hi, m_lo = split(mixing)
        mh[:, at] = m_hi
        ml[:, at] = m_lo
        return acc + mixing[:, :LANES] + mixing[:, LANES:]

    msum = lax.fori_loop(0, rows // 2, mix_tile, jnp.zeros((nn, LANES), F32))
    beta_part = jnp.sum(msum, axis=1, keepdims=True)
    bias_part = jnp.sum(bacc[...].T, axis=0, keepdims=True)
    ext[:, :nn] = dot_nt(mh[...], sqh[...]) + (
        dot_nt(ml[...], sqh[...]) + dot_nt(mh[...], sql[...])
    )
    lane = lax.broadcasted_iota(jnp.int32, (nn, LANES), 1)
    ext[:, nn:] = jnp.where(lane == LANES - 1, beta_part, bias_part)
    mine = pl.multiple_of(core * (nn // 2), nn // 2)
    others = pl.multiple_of((1 - core) * (nn // 2), nn // 2)
    pe = go(remote(ext.at[pl.ds(others, nn // 2)], extp, pe_ss, pe_rs, pair))

    rs_send(0, 2, 0, False)
    rs_send(1, 2, 1, False)

    pe.wait_recv()

    def join_ext(k, c):
        at = pl.ds(pl.multiple_of(mine + k * share, share), share)
        exts[k] = ext[at, :] + extp[pl.ds(pl.multiple_of(k * share, share), share), :]
        return c

    lax.fori_loop(0, n_chip, join_ext, 0)
    extr[chip] = exts[chip]

    def rc_make(j):
        k = wrap(chip + j, n_chip)
        return remote(exts.at[k], extr.at[chip], rc_ss.at[j], rc_rs.at[j], at_chip(k))

    rc_arrive, rc_sent = over_chips(rc_make)
    rs_send(1, 3, 0, False)
    rs_send(0, 3, 1, False)
    rs_send(0, 3, 0, False)
    rs_send(1, 3, 1, False)

    rs_send(1, 4, 0, False)
    rs_send(0, 4, 1, False)

    rb_arrive()

    def add_taps(j, acc):
        return acc + rsr[j].astype(F32)

    wown[...] = lax.fori_loop(1, n_chip, add_taps, dw[1, chip]) * (1.0 / total_cells)
    w_copy = pltpu.make_async_copy(wown, gw_out.at[core, chip], out_sem.at[0])
    w_copy.start()

    def ab_make(j):
        k = wrap(chip + j, n_chip)
        return remote(wown, gw_out.at[core, chip], ab_ss.at[j], ab_rs.at[j], at_chip(k))

    ab_arrive, ab_sent = over_chips(ab_make)
    rs_send(0, 4, 0, False)
    rs_send(1, 4, 1, False)

    rc_arrive()

    def add_ext(k, acc):
        return acc + extr[k]

    plane = lax.fori_loop(1, n_chip, add_ext, extr[0])
    gb_out[...] = plane[0:1, nn : nn + chans] * (1.0 / total_cells)
    extz[lev] = plane

    def z_make(j):
        return remote(
            extz.at[lev], extz.at[lev], z_ss.at[j], z_rs.at[j], (lat, lon, wrap(lev + j, n_lev))
        )

    for j in range(1, n_lev):
        z_make(j).start()

    for way, h in ((1, 0), (0, 1), (0, 0), (1, 1)):
        for k in range(cuts):
            rs_copies[way, far, h, k].wait_recv()
    g = jnp.concatenate(
        [
            gu[2 * lev + h]
            + jnp.concatenate(
                [unpack(arecv[0, far, h, k]) + unpack(arecv[1, far, h, k]) for k in range(cuts)],
                axis=0,
            )
            for h in range(2)
        ],
        axis=1,
    )
    at = lanes(2 * lev, 2)
    m_hi, m_lo = split(g * hr_s[:, at])
    back = dot(gt3[...], jnp.concatenate([m_hi, m_hi, m_lo], axis=0))
    gh = (g * root_s[:, at] + 2.0 * hx[:, lanes(2 * lev + 1, 2)] * back).astype(BF16)
    agr[2 * lev] = gh[:, :LANES]
    agr[2 * lev + 1] = gh[:, LANES:]

    ag_copies = {}

    def ag_send(s):
        for h in range(2):
            for way in range(2):
                if s == far and h != way:
                    continue
                owner = wrap(lev + (1 - s if way else s - 1), n_lev)
                for k in range(cuts):
                    if s > 1:
                        ag_copies[way, s - 1, h, k].wait_recv()
                    block = agr.at[2 * owner + h, pl.ds(k * piece, piece)]
                    ag_copies[way, s, h, k] = go(
                        remote(block, block, g_ss.at[way, s, h, k], g_rs.at[way, s, h, k],
                               above if way else below)
                    )

    put_copies = []

    def put(i, owner):
        block = pl.ds(2 * owner, 2)
        copy = pltpu.make_async_copy(agr.at[block], gh_out.at[block], put_sem.at[i])
        copy.start()
        put_copies.append(copy)

    ag_send(1)
    put(0, lev)
    for j in range(1, n_lev):
        z_make(j).wait_recv()
    whole = extz[0]
    for k in range(1, n_lev):
        whole = whole + extz[k]
    eown[...] = whole * (1.0 / total_cells)
    e_copy = pltpu.make_async_copy(eown, ext_out.at[core, chip], out_sem.at[1])
    e_copy.start()

    def ac_make(j):
        k = wrap(chip + j, n_chip)
        return remote(eown, ext_out.at[core, chip], ac_ss.at[j], ac_rs.at[j], at_chip(k))

    ac_arrive, ac_sent = over_chips(ac_make)
    ag_send(2)
    put(1, wrap(lev + 1, n_lev))
    put(2, wrap(lev - 1, n_lev))
    ab_arrive()
    w_copy.wait()
    pg = go(remote(gw_out.at[core], gw_out.at[core], pg_ss, pg_rs, pair))
    ag_send(3)
    put(3, wrap(lev + 2, n_lev))
    put(4, wrap(lev - 2, n_lev))
    ac_arrive()
    e_copy.wait()
    pc = go(remote(ext_out.at[core], ext_out.at[core], pc_ss, pc_rs, pair))
    ag_send(4)
    for way in range(2):
        for k in range(cuts):
            ag_copies[way, far - 1, 1 - way, k].wait_recv()
    put(5, wrap(lev + 3, n_lev))
    put(6, wrap(lev - 3, n_lev))
    pc.wait_recv()
    pg.wait_recv()
    for way in range(2):
        for k in range(cuts):
            ag_copies[way, far, way, k].wait_recv()
    put(7, wrap(lev + far, n_lev))

    for c in sends:
        c.wait_send()
    rb_sent()
    ab_sent()
    rc_sent()
    ac_sent()
    for j in range(1, n_lev):
        z_make(j).wait_send()
    for c in put_copies:
        c.wait()


def finish(
    dims, agr_ref, wg_ref, ext_ref, gb_ref,
    gh_out, gw_out, gg_out, gbeta_out, gb_out,
    agr, gho, gw_v, ext_v, gg_v, in_sem, out_sem, gw_sem, ext_sem,
):
    nn, rows, parts = dims
    step = nn // parts

    def fetch(k):
        at = pl.ds(k * step, step)
        return pltpu.make_async_copy(agr_ref.at[:, at], agr.at[:, at], in_sem.at[k])

    def store(k):
        at = pl.ds(k * step * rows, step * rows)
        return pltpu.make_async_copy(gho.at[at], gh_out.at[at], out_sem.at[k])

    def fetch_gw(k):
        return pltpu.make_async_copy(wg_ref.at[k], gw_v.at[k], gw_sem.at[0, k])

    def store_gw(k):
        return pltpu.make_async_copy(gw_v.at[k], gw_out.at[k], gw_sem.at[1, k])

    fetch_ext = pltpu.make_async_copy(ext_ref, ext_v, ext_sem.at[0])
    store_gg = pltpu.make_async_copy(gg_v, gg_out, ext_sem.at[1])
    for k in range(parts):
        fetch(k).start()
    fetch_ext.start()
    for k in range(2):
        fetch_gw(k).start()
    gb_out[...] = gb_ref[...]
    eye = lax.broadcasted_iota(jnp.int32, (nn, nn), 0) == lax.broadcasted_iota(
        jnp.int32, (nn, nn), 1
    )
    for k in range(parts):
        fetch(k).wait()
        for i in range(rows):
            gho[pl.ds(k * step * rows + i, step, stride=rows), :] = agr[
                i, k * step : (k + 1) * step, :
            ].astype(F32)
        store(k).start()
        if k < 2:
            fetch_gw(k).wait()
            store_gw(k).start()
    fetch_ext.wait()
    full = ext_v[...].reshape(nn, nn + LANES)
    gg_v[...] = full[:, :nn]
    store_gg.start()
    gbeta_out[...] = jnp.sum(
        jnp.where(eye, full[:, nn + LANES - 1 : nn + LANES], 0.0), axis=0, keepdims=True
    )
    for k in range(parts):
        store(k).wait()
    store_gg.wait()
    for k in range(2):
        store_gw(k).wait()


def local(sizes, target, hidden, weight, bias, gamma, beta):
    n_lat, n_lon, n_lev = sizes
    nn, rows, cols = hidden.shape
    chans = weight.shape[1]
    taps = weight.shape[0]
    n_chip = n_lat // 2 * n_lon
    half = taps // 2 * chans // n_chip
    share = nn // 2 // n_chip
    cells = rows * cols
    rpad = rows + 2
    total_rows = rows * n_lat
    total_cells = total_rows * cols * n_lon
    far = n_lev // 2
    at = np.arange(total_rows).reshape(n_lat, 1, rows) * 2.0 + np.arange(2).reshape(1, 2, 1)
    area = np.cos(math.pi * ((at + 0.5) / (2.0 * total_rows) - 0.5)).astype(np.float32)
    dims = (nn, rows, chans, n_lat, n_lon, n_lev, 4, total_cells)
    wide = nn + LANES
    V = pltpu.VMEM
    D = pltpu.SemaphoreType.DMA
    scratch = [
        V((nn, rows, cols), BF16), V((4, chans, rows, cols), BF16), V((taps, chans, nn), BF16),
        V((nn, nn), F32),
        V((nn * rows, cols), F32), V((4 * chans * rows, cols), F32), V((nn, rpad * cols), F32),
        V((nn, cells), F32), V((nn, cells), F32), V((nn, cells), BF16), V((nn, cells), BF16),
        V((nn, 3 * nn), BF16), V((nn, 3 * nn), BF16), V((nn, taps * chans), BF16),
        V((3 * nn, rpad * cols), BF16), V((2, 4 * chans, rpad * cols), BF16),
        V((64, cells), BF16), V((2, nn, cols), BF16), V((2, nn, cols), BF16),
        V((2, 32, nn), BF16), V((6, 32, nn), BF16),
        V((2, 2, 32, cols), BF16), V((2, 2, 32, cols), BF16), V((2, 2, 32, cols), BF16),
        V((2, n_chip, half, nn), F32), V((n_chip, half, nn), F32), V((n_chip, half, nn), BF16),
        V((n_chip, half, nn), BF16), V((half, nn), F32),
        V((rows, nn, cols), F32), V((cols, cols), F32), V((nn, cells), BF16), V((nn, cells), BF16),
        V((nn, wide), F32), V((nn // 2, wide), F32), V((n_chip, share, wide), F32),
        V((n_chip, share, wide), F32), V((n_lev, share, wide), F32),
        V((share, wide), F32),
        V((2, far + 1, 2, 2, nn // 4 * 3, cols), BF16),
        V((2, far + 1, 2, 2, nn // 4 * 3, cols), BF16),
        V((rows, nn, cols), BF16),
        D((4,)), D((2,)), D((n_lev,)),
        D((2,)), D((2,)), D((6,)), D((6,)), D((2,)), D((2,)), D((6,)), D((6,)),
        D, D, D((n_chip,)), D((n_chip,)), D((n_chip,)), D((n_chip,)), D, D,
        D, D, D((n_chip,)), D((n_chip,)), D((n_lev,)), D((n_lev,)), D((n_chip,)), D((n_chip,)),
        D, D,
        D((2, far + 1, 2, 2)), D((2, far + 1, 2, 2)),
        D((2, far + 1, 2, 2)), D((2, far + 1, 2, 2)),
    ]
    hbm = pl.BlockSpec(memory_space=pl.ANY)
    vmem = pl.BlockSpec(memory_space=pltpu.VMEM)
    smem = pl.BlockSpec(memory_space=pltpu.SMEM)
    agr, wg, ext, gb = pl.pallas_call(
        functools.partial(kernel, dims),
        out_shape=(
            jax.ShapeDtypeStruct((rows, nn, cols), BF16),
            jax.ShapeDtypeStruct((2, n_chip, half, nn), F32),
            jax.ShapeDtypeStruct((2, n_chip, share, wide), F32),
            jax.ShapeDtypeStruct((1, chans), F32),
        ),
        in_specs=[smem, hbm, hbm, hbm, vmem, hbm, vmem],
        out_specs=(hbm, hbm, hbm, vmem),
        scratch_shapes=scratch,
        compiler_params=pltpu.CompilerParams(
            collective_id=0, has_side_effects=True, vmem_limit_bytes=60 * 2**20
        ),
    )(
        jnp.asarray(area.reshape(-1)), hidden, target, weight, bias.reshape(1, chans),
        gamma, beta.reshape(1, nn),
    )
    parts = 4
    gh, gw, gg, gbeta, gb = pl.pallas_call(
        functools.partial(finish, (nn, rows, parts)),
        out_shape=(
            jax.ShapeDtypeStruct((nn * rows, cols), F32),
            jax.ShapeDtypeStruct((2, n_chip, half, nn), F32),
            jax.ShapeDtypeStruct((nn, nn), F32),
            jax.ShapeDtypeStruct((1, nn), F32),
            jax.ShapeDtypeStruct((1, chans), F32),
        ),
        in_specs=[hbm, hbm, hbm, vmem],
        out_specs=(hbm, hbm, hbm, vmem, vmem),
        scratch_shapes=[
            V((rows, nn, cols), BF16), V((nn * rows, cols), F32), V((2, n_chip, half, nn), F32),
            V((2, n_chip, share, wide), F32), V((nn, nn), F32),
            D((parts,)), D((parts,)), D((2, 2)), D((2,)),
        ],
        compiler_params=pltpu.CompilerParams(vmem_limit_bytes=60 * 2**20),
    )(agr, wg, ext, gb)
    return (
        gh.reshape(nn, rows, cols), gw.reshape(taps, chans, nn), gb.reshape(chans), gg,
        gbeta.reshape(nn),
    )


def solution(mesh):
    sizes = tuple(mesh.shape[a] for a in ("lat", "lon", "lev"))
    return jax.shard_map(
        functools.partial(local, sizes),
        mesh=mesh,
        in_specs=(
            P(None, "lev", "lat", "lon"),
            P(None, "lat", "lon"),
            P(None, "lev", None),
            P("lev"),
            P(),
            P(),
        ),
        out_specs=(P(None, "lat", "lon"), P(None, "lev", None), P("lev"), P(), P()),
        check_vma=False,
    )
```

```python
import functools
import math

import jax
import jax.numpy as jnp
import numpy as np
from jax import lax
from jax.experimental import pallas as pl
from jax.experimental.pallas import tpu as pltpu
from jax.sharding import PartitionSpec as P

F32 = jnp.float32
BF16 = jnp.bfloat16
MESH = pl.DeviceIdType.MESH
LANES = 128


def split(x):
    hi = x.astype(BF16)
    return hi, (x - hi.astype(F32)).astype(BF16)


def dot(a, b):
    return jnp.dot(a, b, preferred_element_type=F32)


def dot_nt(a, b):
    return lax.dot_general(a, b, (((1,), (1,)), ((), ())), preferred_element_type=F32)


STEPS = 1920.0


def pack(x):
    hi = x.astype(BF16)
    h = hi.astype(F32)
    scale = pl.reciprocal(jnp.maximum(jnp.abs(h), 1e-30), approx=True) * STEPS
    q = jnp.clip(jnp.floor((x - h) * scale + 0.5), -8.0, 7.0)
    m = x.shape[0] // 2
    return jnp.concatenate([hi, (16.0 * q[:m] + q[m:]).astype(BF16)], axis=0)


def unpack(y):
    m = y.shape[0] // 3
    h, p = y[: 2 * m].astype(F32), y[2 * m :].astype(F32)
    a = jnp.floor((p + 8.0) * 0.0625)
    q = jnp.concatenate([a, p - 16.0 * a], axis=0)
    return h + jnp.abs(h) * (q * (1.0 / STEPS))


def wrap(index, size):
    return lax.rem(index + size, size)


def kernel(
    dims,
    area_ref, hidden_ref, target_ref, weight_ref, bias_ref, gamma_ref, beta_ref,
    gh_out, gw_out, ext_out, gb_out,
    hid_v, tgt_v, w_v, gamma_v,
    hf, tf, hx, root_s, hr_s, sqh, sql, g3, gt3, wt,
    us, gs, sel, hh_send, hh_recv, eu_send, eu_recv, eg_send, eg_recv, eg_corner,
    dw, dwp, rsb, rsr, wg,
    gu, bacc, mh, ml, ext, extp, exts, extr, extz, extg,
    abuf, arecv, agr,
    in_sem, out_sem, put_sem,
    row_ss, row_rs, eu_ss, eu_rs, grow_ss, grow_rs, eg_ss, eg_rs,
    pw_ss, pw_rs, rb_ss, rb_rs, ab_ss, ab_rs, pg_ss, pg_rs,
    pe_ss, pe_rs, rc_ss, rc_rs, z_ss, z_rs, ac_ss, ac_rs, pc_ss, pc_rs,
    a_ss, a_rs, g_ss, g_rs,
):
    nn, rows, chans, n_lat, n_lon, n_lev, n_y, total_cells = dims
    cells = rows * LANES
    rpad = rows + 2
    lat, lon, lev = lax.axis_index("lat"), lax.axis_index("lon"), lax.axis_index("lev")
    core = lax.rem(lat, 2)
    n_chip = (n_lat // 2) * n_lon
    n_xlo = n_lon // n_y
    chip = lax.div(lat, 2) * n_lon + lon
    half = 16 // 2 * chans // n_chip
    share = nn // 2 // n_chip

    def at_chip(k):
        return (lax.div(k, n_lon) * 2 + core, lax.rem(k, n_lon), lev)

    pair = (lat + 1 - 2 * core, lon, lev)
    north = (wrap(lat - 1, n_lat), lon, lev)
    south = (wrap(lat + 1, n_lat), lon, lev)
    west = (lat, wrap(lon - 1, n_lon), lev)
    east = (lat, wrap(lon + 1, n_lon), lev)
    below = (lat, lon, wrap(lev - 1, n_lev))
    above = (lat, lon, wrap(lev + 1, n_lev))

    def remote(src, dst, ss, rs, device):
        return pltpu.make_async_remote_copy(
            src_ref=src, dst_ref=dst, send_sem=ss, recv_sem=rs,
            device_id=device, device_id_type=MESH,
        )

    def lanes(r, count=1):
        if isinstance(r, int):
            return pl.ds(r * LANES, count * LANES)
        return pl.ds(pl.multiple_of(r * LANES, LANES), count * LANES)

    inputs = [
        pltpu.make_async_copy(s, d, in_sem.at[i])
        for i, (s, d) in enumerate(
            ((hidden_ref, hid_v), (gamma_ref, gamma_v), (target_ref, tgt_v), (weight_ref, w_v))
        )
    ]
    for c in inputs:
        c.start()

    barrier = pltpu.get_barrier_semaphore()

    def greet(device):
        pl.semaphore_signal(barrier, inc=1, device_id=device, device_id_type=MESH)

    corners = [
        (wrap(lat + i, n_lat), wrap(lon + j, n_lon), lev) for i in (-1, 1) for j in (-1, 1)
    ]
    northwest, northeast, southwest, southeast = corners
    for device in [north, south] + corners:
        greet(device)

    def greet_chip(j, c):
        greet(at_chip(wrap(chip + j, n_chip)))
        return c

    lax.fori_loop(1, n_chip, greet_chip, 0)

    def greet_lev(j, c):
        greet((lat, lon, wrap(lev + j, n_lev)))
        return c

    lax.fori_loop(1, n_lev, greet_lev, 0)

    inputs[0].wait()
    hf[...] = hid_v[...].astype(F32).reshape(nn * rows, LANES)

    mid = slice(nn, 2 * nn)

    def spread(i, c):
        x = hf[pl.ds(i, nn, stride=rows), :]
        hx[:, lanes(i + 1)] = x
        us[mid, lanes(i + 1)] = x.astype(BF16)
        return c

    lax.fori_loop(0, rows, spread, 0, unroll=2)
    hh_send[0] = us[mid, lanes(1)]
    hh_send[1] = us[mid, lanes(rows)]

    def make_sel(r, c):
        e = lax.broadcasted_iota(jnp.int32, (64, LANES), 0)
        k = lax.broadcasted_iota(jnp.int32, (64, LANES), 1)
        last, first = k == LANES - 1, k == 0
        hit = (last & (e == r)) | (first & (e == 32 + r))
        hit = hit | ((r == rows) & ((last & (e == 0)) | (first & (e == 32))))
        hit = hit | ((r == 1) & ((last & (e == rows + 1)) | (first & (e == 33 + rows))))
        sel[:, lanes(r - 1)] = jnp.where(hit, 1.0, 0.0).astype(BF16)
        return c

    lax.fori_loop(1, rows + 1, make_sel, 0)
    columns = dot_nt(sel[...], us[mid, lanes(1, rows)]).astype(BF16)
    eu_send[0] = columns[:32]
    eu_send[1] = columns[32:]

    pl.semaphore_wait(barrier, 6 + (n_chip - 1) + (n_lev - 1))

    sends = []

    def go(copy):
        copy.start()
        sends.append(copy)
        return copy

    eu_copies = [
        go(remote(eu_send.at[i % 2], eu_recv.at[i], eu_ss.at[i], eu_rs.at[i], device))
        for i, device in enumerate((east, west, southeast, southwest, northeast, northwest))
    ] + [
        go(remote(hh_send.at[0], hh_recv.at[1], row_ss.at[0], row_rs.at[0], north)),
        go(remote(hh_send.at[1], hh_recv.at[0], row_ss.at[1], row_rs.at[1], south)),
    ]

    inputs[1].wait()
    gamma = gamma_v[...]
    g_hi, g_lo = split(gamma)
    g3[...] = jnp.concatenate([g_hi, g_lo, g_hi], axis=1)
    g_hi, g_lo = split(gamma.T)
    gt3[...] = jnp.concatenate([g_hi, g_lo, g_hi], axis=1)
    eye = lax.broadcasted_iota(jnp.int32, (nn, nn), 0) == lax.broadcasted_iota(
        jnp.int32, (nn, nn), 1
    )
    beta_col = jnp.sum(jnp.where(eye, beta_ref[...], 0.0), axis=1, keepdims=True)
    eye_c = lax.broadcasted_iota(jnp.int32, (chans, chans), 0) == lax.broadcasted_iota(
        jnp.int32, (chans, chans), 1
    )
    bias_col = jnp.sum(jnp.where(eye_c, bias_ref[...], 0.0), axis=1, keepdims=True)

    def root_of(x):
        s_hi, s_lo = split(x * x)
        total = dot(g3[...], jnp.concatenate([s_hi, s_hi, s_lo], axis=0))
        return jnp.sqrt(beta_col + total), s_hi, s_lo

    def root_tile(t, c):
        at = lanes(2 * t, 2)
        x = hx[:, lanes(2 * t + 1, 2)]
        root, s_hi, s_lo = root_of(x)
        root_s[:, at] = root
        hr_s[:, at] = x * (0.5 / root)
        sqh[:, at] = s_hi
        sql[:, at] = s_lo
        us[nn : 2 * nn, lanes(2 * t + 1, 2)] = (x * root).astype(BF16)
        return c

    lax.fori_loop(0, rows // 2, root_tile, 0, unroll=2)

    north_in = jnp.where(lat > 0, 1.0, 0.0).astype(F32)
    south_in = jnp.where(lat < n_lat - 1, 1.0, 0.0).astype(F32)

    inputs[3].wait()
    order = []
    for p in range(2):
        for a in range(2):
            for v in range(2):
                for q in range(2):
                    b = v if q else 1 - v
                    order.append(4 * (2 * p + q) + 2 * a + b)
    for g in range(4):
        block = jnp.concatenate([w_v[t] for t in order[4 * g : 4 * g + 4]], axis=0)
        wt[:, 4 * chans * g : 4 * chans * (g + 1)] = block.T

    inputs[2].wait()

    def widen(k, c):
        span = chans * rows
        tf[pl.ds(pl.multiple_of(k * span, span), span), :] = (
            tgt_v[k].astype(F32).reshape(span, LANES)
        )
        return c

    lax.fori_loop(0, 4, widen, 0)
    bacc[...] = jnp.zeros_like(bacc)
    gs[0, : 2 * chans, lanes(0)] = jnp.zeros((2 * chans, LANES), BF16)
    gs[1, : 2 * chans, lanes(rpad - 1)] = jnp.zeros((2 * chans, LANES), BF16)

    for c in eu_copies:
        c.wait_recv()
    row = lax.broadcasted_iota(jnp.int32, (32, nn), 0)

    def side(i):
        x = eu_recv[i].astype(F32)
        x = jnp.where(row == 0, eu_recv[i + 2].astype(F32) * north_in, x)
        return jnp.where(row == rows + 1, eu_recv[i + 4].astype(F32) * south_in, x)

    columns = jnp.concatenate([side(0), side(1), jnp.zeros((64, nn), F32)], axis=0).T
    x = jnp.concatenate(
        [hh_recv[0].astype(F32) * north_in, hh_recv[1].astype(F32) * south_in, columns], axis=1
    )
    root, _, _ = root_of(x)
    edge = (x * root).astype(BF16)
    us[mid, lanes(0)] = edge[:, :LANES]
    us[mid, lanes(rpad - 1)] = edge[:, LANES : 2 * LANES]
    eu_mix = edge[:, 2 * LANES :].astype(F32)

    def from_west(x, e, r):
        at = lax.broadcasted_iota(jnp.int32, x.shape, 1)
        return jnp.where(at == 0, pltpu.roll(e, LANES - r, 1), pltpu.roll(x, 1, 1))

    def from_east(x, e, r):
        at = lax.broadcasted_iota(jnp.int32, x.shape, 1)
        edge = pltpu.roll(e, LANES - 1 - r, 1)
        return jnp.where(at == LANES - 1, edge, pltpu.roll(x, LANES - 1, 1))

    def shift_u(r, c):
        x = us[mid, lanes(r)].astype(F32)
        us[:nn, lanes(r)] = from_west(x, eu_mix, r).astype(BF16)
        us[2 * nn :, lanes(r)] = from_east(x, eu_mix, 32 + r).astype(BF16)
        return c

    lax.fori_loop(0, rpad, shift_u, 0, unroll=3)

    def recon_tile(it, c):
        t = lax.rem(it + rows // 2 - 1, rows // 2)
        for p in range(2):
            area = [area_ref[lat * 2 * rows + p * rows + 2 * t + i] for i in range(2)]
            for q in range(2):
                phase = 2 * p + q
                moved = jnp.concatenate(
                    [us[q * nn : (q + 2) * nn, lanes(2 * t + p + a, 2)] for a in range(2)], axis=0
                )
                w = jnp.concatenate([w_v[4 * phase + k] for k in range(4)], axis=1)
                recon = dot(w, moved) + bias_col
                total = jnp.zeros((chans, LANES), F32)
                for i in range(2):
                    want = tf[pl.ds(phase * chans * rows + 2 * t + i, chans, stride=rows), :]
                    diff = (recon[:, i * LANES : (i + 1) * LANES] - want) * area[i]
                    total = total + diff
                    gs[p, q * chans : (q + 1) * chans, lanes(2 * t + i + 1)] = diff.astype(BF16)
                bacc[:chans, :] += total
        return c

    lax.fori_loop(0, 2, recon_tile, 0, unroll=2)
    grow_copies = [
        go(remote(gs.at[0, 0 : 2 * chans, lanes(1)], gs.at[0, 0 : 2 * chans, lanes(rpad - 1)],
                  grow_ss.at[0], grow_rs.at[0], north)),
        go(remote(gs.at[1, 0 : 2 * chans, lanes(rows)], gs.at[1, 0 : 2 * chans, lanes(0)],
                  grow_ss.at[1], grow_rs.at[1], south)),
    ]
    lax.fori_loop(2, rows // 2, recon_tile, 0, unroll=2)
    pad = LANES - chans
    for p in range(2):
        for q in range(2):
            block = gs[p, q * (chans - pad) : q * (chans - pad) + LANES, lanes(1, rows)]
            eg_send[q, p] = dot_nt(sel[32 * (1 - q) : 32 * (2 - q), :], block).astype(BF16)
    eg_copies = [
        go(remote(src, dst, eg_ss.at[i], eg_rs.at[i], device))
        for i, (src, dst, device) in enumerate((
            (eg_send.at[0], eg_recv.at[0], west),
            (eg_send.at[1], eg_recv.at[1], east),
            (eg_send.at[0, 0], eg_corner.at[0, 0], northwest),
            (eg_send.at[1, 0], eg_corner.at[1, 0], northeast),
            (eg_send.at[0, 1], eg_corner.at[0, 1], southwest),
            (eg_send.at[1, 1], eg_corner.at[1, 1], southeast),
        ))
    ]

    per_tap = chans // half

    def grad_taps(slot, p, q):
        for a in range(2):
            y = dot_nt(
                gs[p, q * chans : (q + 1) * chans, lanes(1, rows)],
                us[q * nn : (q + 2) * nn, lanes(p + a, rows)],
            )
            for b in range(2):
                for k in range(per_tap):
                    dw[slot, (4 * q + 2 * a + b) * per_tap + k] = y[
                        k * half : (k + 1) * half, b * nn : (b + 1) * nn
                    ]

    grad_taps(0, 1 - core, 0)
    grad_taps(0, 1 - core, 1)
    pw = go(remote(dw.at[0], dwp, pw_ss, pw_rs, pair))
    grad_taps(1, core, 0)

    for c in grow_copies + eg_copies:
        c.wait_recv()
    gs[0, : 2 * chans, lanes(rpad - 1)] = (
        gs[0, : 2 * chans, lanes(rpad - 1)].astype(F32) * south_in
    ).astype(BF16)
    gs[1, : 2 * chans, lanes(0)] = (
        gs[1, : 2 * chans, lanes(0)].astype(F32) * north_in
    ).astype(BF16)
    row = lax.broadcasted_iota(jnp.int32, (32, LANES), 0)
    eg_mix = {}
    for p, at, keep in ((0, rows + 1, south_in), (1, 0, north_in)):
        for q in range(2):
            x = jnp.where(
                row == at, eg_corner[q, p].astype(F32) * keep, eg_recv[q, p].astype(F32)
            )
            x = jnp.concatenate([x, jnp.zeros((LANES - 32, LANES), F32)], axis=0).T
            eg_mix[p, q] = x[q * pad : q * pad + chans]

    def shift_g(r, c):
        for p in range(2):
            rr = r + 1 - p
            x = gs[p, : 2 * chans, lanes(rr)].astype(F32)
            gs[p, 2 * chans : 3 * chans, lanes(rr)] = from_east(
                x[:chans], eg_mix[p, 0], rr
            ).astype(BF16)
            gs[p, 3 * chans :, lanes(rr)] = from_west(
                x[chans:], eg_mix[p, 1], rr
            ).astype(BF16)
        return c

    def shift_pair(i, c):
        shift_g(2 * i, c)
        return shift_g(2 * i + 1, c)

    far = n_lev // 2
    opposite = wrap(lev + far, n_lev)
    for r in range(3):
        shift_g(2 * opposite + r, 0)

    def grad_rows(*chunks):
        moved = jnp.concatenate(
            [
                jnp.concatenate([gs[p, :, lanes(2 * k + 2 - p - a, 2)] for k in chunks], axis=1)
                for p in range(2)
                for a in range(2)
            ],
            axis=0,
        )
        y = dot(wt[...], moved)
        for i, k in enumerate(chunks):
            gu[2 * k] = y[:, 2 * i * LANES : (2 * i + 1) * LANES]
            gu[2 * k + 1] = y[:, (2 * i + 1) * LANES : (2 * i + 2) * LANES]

    cuts = 2
    piece = nn // cuts
    rs_copies = {}

    def rs_send(way, s, h, first):
        owner = wrap(lev + (far + 1 - s if way else s - far - 1), n_lev)
        for k in range(cuts):
            at = pl.ds(k * piece, piece)
            x = gu[2 * owner + h, at]
            if not first:
                rs_copies[way, s - 1, h, k].wait_recv()
                x = x + unpack(arecv[way, s - 1, h, k])
            abuf[way, s, h, k] = pack(x)
            rs_copies[way, s, h, k] = go(
                remote(abuf.at[way, s, h, k], arecv.at[way, s, h, k], a_ss.at[way, s, h, k],
                       a_rs.at[way, s, h, k], above if way else below)
            )

    def over_chips(make):
        def start(j, c):
            make(j).start()
            return c

        def arrive(j, c):
            make(j).wait_recv()
            return c

        def sent(j, c):
            make(j).wait_send()
            return c

        lax.fori_loop(1, n_chip, start, 0)
        return (
            lambda: lax.fori_loop(1, n_chip, arrive, 0),
            lambda: lax.fori_loop(1, n_chip, sent, 0),
        )

    grad_rows(opposite)
    rs_send(0, 1, 0, True)
    rs_send(1, 1, 1, True)
    lax.fori_loop(0, (rows + 1) // 2, shift_pair, 0)
    shift_g(rows, 0)
    grad_rows(wrap(lev + far - 1, n_lev), wrap(lev + far + 1, n_lev))
    rs_send(1, 2, 0, True)
    rs_send(0, 2, 1, True)
    grad_taps(1, core, 1)
    pw.wait_recv()

    def join(k, c):
        dw[1, k] = dw[1, k] + dwp[k]
        rsb[k] = dw[1, k].astype(BF16)
        return c

    lax.fori_loop(0, n_chip, join, 0)

    def rb_make(j):
        k = wrap(chip + j, n_chip)
        return remote(rsb.at[k], rsr.at[j], rb_ss.at[j], rb_rs.at[j], at_chip(k))

    rb_arrive, rb_sent = over_chips(rb_make)
    grad_rows(wrap(lev + far - 2, n_lev), wrap(lev + far + 2, n_lev))
    grad_rows(wrap(lev + 1, n_lev), wrap(lev + n_lev - 1, n_lev))
    grad_rows(lev)

    def mix_tile(t, acc):
        at = lanes(2 * t, 2)
        g = jnp.concatenate([gu[2 * t], gu[2 * t + 1]], axis=1)
        mixing = g * hr_s[:, at]
        m_hi, m_lo = split(mixing)
        mh[:, at] = m_hi
        ml[:, at] = m_lo
        return acc + mixing[:, :LANES] + mixing[:, LANES:]

    msum = lax.fori_loop(0, rows // 2, mix_tile, jnp.zeros((nn, LANES), F32))
    beta_part = jnp.sum(msum, axis=1, keepdims=True)
    bias_part = jnp.sum(bacc[...].T, axis=0, keepdims=True)
    ext[:, :nn] = dot_nt(mh[...], sqh[...]) + (
        dot_nt(ml[...], sqh[...]) + dot_nt(mh[...], sql[...])
    )
    lane = lax.broadcasted_iota(jnp.int32, (nn, LANES), 1)
    ext[:, nn:] = jnp.where(lane == LANES - 1, beta_part, bias_part)
    mine = pl.multiple_of(core * (nn // 2), nn // 2)
    others = pl.multiple_of((1 - core) * (nn // 2), nn // 2)
    pe = go(remote(ext.at[pl.ds(others, nn // 2)], extp, pe_ss, pe_rs, pair))

    rs_send(0, 2, 0, False)
    rs_send(1, 2, 1, False)

    pe.wait_recv()

    def join_ext(k, c):
        at = pl.ds(pl.multiple_of(mine + k * share, share), share)
        exts[k] = ext[at, :] + extp[pl.ds(pl.multiple_of(k * share, share), share), :]
        return c

    lax.fori_loop(0, n_chip, join_ext, 0)
    extr[chip] = exts[chip]

    def rc_make(j):
        k = wrap(chip + j, n_chip)
        return remote(exts.at[k], extr.at[chip], rc_ss.at[j], rc_rs.at[j], at_chip(k))

    rc_arrive, rc_sent = over_chips(rc_make)
    rs_send(1, 3, 0, False)
    rs_send(0, 3, 1, False)
    rs_send(0, 3, 0, False)
    rs_send(1, 3, 1, False)

    rs_send(1, 4, 0, False)
    rs_send(0, 4, 1, False)

    rb_arrive()

    def add_taps(j, acc):
        return acc + rsr[j].astype(F32)

    wg[core, chip] = lax.fori_loop(1, n_chip, add_taps, dw[1, chip]) * (1.0 / total_cells)

    def ab_make(j):
        k = wrap(chip + j, n_chip)
        block = wg.at[core, chip]
        return remote(block, block, ab_ss.at[j], ab_rs.at[j], at_chip(k))

    ab_arrive, ab_sent = over_chips(ab_make)
    rs_send(0, 4, 0, False)
    rs_send(1, 4, 1, False)

    rc_arrive()

    def add_ext(k, acc):
        return acc + extr[k]

    plane = lax.fori_loop(1, n_chip, add_ext, extr[0])
    gb_out[...] = plane[0:1, nn : nn + chans] * (1.0 / total_cells)
    extz[lev] = plane

    def z_make(j):
        return remote(
            extz.at[lev], extz.at[lev], z_ss.at[j], z_rs.at[j], (lat, lon, wrap(lev + j, n_lev))
        )

    for j in range(1, n_lev):
        z_make(j).start()

    for way, h in ((1, 0), (0, 1), (0, 0), (1, 1)):
        for k in range(cuts):
            rs_copies[way, far, h, k].wait_recv()
    g = jnp.concatenate(
        [
            gu[2 * lev + h]
            + jnp.concatenate(
                [unpack(arecv[0, far, h, k]) + unpack(arecv[1, far, h, k]) for k in range(cuts)],
                axis=0,
            )
            for h in range(2)
        ],
        axis=1,
    )
    at = lanes(2 * lev, 2)
    m_hi, m_lo = split(g * hr_s[:, at])
    back = dot(gt3[...], jnp.concatenate([m_hi, m_hi, m_lo], axis=0))
    gh = (g * root_s[:, at] + 2.0 * hx[:, lanes(2 * lev + 1, 2)] * back).astype(BF16)
    agr[2 * lev] = gh[:, :LANES]
    agr[2 * lev + 1] = gh[:, LANES:]

    ag_copies = {}

    def ag_send(s):
        for h in range(2):
            for way in range(2):
                if s == far and h != way:
                    continue
                owner = wrap(lev + (1 - s if way else s - 1), n_lev)
                for k in range(cuts):
                    if s > 1:
                        ag_copies[way, s - 1, h, k].wait_recv()
                    block = agr.at[2 * owner + h, pl.ds(k * piece, piece)]
                    ag_copies[way, s, h, k] = go(
                        remote(block, block, g_ss.at[way, s, h, k], g_rs.at[way, s, h, k],
                               above if way else below)
                    )

    put_copies = []

    def put(i, owner):
        block = pl.ds(2 * owner, 2)
        copy = pltpu.make_async_copy(agr.at[block], gh_out.at[block], put_sem.at[i])
        copy.start()
        put_copies.append(copy)

    ag_send(1)
    put(0, lev)
    for j in range(1, n_lev):
        z_make(j).wait_recv()
    whole = extz[0]
    for k in range(1, n_lev):
        whole = whole + extz[k]
    extg[core, chip] = whole * (1.0 / total_cells)

    def ac_make(j):
        k = wrap(chip + j, n_chip)
        block = extg.at[core, chip]
        return remote(block, block, ac_ss.at[j], ac_rs.at[j], at_chip(k))

    ac_arrive, ac_sent = over_chips(ac_make)
    ag_send(2)
    put(1, wrap(lev + 1, n_lev))
    put(2, wrap(lev - 1, n_lev))
    ab_arrive()
    pg = go(remote(wg.at[core], wg.at[core], pg_ss, pg_rs, pair))
    w_copies = [
        pltpu.make_async_copy(wg.at[part], gw_out.at[part], out_sem.at[i])
        for i, part in enumerate((core, 1 - core))
    ]
    w_copies[0].start()
    ag_send(3)
    put(3, wrap(lev + 2, n_lev))
    put(4, wrap(lev - 2, n_lev))
    ac_arrive()
    pc = go(remote(extg.at[core], extg.at[core], pc_ss, pc_rs, pair))
    ag_send(4)
    for way in range(2):
        for k in range(cuts):
            ag_copies[way, far - 1, 1 - way, k].wait_recv()
    put(5, wrap(lev + 3, n_lev))
    put(6, wrap(lev - 3, n_lev))
    pg.wait_recv()
    w_copies[1].start()
    pc.wait_recv()
    e_copy = pltpu.make_async_copy(extg, ext_out, out_sem.at[2])
    e_copy.start()
    for way in range(2):
        for k in range(cuts):
            ag_copies[way, far, way, k].wait_recv()
    put(7, wrap(lev + far, n_lev))

    for c in sends:
        c.wait_send()
    rb_sent()
    ab_sent()
    rc_sent()
    ac_sent()
    for j in range(1, n_lev):
        z_make(j).wait_send()
    for c in put_copies + w_copies + [e_copy]:
        c.wait()


def finish(
    dims, agr_ref, wg_ref, ext_ref, gb_ref,
    gh_out, gw_out, gg_out, gbeta_out, gb_out,
    agr, gho, gw_v, ext_v, gg_v, in_sem, out_sem, gw_sem, ext_sem,
):
    nn, rows, parts = dims
    step = nn // parts

    def fetch(k):
        at = pl.ds(k * step, step)
        return pltpu.make_async_copy(agr_ref.at[:, at], agr.at[:, at], in_sem.at[k])

    def store(k):
        at = pl.ds(k * step * rows, step * rows)
        return pltpu.make_async_copy(gho.at[at], gh_out.at[at], out_sem.at[k])

    def fetch_gw(k):
        return pltpu.make_async_copy(wg_ref.at[k], gw_v.at[k], gw_sem.at[0, k])

    def store_gw(k):
        return pltpu.make_async_copy(gw_v.at[k], gw_out.at[k], gw_sem.at[1, k])

    fetch_ext = pltpu.make_async_copy(ext_ref, ext_v, ext_sem.at[0])
    store_gg = pltpu.make_async_copy(gg_v, gg_out, ext_sem.at[1])
    for k in range(parts):
        fetch(k).start()
    fetch_ext.start()
    for k in range(2):
        fetch_gw(k).start()
    gb_out[...] = gb_ref[...]
    eye = lax.broadcasted_iota(jnp.int32, (nn, nn), 0) == lax.broadcasted_iota(
        jnp.int32, (nn, nn), 1
    )
    for k in range(parts):
        fetch(k).wait()
        for i in range(rows):
            gho[pl.ds(k * step * rows + i, step, stride=rows), :] = agr[
                i, k * step : (k + 1) * step, :
            ].astype(F32)
        store(k).start()
        if k < 2:
            fetch_gw(k).wait()
            store_gw(k).start()
    fetch_ext.wait()
    full = ext_v[...].reshape(nn, nn + LANES)
    gg_v[...] = full[:, :nn]
    store_gg.start()
    gbeta_out[...] = jnp.sum(
        jnp.where(eye, full[:, nn + LANES - 1 : nn + LANES], 0.0), axis=0, keepdims=True
    )
    for k in range(parts):
        store(k).wait()
    store_gg.wait()
    for k in range(2):
        store_gw(k).wait()


def local(sizes, target, hidden, weight, bias, gamma, beta):
    n_lat, n_lon, n_lev = sizes
    nn, rows, cols = hidden.shape
    chans = weight.shape[1]
    taps = weight.shape[0]
    n_chip = n_lat // 2 * n_lon
    half = taps // 2 * chans // n_chip
    share = nn // 2 // n_chip
    cells = rows * cols
    rpad = rows + 2
    total_rows = rows * n_lat
    total_cells = total_rows * cols * n_lon
    far = n_lev // 2
    at = np.arange(total_rows).reshape(n_lat, 1, rows) * 2.0 + np.arange(2).reshape(1, 2, 1)
    area = np.cos(math.pi * ((at + 0.5) / (2.0 * total_rows) - 0.5)).astype(np.float32)
    dims = (nn, rows, chans, n_lat, n_lon, n_lev, 4, total_cells)
    wide = nn + LANES
    V = pltpu.VMEM
    D = pltpu.SemaphoreType.DMA
    scratch = [
        V((nn, rows, cols), BF16), V((4, chans, rows, cols), BF16), V((taps, chans, nn), BF16),
        V((nn, nn), F32),
        V((nn * rows, cols), F32), V((4 * chans * rows, cols), F32), V((nn, rpad * cols), F32),
        V((nn, cells), F32), V((nn, cells), F32), V((nn, cells), BF16), V((nn, cells), BF16),
        V((nn, 3 * nn), BF16), V((nn, 3 * nn), BF16), V((nn, taps * chans), BF16),
        V((3 * nn, rpad * cols), BF16), V((2, 4 * chans, rpad * cols), BF16),
        V((64, cells), BF16), V((2, nn, cols), BF16), V((2, nn, cols), BF16),
        V((2, 32, nn), BF16), V((6, 32, nn), BF16),
        V((2, 2, 32, cols), BF16), V((2, 2, 32, cols), BF16), V((2, 2, 32, cols), BF16),
        V((2, n_chip, half, nn), F32), V((n_chip, half, nn), F32), V((n_chip, half, nn), BF16),
        V((n_chip, half, nn), BF16), V((2, n_chip, half, nn), F32),
        V((rows, nn, cols), F32), V((cols, cols), F32), V((nn, cells), BF16), V((nn, cells), BF16),
        V((nn, wide), F32), V((nn // 2, wide), F32), V((n_chip, share, wide), F32),
        V((n_chip, share, wide), F32), V((n_lev, share, wide), F32),
        V((2, n_chip, share, wide), F32),
        V((2, far + 1, 2, 2, nn // 4 * 3, cols), BF16),
        V((2, far + 1, 2, 2, nn // 4 * 3, cols), BF16),
        V((rows, nn, cols), BF16),
        D((4,)), D((3,)), D((n_lev,)),
        D((2,)), D((2,)), D((6,)), D((6,)), D((2,)), D((2,)), D((6,)), D((6,)),
        D, D, D((n_chip,)), D((n_chip,)), D((n_chip,)), D((n_chip,)), D, D,
        D, D, D((n_chip,)), D((n_chip,)), D((n_lev,)), D((n_lev,)), D((n_chip,)), D((n_chip,)),
        D, D,
        D((2, far + 1, 2, 2)), D((2, far + 1, 2, 2)),
        D((2, far + 1, 2, 2)), D((2, far + 1, 2, 2)),
    ]
    hbm = pl.BlockSpec(memory_space=pl.ANY)
    vmem = pl.BlockSpec(memory_space=pltpu.VMEM)
    smem = pl.BlockSpec(memory_space=pltpu.SMEM)
    agr, wg, ext, gb = pl.pallas_call(
        functools.partial(kernel, dims),
        out_shape=(
            jax.ShapeDtypeStruct((rows, nn, cols), BF16),
            jax.ShapeDtypeStruct((2, n_chip, half, nn), F32),
            jax.ShapeDtypeStruct((2, n_chip, share, wide), F32),
            jax.ShapeDtypeStruct((1, chans), F32),
        ),
        in_specs=[smem, hbm, hbm, hbm, vmem, hbm, vmem],
        out_specs=(hbm, hbm, hbm, vmem),
        scratch_shapes=scratch,
        compiler_params=pltpu.CompilerParams(
            collective_id=0, has_side_effects=True, vmem_limit_bytes=60 * 2**20
        ),
    )(
        jnp.asarray(area.reshape(-1)), hidden, target, weight, bias.reshape(1, chans),
        gamma, beta.reshape(1, nn),
    )
    parts = 4
    gh, gw, gg, gbeta, gb = pl.pallas_call(
        functools.partial(finish, (nn, rows, parts)),
        out_shape=(
            jax.ShapeDtypeStruct((nn * rows, cols), F32),
            jax.ShapeDtypeStruct((2, n_chip, half, nn), F32),
            jax.ShapeDtypeStruct((nn, nn), F32),
            jax.ShapeDtypeStruct((1, nn), F32),
            jax.ShapeDtypeStruct((1, chans), F32),
        ),
        in_specs=[hbm, hbm, hbm, vmem],
        out_specs=(hbm, hbm, hbm, vmem, vmem),
        scratch_shapes=[
            V((rows, nn, cols), BF16), V((nn * rows, cols), F32), V((2, n_chip, half, nn), F32),
            V((2, n_chip, share, wide), F32), V((nn, nn), F32),
            D((parts,)), D((parts,)), D((2, 2)), D((2,)),
        ],
        compiler_params=pltpu.CompilerParams(vmem_limit_bytes=60 * 2**20),
    )(agr, wg, ext, gb)
    return (
        gh.reshape(nn, rows, cols), gw.reshape(taps, chans, nn), gb.reshape(chans), gg,
        gbeta.reshape(nn),
    )


def solution(mesh):
    sizes = tuple(mesh.shape[a] for a in ("lat", "lon", "lev"))
    return jax.shard_map(
        functools.partial(local, sizes),
        mesh=mesh,
        in_specs=(
            P(None, "lev", "lat", "lon"),
            P(None, "lat", "lon"),
            P(None, "lev", None),
            P("lev"),
            P(),
            P(),
        ),
        out_specs=(P(None, "lat", "lon"), P(None, "lev", None), P("lev"), P(), P()),
        check_vma=False,
    )
```

```python
import functools
import math

import jax
import jax.numpy as jnp
import numpy as np
from jax import lax
from jax.experimental import pallas as pl
from jax.experimental.pallas import tpu as pltpu
from jax.sharding import PartitionSpec as P

F32 = jnp.float32
BF16 = jnp.bfloat16
MESH = pl.DeviceIdType.MESH
LANES = 128


def split(x):
    hi = x.astype(BF16)
    return hi, (x - hi.astype(F32)).astype(BF16)


def dot(a, b):
    return jnp.dot(a, b, preferred_element_type=F32)


def dot_nt(a, b):
    return lax.dot_general(a, b, (((1,), (1,)), ((), ())), preferred_element_type=F32)


STEPS = 1920.0


def pack(x):
    hi = x.astype(BF16)
    h = hi.astype(F32)
    scale = pl.reciprocal(jnp.maximum(jnp.abs(h), 1e-30), approx=True) * STEPS
    q = jnp.clip(jnp.floor((x - h) * scale + 0.5), -8.0, 7.0)
    m = x.shape[0] // 2
    return jnp.concatenate([hi, (16.0 * q[:m] + q[m:]).astype(BF16)], axis=0)


def unpack(y):
    m = y.shape[0] // 3
    h, p = y[: 2 * m].astype(F32), y[2 * m :].astype(F32)
    a = jnp.floor((p + 8.0) * 0.0625)
    q = jnp.concatenate([a, p - 16.0 * a], axis=0)
    return h + jnp.abs(h) * (q * (1.0 / STEPS))


def wrap(index, size):
    return lax.rem(index + size, size)


def kernel(
    dims,
    area_ref, hidden_ref, target_ref, weight_ref, bias_ref, gamma_ref, beta_ref,
    gh_out, gw_out, ext_out, gb_out,
    hid_v, tgt_v, w_v, gamma_v,
    hf, tf, hx, root_s, hr_s, sqh, sql, g3, gt3, wt,
    us, gs, sel, hh_send, hh_recv, eu_send, eu_recv, eg_send, eg_recv, eg_corner,
    dw, dwp, rsb, rsr, wg,
    gu, bacc, mh, ml, ext, extp, exts, extr, extz, extg,
    abuf, arecv, agr,
    in_sem, out_sem, put_sem,
    row_ss, row_rs, eu_ss, eu_rs, grow_ss, grow_rs, eg_ss, eg_rs,
    pw_ss, pw_rs, rb_ss, rb_rs, ab_ss, ab_rs, pg_ss, pg_rs,
    pe_ss, pe_rs, rc_ss, rc_rs, z_ss, z_rs, ac_ss, ac_rs, pc_ss, pc_rs,
    a_ss, a_rs, g_ss, g_rs,
):
    nn, rows, chans, n_lat, n_lon, n_lev, n_y, total_cells = dims
    cells = rows * LANES
    rpad = rows + 2
    lat, lon, lev = lax.axis_index("lat"), lax.axis_index("lon"), lax.axis_index("lev")
    core = lax.rem(lat, 2)
    n_chip = (n_lat // 2) * n_lon
    n_xlo = n_lon // n_y
    chip = lax.div(lat, 2) * n_lon + lon
    half = 16 // 2 * chans // n_chip
    share = nn // 2 // n_chip

    def at_chip(k):
        return (lax.div(k, n_lon) * 2 + core, lax.rem(k, n_lon), lev)

    pair = (lat + 1 - 2 * core, lon, lev)
    north = (wrap(lat - 1, n_lat), lon, lev)
    south = (wrap(lat + 1, n_lat), lon, lev)
    west = (lat, wrap(lon - 1, n_lon), lev)
    east = (lat, wrap(lon + 1, n_lon), lev)
    below = (lat, lon, wrap(lev - 1, n_lev))
    above = (lat, lon, wrap(lev + 1, n_lev))

    def remote(src, dst, ss, rs, device):
        return pltpu.make_async_remote_copy(
            src_ref=src, dst_ref=dst, send_sem=ss, recv_sem=rs,
            device_id=device, device_id_type=MESH,
        )

    def lanes(r, count=1):
        if isinstance(r, int):
            return pl.ds(r * LANES, count * LANES)
        return pl.ds(pl.multiple_of(r * LANES, LANES), count * LANES)

    inputs = [
        pltpu.make_async_copy(s, d, in_sem.at[i])
        for i, (s, d) in enumerate(
            ((hidden_ref, hid_v), (gamma_ref, gamma_v), (target_ref, tgt_v), (weight_ref, w_v))
        )
    ]
    for c in inputs:
        c.start()

    barrier = pltpu.get_barrier_semaphore()

    def greet(device):
        pl.semaphore_signal(barrier, inc=1, device_id=device, device_id_type=MESH)

    corners = [
        (wrap(lat + i, n_lat), wrap(lon + j, n_lon), lev) for i in (-1, 1) for j in (-1, 1)
    ]
    northwest, northeast, southwest, southeast = corners
    for device in [north, south] + corners:
        greet(device)

    def greet_chip(j, c):
        greet(at_chip(wrap(chip + j, n_chip)))
        return c

    lax.fori_loop(1, n_chip, greet_chip, 0)

    def greet_lev(j, c):
        greet((lat, lon, wrap(lev + j, n_lev)))
        return c

    lax.fori_loop(1, n_lev, greet_lev, 0)

    inputs[0].wait()
    hf[...] = hid_v[...].astype(F32).reshape(nn * rows, LANES)

    mid = slice(nn, 2 * nn)

    def spread(i, c):
        x = hf[pl.ds(i, nn, stride=rows), :]
        hx[:, lanes(i + 1)] = x
        us[mid, lanes(i + 1)] = x.astype(BF16)
        return c

    lax.fori_loop(0, rows, spread, 0, unroll=2)
    hh_send[0] = us[mid, lanes(1)]
    hh_send[1] = us[mid, lanes(rows)]

    def make_sel(r, c):
        e = lax.broadcasted_iota(jnp.int32, (64, LANES), 0)
        k = lax.broadcasted_iota(jnp.int32, (64, LANES), 1)
        last, first = k == LANES - 1, k == 0
        hit = (last & (e == r)) | (first & (e == 32 + r))
        hit = hit | ((r == rows) & ((last & (e == 0)) | (first & (e == 32))))
        hit = hit | ((r == 1) & ((last & (e == rows + 1)) | (first & (e == 33 + rows))))
        sel[:, lanes(r - 1)] = jnp.where(hit, 1.0, 0.0).astype(BF16)
        return c

    lax.fori_loop(1, rows + 1, make_sel, 0)
    columns = dot_nt(sel[...], us[mid, lanes(1, rows)]).astype(BF16)
    eu_send[0] = columns[:32]
    eu_send[1] = columns[32:]

    pl.semaphore_wait(barrier, 6 + (n_chip - 1) + (n_lev - 1))

    sends = []

    def go(copy):
        copy.start()
        sends.append(copy)
        return copy

    eu_copies = [
        go(remote(eu_send.at[i % 2], eu_recv.at[i], eu_ss.at[i], eu_rs.at[i], device))
        for i, device in enumerate((east, west, southeast, southwest, northeast, northwest))
    ] + [
        go(remote(hh_send.at[0], hh_recv.at[1], row_ss.at[0], row_rs.at[0], north)),
        go(remote(hh_send.at[1], hh_recv.at[0], row_ss.at[1], row_rs.at[1], south)),
    ]

    inputs[1].wait()
    gamma = gamma_v[...]
    g_hi, g_lo = split(gamma)
    g3[...] = jnp.concatenate([g_hi, g_lo, g_hi], axis=1)
    g_hi, g_lo = split(gamma.T)
    gt3[...] = jnp.concatenate([g_hi, g_lo, g_hi], axis=1)
    eye = lax.broadcasted_iota(jnp.int32, (nn, nn), 0) == lax.broadcasted_iota(
        jnp.int32, (nn, nn), 1
    )
    beta_col = jnp.sum(jnp.where(eye, beta_ref[...], 0.0), axis=1, keepdims=True)
    eye_c = lax.broadcasted_iota(jnp.int32, (chans, chans), 0) == lax.broadcasted_iota(
        jnp.int32, (chans, chans), 1
    )
    bias_col = jnp.sum(jnp.where(eye_c, bias_ref[...], 0.0), axis=1, keepdims=True)

    def root_of(x):
        s_hi, s_lo = split(x * x)
        total = dot(g3[...], jnp.concatenate([s_hi, s_hi, s_lo], axis=0))
        return jnp.sqrt(beta_col + total), s_hi, s_lo

    def root_tile(t, c):
        at = lanes(2 * t, 2)
        x = hx[:, lanes(2 * t + 1, 2)]
        root, s_hi, s_lo = root_of(x)
        root_s[:, at] = root
        hr_s[:, at] = x * (0.5 / root)
        sqh[:, at] = s_hi
        sql[:, at] = s_lo
        us[nn : 2 * nn, lanes(2 * t + 1, 2)] = (x * root).astype(BF16)
        return c

    lax.fori_loop(0, rows // 2, root_tile, 0, unroll=2)

    north_in = jnp.where(lat > 0, 1.0, 0.0).astype(F32)
    south_in = jnp.where(lat < n_lat - 1, 1.0, 0.0).astype(F32)

    inputs[3].wait()
    order = []
    for p in range(2):
        for a in range(2):
            for v in range(2):
                for q in range(2):
                    b = v if q else 1 - v
                    order.append(4 * (2 * p + q) + 2 * a + b)
    for g in range(4):
        block = jnp.concatenate([w_v[t] for t in order[4 * g : 4 * g + 4]], axis=0)
        wt[:, 4 * chans * g : 4 * chans * (g + 1)] = block.T

    inputs[2].wait()

    def widen(k, c):
        span = chans * rows
        tf[pl.ds(pl.multiple_of(k * span, span), span), :] = (
            tgt_v[k].astype(F32).reshape(span, LANES)
        )
        return c

    lax.fori_loop(0, 4, widen, 0)
    bacc[...] = jnp.zeros_like(bacc)
    gs[0, : 2 * chans, lanes(0)] = jnp.zeros((2 * chans, LANES), BF16)
    gs[1, : 2 * chans, lanes(rpad - 1)] = jnp.zeros((2 * chans, LANES), BF16)

    for c in eu_copies:
        c.wait_recv()
    row = lax.broadcasted_iota(jnp.int32, (32, nn), 0)

    def side(i):
        x = eu_recv[i].astype(F32)
        x = jnp.where(row == 0, eu_recv[i + 2].astype(F32) * north_in, x)
        return jnp.where(row == rows + 1, eu_recv[i + 4].astype(F32) * south_in, x)

    columns = jnp.concatenate([side(0), side(1), jnp.zeros((64, nn), F32)], axis=0).T
    x = jnp.concatenate(
        [hh_recv[0].astype(F32) * north_in, hh_recv[1].astype(F32) * south_in, columns], axis=1
    )
    root, _, _ = root_of(x)
    edge = (x * root).astype(BF16)
    us[mid, lanes(0)] = edge[:, :LANES]
    us[mid, lanes(rpad - 1)] = edge[:, LANES : 2 * LANES]
    eu_mix = edge[:, 2 * LANES :].astype(F32)

    def from_west(x, e, r):
        at = lax.broadcasted_iota(jnp.int32, x.shape, 1)
        return jnp.where(at == 0, pltpu.roll(e, LANES - r, 1), pltpu.roll(x, 1, 1))

    def from_east(x, e, r):
        at = lax.broadcasted_iota(jnp.int32, x.shape, 1)
        edge = pltpu.roll(e, LANES - 1 - r, 1)
        return jnp.where(at == LANES - 1, edge, pltpu.roll(x, LANES - 1, 1))

    def shift_u(r, c):
        x = us[mid, lanes(r)].astype(F32)
        us[:nn, lanes(r)] = from_west(x, eu_mix, r).astype(BF16)
        us[2 * nn :, lanes(r)] = from_east(x, eu_mix, 32 + r).astype(BF16)
        return c

    lax.fori_loop(0, rpad, shift_u, 0, unroll=3)

    def recon_tile(it, c):
        t = lax.rem(it + rows // 2 - 1, rows // 2)
        for p in range(2):
            area = [area_ref[lat * 2 * rows + p * rows + 2 * t + i] for i in range(2)]
            for q in range(2):
                phase = 2 * p + q
                moved = jnp.concatenate(
                    [us[q * nn : (q + 2) * nn, lanes(2 * t + p + a, 2)] for a in range(2)], axis=0
                )
                w = jnp.concatenate([w_v[4 * phase + k] for k in range(4)], axis=1)
                recon = dot(w, moved) + bias_col
                total = jnp.zeros((chans, LANES), F32)
                for i in range(2):
                    want = tf[pl.ds(phase * chans * rows + 2 * t + i, chans, stride=rows), :]
                    diff = (recon[:, i * LANES : (i + 1) * LANES] - want) * area[i]
                    total = total + diff
                    gs[p, q * chans : (q + 1) * chans, lanes(2 * t + i + 1)] = diff.astype(BF16)
                bacc[:chans, :] += total
        return c

    lax.fori_loop(0, 2, recon_tile, 0, unroll=2)
    grow_copies = [
        go(remote(gs.at[0, 0 : 2 * chans, lanes(1)], gs.at[0, 0 : 2 * chans, lanes(rpad - 1)],
                  grow_ss.at[0], grow_rs.at[0], north)),
        go(remote(gs.at[1, 0 : 2 * chans, lanes(rows)], gs.at[1, 0 : 2 * chans, lanes(0)],
                  grow_ss.at[1], grow_rs.at[1], south)),
    ]
    lax.fori_loop(2, rows // 2, recon_tile, 0, unroll=2)
    pad = LANES - chans
    for p in range(2):
        for q in range(2):
            block = gs[p, q * (chans - pad) : q * (chans - pad) + LANES, lanes(1, rows)]
            eg_send[q, p] = dot_nt(sel[32 * (1 - q) : 32 * (2 - q), :], block).astype(BF16)
    eg_copies = [
        go(remote(src, dst, eg_ss.at[i], eg_rs.at[i], device))
        for i, (src, dst, device) in enumerate((
            (eg_send.at[0], eg_recv.at[0], west),
            (eg_send.at[1], eg_recv.at[1], east),
            (eg_send.at[0, 0], eg_corner.at[0, 0], northwest),
            (eg_send.at[1, 0], eg_corner.at[1, 0], northeast),
            (eg_send.at[0, 1], eg_corner.at[0, 1], southwest),
            (eg_send.at[1, 1], eg_corner.at[1, 1], southeast),
        ))
    ]

    per_tap = chans // half

    def grad_taps(slot, p, q):
        for a in range(2):
            y = dot_nt(
                gs[p, q * chans : (q + 1) * chans, lanes(1, rows)],
                us[q * nn : (q + 2) * nn, lanes(p + a, rows)],
            )
            for b in range(2):
                for k in range(per_tap):
                    dw[slot, (4 * q + 2 * a + b) * per_tap + k] = y[
                        k * half : (k + 1) * half, b * nn : (b + 1) * nn
                    ]

    grad_taps(0, 1 - core, 0)
    grad_taps(0, 1 - core, 1)
    pw = go(remote(dw.at[0], dwp, pw_ss, pw_rs, pair))
    grad_taps(1, core, 0)

    for c in grow_copies + eg_copies:
        c.wait_recv()
    gs[0, : 2 * chans, lanes(rpad - 1)] = (
        gs[0, : 2 * chans, lanes(rpad - 1)].astype(F32) * south_in
    ).astype(BF16)
    gs[1, : 2 * chans, lanes(0)] = (
        gs[1, : 2 * chans, lanes(0)].astype(F32) * north_in
    ).astype(BF16)
    row = lax.broadcasted_iota(jnp.int32, (32, LANES), 0)
    eg_mix = {}
    for p, at, keep in ((0, rows + 1, south_in), (1, 0, north_in)):
        for q in range(2):
            x = jnp.where(
                row == at, eg_corner[q, p].astype(F32) * keep, eg_recv[q, p].astype(F32)
            )
            x = jnp.concatenate([x, jnp.zeros((LANES - 32, LANES), F32)], axis=0).T
            eg_mix[p, q] = x[q * pad : q * pad + chans]

    def shift_g(r, c):
        for p in range(2):
            rr = r + 1 - p
            x = gs[p, : 2 * chans, lanes(rr)].astype(F32)
            gs[p, 2 * chans : 3 * chans, lanes(rr)] = from_east(
                x[:chans], eg_mix[p, 0], rr
            ).astype(BF16)
            gs[p, 3 * chans :, lanes(rr)] = from_west(
                x[chans:], eg_mix[p, 1], rr
            ).astype(BF16)
        return c

    def shift_pair(i, c):
        shift_g(2 * i, c)
        return shift_g(2 * i + 1, c)

    far = n_lev // 2
    opposite = wrap(lev + far, n_lev)
    for r in range(3):
        shift_g(2 * opposite + r, 0)

    def grad_rows(*chunks):
        moved = jnp.concatenate(
            [
                jnp.concatenate([gs[p, :, lanes(2 * k + 2 - p - a, 2)] for k in chunks], axis=1)
                for p in range(2)
                for a in range(2)
            ],
            axis=0,
        )
        y = dot(wt[...], moved)
        for i, k in enumerate(chunks):
            gu[2 * k] = y[:, 2 * i * LANES : (2 * i + 1) * LANES]
            gu[2 * k + 1] = y[:, (2 * i + 1) * LANES : (2 * i + 2) * LANES]

    cuts = 2
    piece = nn // cuts
    rs_copies = {}

    def rs_send(way, s, h, first):
        owner = wrap(lev + (far + 1 - s if way else s - far - 1), n_lev)
        for k in range(cuts):
            at = pl.ds(k * piece, piece)
            x = gu[2 * owner + h, at]
            if not first:
                rs_copies[way, s - 1, h, k].wait_recv()
                x = x + unpack(arecv[way, s - 1, h, k])
            abuf[way, s, h, k] = pack(x)
            rs_copies[way, s, h, k] = go(
                remote(abuf.at[way, s, h, k], arecv.at[way, s, h, k], a_ss.at[way, s, h, k],
                       a_rs.at[way, s, h, k], above if way else below)
            )

    def over_chips(make):
        def start(j, c):
            make(j).start()
            return c

        def arrive(j, c):
            make(j).wait_recv()
            return c

        def sent(j, c):
            make(j).wait_send()
            return c

        lax.fori_loop(1, n_chip, start, 0)
        return (
            lambda: lax.fori_loop(1, n_chip, arrive, 0),
            lambda: lax.fori_loop(1, n_chip, sent, 0),
        )

    grad_rows(opposite)
    rs_send(0, 1, 0, True)
    rs_send(1, 1, 1, True)
    lax.fori_loop(0, (rows + 1) // 2, shift_pair, 0)
    shift_g(rows, 0)
    grad_rows(wrap(lev + far - 1, n_lev), wrap(lev + far + 1, n_lev))
    rs_send(1, 2, 0, True)
    rs_send(0, 2, 1, True)
    grad_taps(1, core, 1)
    pw.wait_recv()

    def join(k, c):
        dw[1, k] = dw[1, k] + dwp[k]
        rsb[k] = dw[1, k].astype(BF16)
        return c

    lax.fori_loop(0, n_chip, join, 0)

    def rb_make(j):
        k = wrap(chip + j, n_chip)
        return remote(rsb.at[k], rsr.at[j], rb_ss.at[j], rb_rs.at[j], at_chip(k))

    rb_arrive, rb_sent = over_chips(rb_make)
    rs_send(0, 2, 0, False)
    rs_send(1, 2, 1, False)
    grad_rows(wrap(lev + far - 2, n_lev), wrap(lev + far + 2, n_lev))
    grad_rows(wrap(lev + 1, n_lev), wrap(lev + n_lev - 1, n_lev))
    grad_rows(lev)

    def mix_tile(t, acc):
        at = lanes(2 * t, 2)
        g = jnp.concatenate([gu[2 * t], gu[2 * t + 1]], axis=1)
        mixing = g * hr_s[:, at]
        m_hi, m_lo = split(mixing)
        mh[:, at] = m_hi
        ml[:, at] = m_lo
        return acc + mixing[:, :LANES] + mixing[:, LANES:]

    msum = lax.fori_loop(0, rows // 2, mix_tile, jnp.zeros((nn, LANES), F32))
    beta_part = jnp.sum(msum, axis=1, keepdims=True)
    bias_part = jnp.sum(bacc[...].T, axis=0, keepdims=True)
    ext[:, :nn] = dot_nt(mh[...], sqh[...]) + (
        dot_nt(ml[...], sqh[...]) + dot_nt(mh[...], sql[...])
    )
    lane = lax.broadcasted_iota(jnp.int32, (nn, LANES), 1)
    ext[:, nn:] = jnp.where(lane == LANES - 1, beta_part, bias_part)
    mine = pl.multiple_of(core * (nn // 2), nn // 2)
    others = pl.multiple_of((1 - core) * (nn // 2), nn // 2)
    pe = go(remote(ext.at[pl.ds(others, nn // 2)], extp, pe_ss, pe_rs, pair))

    pe.wait_recv()

    def join_ext(k, c):
        at = pl.ds(pl.multiple_of(mine + k * share, share), share)
        exts[k] = ext[at, :] + extp[pl.ds(pl.multiple_of(k * share, share), share), :]
        return c

    lax.fori_loop(0, n_chip, join_ext, 0)
    extr[chip] = exts[chip]

    def rc_make(j):
        k = wrap(chip + j, n_chip)
        return remote(exts.at[k], extr.at[chip], rc_ss.at[j], rc_rs.at[j], at_chip(k))

    rc_arrive, rc_sent = over_chips(rc_make)
    rs_send(1, 3, 0, False)
    rs_send(0, 3, 1, False)
    rs_send(0, 3, 0, False)
    rs_send(1, 3, 1, False)

    rs_send(1, 4, 0, False)
    rs_send(0, 4, 1, False)

    rb_arrive()

    def add_taps(j, acc):
        return acc + rsr[j].astype(F32)

    wg[core, chip] = lax.fori_loop(1, n_chip, add_taps, dw[1, chip]) * (1.0 / total_cells)

    def ab_make(j):
        k = wrap(chip + j, n_chip)
        block = wg.at[core, chip]
        return remote(block, block, ab_ss.at[j], ab_rs.at[j], at_chip(k))

    ab_arrive, ab_sent = over_chips(ab_make)
    rs_send(0, 4, 0, False)
    rs_send(1, 4, 1, False)

    rc_arrive()

    def add_ext(k, acc):
        return acc + extr[k]

    plane = lax.fori_loop(1, n_chip, add_ext, extr[0])
    gb_out[...] = plane[0:1, nn : nn + chans] * (1.0 / total_cells)
    extz[lev] = plane

    def z_make(j):
        return remote(
            extz.at[lev], extz.at[lev], z_ss.at[j], z_rs.at[j], (lat, lon, wrap(lev + j, n_lev))
        )

    for j in range(1, n_lev):
        z_make(j).start()

    for way, h in ((1, 0), (0, 1), (0, 0), (1, 1)):
        for k in range(cuts):
            rs_copies[way, far, h, k].wait_recv()
    g = jnp.concatenate(
        [
            gu[2 * lev + h]
            + jnp.concatenate(
                [unpack(arecv[0, far, h, k]) + unpack(arecv[1, far, h, k]) for k in range(cuts)],
                axis=0,
            )
            for h in range(2)
        ],
        axis=1,
    )
    at = lanes(2 * lev, 2)
    m_hi, m_lo = split(g * hr_s[:, at])
    back = dot(gt3[...], jnp.concatenate([m_hi, m_hi, m_lo], axis=0))
    gh = (g * root_s[:, at] + 2.0 * hx[:, lanes(2 * lev + 1, 2)] * back).astype(BF16)
    agr[2 * lev] = gh[:, :LANES]
    agr[2 * lev + 1] = gh[:, LANES:]

    ag_copies = {}

    def ag_send(s):
        for h in range(2):
            for way in range(2):
                if s == far and h != way:
                    continue
                owner = wrap(lev + (1 - s if way else s - 1), n_lev)
                for k in range(cuts):
                    if s > 1:
                        ag_copies[way, s - 1, h, k].wait_recv()
                    block = agr.at[2 * owner + h, pl.ds(k * piece, piece)]
                    ag_copies[way, s, h, k] = go(
                        remote(block, block, g_ss.at[way, s, h, k], g_rs.at[way, s, h, k],
                               above if way else below)
                    )

    put_copies = []

    def put(i, owner):
        block = pl.ds(2 * owner, 2)
        copy = pltpu.make_async_copy(agr.at[block], gh_out.at[block], put_sem.at[i])
        copy.start()
        put_copies.append(copy)

    ag_send(1)
    put(0, lev)
    for j in range(1, n_lev):
        z_make(j).wait_recv()
    whole = extz[0]
    for k in range(1, n_lev):
        whole = whole + extz[k]
    extg[core, chip] = whole * (1.0 / total_cells)

    def ac_make(j):
        k = wrap(chip + j, n_chip)
        block = extg.at[core, chip]
        return remote(block, block, ac_ss.at[j], ac_rs.at[j], at_chip(k))

    ac_arrive, ac_sent = over_chips(ac_make)
    ag_send(2)
    put(1, wrap(lev + 1, n_lev))
    put(2, wrap(lev - 1, n_lev))
    ab_arrive()
    pg = go(remote(wg.at[core], wg.at[core], pg_ss, pg_rs, pair))
    w_copies = [
        pltpu.make_async_copy(wg.at[part], gw_out.at[part], out_sem.at[i])
        for i, part in enumerate((core, 1 - core))
    ]
    w_copies[0].start()
    ag_send(3)
    put(3, wrap(lev + 2, n_lev))
    put(4, wrap(lev - 2, n_lev))
    ac_arrive()
    pc = go(remote(extg.at[core], extg.at[core], pc_ss, pc_rs, pair))
    ag_send(4)
    for way in range(2):
        for k in range(cuts):
            ag_copies[way, far - 1, 1 - way, k].wait_recv()
    put(5, wrap(lev + 3, n_lev))
    put(6, wrap(lev - 3, n_lev))
    pg.wait_recv()
    w_copies[1].start()
    pc.wait_recv()
    e_copy = pltpu.make_async_copy(extg, ext_out, out_sem.at[2])
    e_copy.start()
    for way in range(2):
        for k in range(cuts):
            ag_copies[way, far, way, k].wait_recv()
    put(7, wrap(lev + far, n_lev))

    for c in sends:
        c.wait_send()
    rb_sent()
    ab_sent()
    rc_sent()
    ac_sent()
    for j in range(1, n_lev):
        z_make(j).wait_send()
    for c in put_copies + w_copies + [e_copy]:
        c.wait()


def finish(
    dims, agr_ref, wg_ref, ext_ref, gb_ref,
    gh_out, gw_out, gg_out, gbeta_out, gb_out,
    agr, gho, gw_v, ext_v, gg_v, in_sem, out_sem, gw_sem, ext_sem,
):
    nn, rows, parts = dims
    step = nn // parts

    def fetch(k):
        at = pl.ds(k * step, step)
        return pltpu.make_async_copy(agr_ref.at[:, at], agr.at[:, at], in_sem.at[k])

    def store(k):
        at = pl.ds(k * step * rows, step * rows)
        return pltpu.make_async_copy(gho.at[at], gh_out.at[at], out_sem.at[k])

    def fetch_gw(k):
        return pltpu.make_async_copy(wg_ref.at[k], gw_v.at[k], gw_sem.at[0, k])

    def store_gw(k):
        return pltpu.make_async_copy(gw_v.at[k], gw_out.at[k], gw_sem.at[1, k])

    fetch_ext = pltpu.make_async_copy(ext_ref, ext_v, ext_sem.at[0])
    store_gg = pltpu.make_async_copy(gg_v, gg_out, ext_sem.at[1])
    for k in range(parts):
        fetch(k).start()
    fetch_ext.start()
    for k in range(2):
        fetch_gw(k).start()
    gb_out[...] = gb_ref[...]
    eye = lax.broadcasted_iota(jnp.int32, (nn, nn), 0) == lax.broadcasted_iota(
        jnp.int32, (nn, nn), 1
    )
    for k in range(parts):
        fetch(k).wait()
        for i in range(rows):
            gho[pl.ds(k * step * rows + i, step, stride=rows), :] = agr[
                i, k * step : (k + 1) * step, :
            ].astype(F32)
        store(k).start()
        if k < 2:
            fetch_gw(k).wait()
            store_gw(k).start()
    fetch_ext.wait()
    full = ext_v[...].reshape(nn, nn + LANES)
    gg_v[...] = full[:, :nn]
    store_gg.start()
    gbeta_out[...] = jnp.sum(
        jnp.where(eye, full[:, nn + LANES - 1 : nn + LANES], 0.0), axis=0, keepdims=True
    )
    for k in range(parts):
        store(k).wait()
    store_gg.wait()
    for k in range(2):
        store_gw(k).wait()


def local(sizes, target, hidden, weight, bias, gamma, beta):
    n_lat, n_lon, n_lev = sizes
    nn, rows, cols = hidden.shape
    chans = weight.shape[1]
    taps = weight.shape[0]
    n_chip = n_lat // 2 * n_lon
    half = taps // 2 * chans // n_chip
    share = nn // 2 // n_chip
    cells = rows * cols
    rpad = rows + 2
    total_rows = rows * n_lat
    total_cells = total_rows * cols * n_lon
    far = n_lev // 2
    at = np.arange(total_rows).reshape(n_lat, 1, rows) * 2.0 + np.arange(2).reshape(1, 2, 1)
    area = np.cos(math.pi * ((at + 0.5) / (2.0 * total_rows) - 0.5)).astype(np.float32)
    dims = (nn, rows, chans, n_lat, n_lon, n_lev, 4, total_cells)
    wide = nn + LANES
    V = pltpu.VMEM
    D = pltpu.SemaphoreType.DMA
    scratch = [
        V((nn, rows, cols), BF16), V((4, chans, rows, cols), BF16), V((taps, chans, nn), BF16),
        V((nn, nn), F32),
        V((nn * rows, cols), F32), V((4 * chans * rows, cols), F32), V((nn, rpad * cols), F32),
        V((nn, cells), F32), V((nn, cells), F32), V((nn, cells), BF16), V((nn, cells), BF16),
        V((nn, 3 * nn), BF16), V((nn, 3 * nn), BF16), V((nn, taps * chans), BF16),
        V((3 * nn, rpad * cols), BF16), V((2, 4 * chans, rpad * cols), BF16),
        V((64, cells), BF16), V((2, nn, cols), BF16), V((2, nn, cols), BF16),
        V((2, 32, nn), BF16), V((6, 32, nn), BF16),
        V((2, 2, 32, cols), BF16), V((2, 2, 32, cols), BF16), V((2, 2, 32, cols), BF16),
        V((2, n_chip, half, nn), F32), V((n_chip, half, nn), F32), V((n_chip, half, nn), BF16),
        V((n_chip, half, nn), BF16), V((2, n_chip, half, nn), F32),
        V((rows, nn, cols), F32), V((cols, cols), F32), V((nn, cells), BF16), V((nn, cells), BF16),
        V((nn, wide), F32), V((nn // 2, wide), F32), V((n_chip, share, wide), F32),
        V((n_chip, share, wide), F32), V((n_lev, share, wide), F32),
        V((2, n_chip, share, wide), F32),
        V((2, far + 1, 2, 2, nn // 4 * 3, cols), BF16),
        V((2, far + 1, 2, 2, nn // 4 * 3, cols), BF16),
        V((rows, nn, cols), BF16),
        D((4,)), D((3,)), D((n_lev,)),
        D((2,)), D((2,)), D((6,)), D((6,)), D((2,)), D((2,)), D((6,)), D((6,)),
        D, D, D((n_chip,)), D((n_chip,)), D((n_chip,)), D((n_chip,)), D, D,
        D, D, D((n_chip,)), D((n_chip,)), D((n_lev,)), D((n_lev,)), D((n_chip,)), D((n_chip,)),
        D, D,
        D((2, far + 1, 2, 2)), D((2, far + 1, 2, 2)),
        D((2, far + 1, 2, 2)), D((2, far + 1, 2, 2)),
    ]
    hbm = pl.BlockSpec(memory_space=pl.ANY)
    vmem = pl.BlockSpec(memory_space=pltpu.VMEM)
    smem = pl.BlockSpec(memory_space=pltpu.SMEM)
    agr, wg, ext, gb = pl.pallas_call(
        functools.partial(kernel, dims),
        out_shape=(
            jax.ShapeDtypeStruct((rows, nn, cols), BF16),
            jax.ShapeDtypeStruct((2, n_chip, half, nn), F32),
            jax.ShapeDtypeStruct((2, n_chip, share, wide), F32),
            jax.ShapeDtypeStruct((1, chans), F32),
        ),
        in_specs=[smem, hbm, hbm, hbm, vmem, hbm, vmem],
        out_specs=(hbm, hbm, hbm, vmem),
        scratch_shapes=scratch,
        compiler_params=pltpu.CompilerParams(
            collective_id=0, has_side_effects=True, vmem_limit_bytes=60 * 2**20
        ),
    )(
        jnp.asarray(area.reshape(-1)), hidden, target, weight, bias.reshape(1, chans),
        gamma, beta.reshape(1, nn),
    )
    parts = 4
    gh, gw, gg, gbeta, gb = pl.pallas_call(
        functools.partial(finish, (nn, rows, parts)),
        out_shape=(
            jax.ShapeDtypeStruct((nn * rows, cols), F32),
            jax.ShapeDtypeStruct((2, n_chip, half, nn), F32),
            jax.ShapeDtypeStruct((nn, nn), F32),
            jax.ShapeDtypeStruct((1, nn), F32),
            jax.ShapeDtypeStruct((1, chans), F32),
        ),
        in_specs=[hbm, hbm, hbm, vmem],
        out_specs=(hbm, hbm, hbm, vmem, vmem),
        scratch_shapes=[
            V((rows, nn, cols), BF16), V((nn * rows, cols), F32), V((2, n_chip, half, nn), F32),
            V((2, n_chip, share, wide), F32), V((nn, nn), F32),
            D((parts,)), D((parts,)), D((2, 2)), D((2,)),
        ],
        compiler_params=pltpu.CompilerParams(vmem_limit_bytes=60 * 2**20),
    )(agr, wg, ext, gb)
    return (
        gh.reshape(nn, rows, cols), gw.reshape(taps, chans, nn), gb.reshape(chans), gg,
        gbeta.reshape(nn),
    )


def solution(mesh):
    sizes = tuple(mesh.shape[a] for a in ("lat", "lon", "lev"))
    return jax.shard_map(
        functools.partial(local, sizes),
        mesh=mesh,
        in_specs=(
            P(None, "lev", "lat", "lon"),
            P(None, "lat", "lon"),
            P(None, "lev", None),
            P("lev"),
            P(),
            P(),
        ),
        out_specs=(P(None, "lat", "lon"), P(None, "lev", None), P("lev"), P(), P()),
        check_vma=False,
    )
```
